128 devices in a mesh: row: 8 (over y_hi, z), col: 16 (over y_lo, x, core).
Axes of the slice: x: 4, y: 4 (y_hi: 2, y_lo: 2; y = y_hi * 2 + y_lo), z: 4, core: 2. Of those that a mesh axis runs over, the one named last changes fastest.
Arguments:
- iterate: float32 [6144, 4096], P('row', 'col'), may hold values from -6 to 6
- factor: float32 [4096, 4096], P(None, 'col'), may hold values from -0.0625 to 0.0625
- inverses: float32 [8, 512, 512], replicated, as said below
Outputs:
- gram_matrix: float32 [4096, 4096], P('row', 'col')
- panel_factor: float32 [4096, 512], P(('row', 'col'))
- solved: float32 [6144, 4096], P('row', 'col')
The draws below stay inside these ranges and needn't reach their ends.
Inputs may be any that keep to these rules, and one draw needn't show every extreme that they name: Each block of inverses is upper triangular with positive diagonal entries.
All inputs are finite; a program needn't handle non-finite values.
Results may differ from the reference program's by a relative error of at most 0.00013.
Values sent between devices are 32-bit elements; how exact they have to be, the bound alone decides.
A program may use at most 128 MiB of HBM per device.

```python
import jax
import jax.numpy as jnp
from jax import lax

NB = 4096
PB = 512
ROWS = 6144
PANELS = 8


def draw_inverses(key, part):
    key = jax.random.fold_in(key, 7)
    diag_key, off_key = jax.random.split(key)
    diag_vals = jnp.exp(jax.random.uniform(diag_key, (PANELS, PB), jnp.float32, jnp.log(0.4), jnp.log(1.0)))
    off_vals = 0.3 * jax.random.normal(off_key, (PANELS, PB, PB), jnp.float32) / jnp.sqrt(1.0 * PB)
    row_ids = jnp.arange(PB)[:, None]
    col_ids = jnp.arange(PB)[None, :]
    upper = jnp.where(row_ids < col_ids, off_vals, 0.0)
    on_diag = jnp.where(row_ids == col_ids, diag_vals[:, None, :], 0.0)
    return (upper + on_diag).astype(jnp.float32)


def levels(rng, extent, cuts, low, high):
    level, own = 1.0, jax.random.fold_in(rng, 6)
    for position, blocks in cuts:
        steps = jnp.exp(jax.random.uniform(jax.random.fold_in(own, position), (blocks,), jnp.float32, low / len(cuts), high / len(cuts)))
        level = level * jnp.repeat(steps, extent[position] // blocks).reshape([-1 if axis == position else 1 for axis in range(len(extent))])
    return level


def bell_draw(stream_key, extent, scale, limit, pieces=(), kind=jnp.bfloat16):
    loudness = levels(stream_key, extent, pieces, -0.22, 0.18) if pieces else 1.0
    values = jax.random.normal(stream_key, extent, jnp.float32) * scale * loudness
    return jnp.minimum(jnp.maximum(values, -limit), limit).astype(kind)


def setup_inputs(seed: int = 0) -> dict:
    key_list = jax.random.split(jax.random.key(seed), 4)
    return {
        "iterate": bell_draw(key_list[0], (ROWS, NB), 1.0, 6.0, ((0, 8), (1, 16)), jnp.float32),
        "factor": jnp.clip(jax.random.uniform(key_list[1], (NB, NB), jnp.float32, -0.0625, 0.0625) * levels(key_list[1], (NB, NB), ((1, 16),), -0.4, 0.0), -0.0625, 0.0625),
        "inverses": draw_inverses(jax.random.fold_in(key_list[3], 71), 0),
    }


def reference(iterate, factor, inverses):
    total_rows = iterate.shape[0]
    highest = lax.Precision.HIGHEST
    scale_factor = 3.0 / total_rows
    product = jnp.dot(iterate.T.astype(jnp.float32), iterate.astype(jnp.float32), precision=highest, preferred_element_type=jnp.float32)
    gram_matrix = jnp.eye(NB, dtype=jnp.float32) + scale_factor * product
    leading = jnp.linalg.cholesky(gram_matrix[:PB, :PB])
    panel_factor = jax.scipy.linalg.solve_triangular(leading, gram_matrix[:, :PB].T, lower=True).T
    blocks_done = []
    for panel_idx in range(PANELS):
        remaining = iterate[:, panel_idx * PB:(panel_idx + 1) * PB]
        if panel_idx > 0:
            earlier = jnp.concatenate(blocks_done, axis=1)
            coupling = factor[:panel_idx * PB, panel_idx * PB:(panel_idx + 1) * PB]
            remaining = remaining - jnp.dot(earlier.astype(jnp.float32), coupling.astype(jnp.float32), precision=highest, preferred_element_type=jnp.float32)
        block_out = jnp.dot(remaining.astype(jnp.float32), inverses[panel_idx].astype(jnp.float32), precision=highest, preferred_element_type=jnp.float32)
        blocks_done.append(block_out)
    solved = jnp.concatenate(blocks_done, axis=1)
    return (gram_matrix, panel_factor, solved)
```

```python
import functools

import jax
import jax.numpy as jnp
from jax import lax
from jax.experimental import pallas as pl
from jax.experimental.pallas import tpu as pltpu
from jax.sharding import PartitionSpec as P

ROUTES = (
    ((0, 1), (0, 3), (0, 4), (1, 2), (1, 5), (4, 7), (7, 6)),
    ((1, 2), (1, 5), (2, 3), (2, 6), (5, 4), (6, 7)),
    ((2, 3), (2, 6), (3, 7), (6, 5), (7, 4)),
    ((3, 7), (7, 4), (7, 6), (6, 5)),
    ((4, 5), (4, 7), (5, 6)),
    ((5, 6), (6, 7)),
    ((6, 7),),
    (),
)
CHIPS = 8
CHUNKS = 6
SLOTS = 5
MESH = pl.DeviceIdType.MESH


def split(value):
    high = value.astype(jnp.bfloat16)
    return high, (value - high.astype(jnp.float32)).astype(jnp.bfloat16)


def dot3(left, right_high, right_low):
    high, low = split(left)
    dot = functools.partial(jnp.dot, preferred_element_type=jnp.float32)
    return dot(high, right_high) + (dot(high, right_low) + dot(low, right_high))


def solve_kernel(base_ref, high_ref, low_ref, out_ref, panels, part, part_in, send, recv, part_send, part_recv):
    row = lax.axis_index("row")
    col = lax.axis_index("col")
    chip = col // 2
    core = col % 2
    width = out_ref.shape[1]
    rows = out_ref.shape[0] // CHUNKS
    sibling = (row, 2 * chip + 1 - core)

    barrier = pltpu.get_barrier_semaphore()
    for step in range(1, CHIPS):
        pl.semaphore_signal(
            barrier, inc=1, device_id=(row, 2 * ((chip + step) % CHIPS) + core), device_id_type=MESH
        )
    pl.semaphore_signal(barrier, inc=1, device_id=sibling, device_id_type=MESH)
    pl.semaphore_wait(barrier, CHIPS)

    def run(me):
        onward = [[b for a, b in ROUTES[j] if a == me] for j in range(CHIPS)]
        slots = {}
        for j in range(CHIPS):
            for target in onward[j]:
                slots[j, target] = len(slots)
        early = 4 if me >= 4 else 0
        lag = me - early

        def window(t):
            return pl.ds(pl.multiple_of(t * rows, rows), rows)

        def transfer(j, target, t):
            source = out_ref.at[window(t)] if j == me else panels.at[j, window(t)]
            return pltpu.make_async_remote_copy(
                src_ref=source,
                dst_ref=panels.at[j, window(t)],
                send_sem=send.at[slots.get((j, target), 0), t],
                recv_sem=recv.at[j, t],
                device_id=(row, 2 * target + core),
                device_id_type=MESH,
            )

        def exchange(t):
            return pltpu.make_async_remote_copy(
                src_ref=part.at[t, 1 - core],
                dst_ref=part_in.at[t],
                send_sem=part_send.at[t],
                recv_sem=part_recv.at[t],
                device_id=sibling,
                device_id_type=MESH,
            )

        def arrive(j, t):
            transfer(j, (me + 1) % CHIPS, t).wait_recv()
            for target in onward[j]:
                transfer(j, target, t).start()

        def finish(t):
            total = base_ref[window(t)]
            for j in range(me):
                if j >= early:
                    arrive(j, t)
                span = pl.ds(j * width, width)
                total = total - dot3(panels[j, window(t)], high_ref[span], low_ref[span])
            part[t, 0] = total[:, :width]
            part[t, 1] = total[:, width:]
            exchange(t).start()
            exchange(t).wait_recv()
            out_ref[window(t)] = part[t, core] + part_in[t]
            for target in onward[me]:
                transfer(me, target, t).start()

        def step(tick, carry):
            if early:

                @pl.when(tick < CHUNKS)
                def _():
                    for j in range(early):
                        arrive(j, tick)

                @pl.when(tick >= lag)
                def _():
                    finish(tick - lag)

            else:
                finish(tick)
            return carry

        lax.fori_loop(0, CHUNKS + lag, step, 0) if early else lax.fori_loop(0, CHUNKS, step, 0)

        def drain(t, carry):
            exchange(t).wait_send()
            for j, target in slots:
                transfer(j, target, t).wait_send()
            return carry

        lax.fori_loop(0, CHUNKS, drain, 0)

    for me in range(CHIPS):
        pl.when(chip == me)(functools.partial(run, me))


def solve(iterate, factor, inverses):
    n_rows, width = iterate.shape
    order, _ = factor.shape
    rows = n_rows // CHUNKS
    high = lax.Precision.HIGH
    chip = lax.axis_index("col") // 2
    core = lax.axis_index("col") % 2
    inverse = lax.dynamic_index_in_dim(inverses, chip, 0, keepdims=False)
    blocks = factor.reshape(CHIPS, 2, width, width)
    mine = lax.dynamic_index_in_dim(blocks, core, 1, keepdims=False).reshape(order // 2, width)
    theirs = lax.dynamic_index_in_dim(blocks, 1 - core, 1, keepdims=False).reshape(order // 2, width)
    pairs = [(c, c ^ 1) for c in range(2 * CHIPS)]
    theirs = lax.ppermute(theirs, "col", pairs)
    both = jnp.where(core == 0, jnp.concatenate([mine, theirs], 1), jnp.concatenate([theirs, mine], 1))
    coupling = jnp.dot(both, inverse, precision=high, preferred_element_type=jnp.float32)
    rounded = lax.reduce_precision(coupling, 8, 7)
    w_high = rounded.astype(jnp.bfloat16)
    w_low = (coupling - rounded).astype(jnp.bfloat16)
    half = lax.dynamic_slice_in_dim(inverse, core * width, width, 0)
    base = jnp.dot(iterate, half, precision=high, preferred_element_type=jnp.float32)
    vmem = pl.BlockSpec(memory_space=pltpu.VMEM)
    return pl.pallas_call(
        solve_kernel,
        out_shape=jax.ShapeDtypeStruct((n_rows, width), jnp.float32),
        in_specs=[vmem] * 3,
        out_specs=vmem,
        scratch_shapes=[
            pltpu.VMEM((CHIPS - 1, n_rows, width), jnp.float32),
            pltpu.VMEM((CHUNKS, 2, rows, width), jnp.float32),
            pltpu.VMEM((CHUNKS, rows, width), jnp.float32),
            pltpu.SemaphoreType.DMA((SLOTS, CHUNKS)),
            pltpu.SemaphoreType.DMA((CHIPS, CHUNKS)),
            pltpu.SemaphoreType.DMA((CHUNKS,)),
            pltpu.SemaphoreType.DMA((CHUNKS,)),
        ],
        compiler_params=pltpu.CompilerParams(
            collective_id=0, has_side_effects=True, vmem_limit_bytes=40 << 20
        ),
        cost_estimate=pl.CostEstimate(flops=3 * 10**9, bytes_accessed=10**7, transcendentals=0),
    )(base, w_high, w_low)


def from_root(block, axis, source):
    block = jnp.where(lax.axis_index(axis) == source, block, jnp.zeros_like(block))
    return lax.psum(block, axis)


def on_device(iterate, factor, inverses):
    highest = lax.Precision.HIGHEST
    row_dev, local_width = iterate.shape
    n_rows = lax.axis_size("row")
    n_cols = lax.axis_size("col")
    full_order = local_width * n_cols
    panel_width = inverses.shape[1]
    panels = inverses.shape[0]
    owners = panel_width // local_width
    row_index = lax.axis_index("row")
    col_index = lax.axis_index("col")
    scale_factor = 3.0 / (row_dev * n_rows)
    block_rows = full_order // n_rows
    gathered = lax.all_gather(iterate, "col", axis=1, tiled=True)
    summed = lax.psum_scatter(
        lax.dot_general(
            gathered,
            iterate,
            (((0,), (0,)), ((), ())),
            precision=highest,
            preferred_element_type=jnp.float32,
        ),
        "row",
        scatter_dimension=0,
        tiled=True,
    )
    row_ids = row_index * block_rows + jnp.arange(block_rows)[:, None]
    col_ids = col_index * local_width + jnp.arange(local_width)[None, :]
    gram_block = jnp.where(row_ids == col_ids, 1.0, 0.0).astype(jnp.float32) + scale_factor * summed
    offset = jnp.minimum(col_index * local_width, panel_width - local_width)
    empty = jnp.zeros((block_rows, panel_width), jnp.float32)
    placed = lax.dynamic_update_slice_in_dim(empty, gram_block, offset, 1)
    placed = jnp.where(col_index < owners, placed, 0.0)
    panel_rows = lax.psum(placed, "col")
    leading_rows = from_root(panel_rows, "row", 0)
    leading = jnp.linalg.cholesky(leading_rows)
    share_rows = block_rows // n_cols
    my_rows = lax.dynamic_slice_in_dim(panel_rows, col_index * share_rows, share_rows, 0)
    panel_factor = jax.scipy.linalg.solve_triangular(leading, my_rows.T, lower=True).T
    solved = solve(iterate, factor, inverses)
    return (gram_block, panel_factor, solved)


def solution(mesh):
    placed = (P("row", "col"), P(None, "col"), P())
    return jax.shard_map(
        on_device,
        mesh=mesh,
        in_specs=placed,
        out_specs=(P("row", "col"), P(("row", "col"), None), P("row", "col")),
        check_vma=False,
    )
```

```python
import functools

import jax
import jax.numpy as jnp
from jax import lax
from jax.experimental import pallas as pl
from jax.experimental.pallas import tpu as pltpu
from jax.sharding import PartitionSpec as P

ROUTES = (
    ((0, 1), (0, 3), (0, 4), (1, 2), (1, 5), (4, 7), (7, 6)),
    ((1, 2), (1, 5), (2, 3), (2, 6), (5, 4), (6, 7)),
    ((2, 3), (2, 6), (3, 7), (6, 5), (7, 4)),
    ((3, 7), (7, 4), (7, 6), (6, 5)),
    ((4, 5), (4, 7), (5, 6)),
    ((5, 6), (6, 7)),
    ((6, 7),),
    (),
)
CHIPS = 8
CHUNKS = 6
SLOTS = 5
LAG = 4
MESH = pl.DeviceIdType.MESH


def split(value):
    high = value.astype(jnp.bfloat16)
    return high, (value - high.astype(jnp.float32)).astype(jnp.bfloat16)


def dot3(left, right_high, right_low):
    high, low = split(left)
    dot = functools.partial(jnp.dot, preferred_element_type=jnp.float32)
    return dot(high, right_high) + (dot(high, right_low) + dot(low, right_high))


def solve_kernel(base_ref, high_ref, low_ref, out_ref, panels, part, part_in, send, recv, part_send, part_recv):
    row = lax.axis_index("row")
    col = lax.axis_index("col")
    chip = col // 2
    core = col % 2
    width = out_ref.shape[1]
    rows = out_ref.shape[0] // CHUNKS
    sibling = (row, 2 * chip + 1 - core)

    barrier = pltpu.get_barrier_semaphore()
    for step in range(1, CHIPS):
        pl.semaphore_signal(
            barrier, inc=1, device_id=(row, 2 * ((chip + step) % CHIPS) + core), device_id_type=MESH
        )
    pl.semaphore_signal(barrier, inc=1, device_id=sibling, device_id_type=MESH)
    pl.semaphore_wait(barrier, CHIPS)

    def run(me):
        onward = [[b for a, b in ROUTES[j] if a == me] for j in range(CHIPS)]
        slots = {}
        for j in range(CHIPS):
            for target in onward[j]:
                slots[j, target] = len(slots)
        early = 4 if me >= 4 else 0
        stages = [(0, [j for j in range(early) if j + 4 in (me, me - 1)])]
        stages.append((2, [j for j in range(early) if j not in stages[0][1] and onward[j]]))
        relayed = stages[0][1] + stages[1][1]
        lag = LAG if early else 0

        def window(t):
            return pl.ds(pl.multiple_of(t * rows, rows), rows)

        def transfer(j, target, t):
            source = out_ref.at[window(t)] if j == me else panels.at[j, window(t)]
            return pltpu.make_async_remote_copy(
                src_ref=source,
                dst_ref=panels.at[j, window(t)],
                send_sem=send.at[slots.get((j, target), 0), t],
                recv_sem=recv.at[j, t],
                device_id=(row, 2 * target + core),
                device_id_type=MESH,
            )

        def exchange(t):
            return pltpu.make_async_remote_copy(
                src_ref=part.at[t, 1 - core],
                dst_ref=part_in.at[t],
                send_sem=part_send.at[t],
                recv_sem=part_recv.at[t],
                device_id=sibling,
                device_id_type=MESH,
            )

        def arrive(j, t):
            transfer(j, (me + 1) % CHIPS, t).wait_recv()
            for target in onward[j]:
                transfer(j, target, t).start()

        def finish(t):
            total = base_ref[window(t)]
            for j in range(me):
                if j not in relayed:
                    arrive(j, t)
                span = pl.ds(j * width, width)
                total = total - dot3(panels[j, window(t)], high_ref[span], low_ref[span])
            part[t, 0] = total[:, :width]
            part[t, 1] = total[:, width:]
            exchange(t).start()
            exchange(t).wait_recv()
            out_ref[window(t)] = part[t, core] + part_in[t]
            for target in onward[me]:
                transfer(me, target, t).start()

        def step(tick, carry):
            for delay, sources in stages:
                if sources:

                    @pl.when((tick >= delay) & (tick < CHUNKS + delay))
                    def _():
                        for j in sources:
                            arrive(j, tick - delay)

            if lag:
                pl.when(tick >= lag)(lambda: finish(tick - lag))
            else:
                finish(tick)
            return carry

        lax.fori_loop(0, CHUNKS + lag, step, 0)

        def drain(t, carry):
            exchange(t).wait_send()
            for j, target in slots:
                transfer(j, target, t).wait_send()
            return carry

        lax.fori_loop(0, CHUNKS, drain, 0)

    for me in range(CHIPS):
        pl.when(chip == me)(functools.partial(run, me))


def solve(iterate, factor, inverses):
    n_rows, width = iterate.shape
    order, _ = factor.shape
    rows = n_rows // CHUNKS
    high = lax.Precision.HIGH
    chip = lax.axis_index("col") // 2
    core = lax.axis_index("col") % 2
    inverse = lax.dynamic_index_in_dim(inverses, chip, 0, keepdims=False)
    blocks = factor.reshape(CHIPS, 2, width, width)
    mine = lax.dynamic_index_in_dim(blocks, core, 1, keepdims=False).reshape(order // 2, width)
    theirs = lax.dynamic_index_in_dim(blocks, 1 - core, 1, keepdims=False).reshape(order // 2, width)
    pairs = [(c, c ^ 1) for c in range(2 * CHIPS)]
    theirs = lax.ppermute(theirs, "col", pairs)
    both = jnp.where(core == 0, jnp.concatenate([mine, theirs], 1), jnp.concatenate([theirs, mine], 1))
    coupling = jnp.dot(both, inverse, precision=high, preferred_element_type=jnp.float32)
    rounded = lax.reduce_precision(coupling, 8, 7)
    w_high = rounded.astype(jnp.bfloat16)
    w_low = (coupling - rounded).astype(jnp.bfloat16)
    half = lax.dynamic_slice_in_dim(inverse, core * width, width, 0)
    base = jnp.dot(iterate, half, precision=high, preferred_element_type=jnp.float32)
    vmem = pl.BlockSpec(memory_space=pltpu.VMEM)
    return pl.pallas_call(
        solve_kernel,
        out_shape=jax.ShapeDtypeStruct((n_rows, width), jnp.float32),
        in_specs=[vmem] * 3,
        out_specs=vmem,
        scratch_shapes=[
            pltpu.VMEM((CHIPS - 1, n_rows, width), jnp.float32),
            pltpu.VMEM((CHUNKS, 2, rows, width), jnp.float32),
            pltpu.VMEM((CHUNKS, rows, width), jnp.float32),
            pltpu.SemaphoreType.DMA((SLOTS, CHUNKS)),
            pltpu.SemaphoreType.DMA((CHIPS, CHUNKS)),
            pltpu.SemaphoreType.DMA((CHUNKS,)),
            pltpu.SemaphoreType.DMA((CHUNKS,)),
        ],
        compiler_params=pltpu.CompilerParams(
            collective_id=0, has_side_effects=True, vmem_limit_bytes=40 << 20
        ),
        cost_estimate=pl.CostEstimate(flops=3 * 10**9, bytes_accessed=10**7, transcendentals=0),
    )(base, w_high, w_low)


def from_root(block, axis, source):
    block = jnp.where(lax.axis_index(axis) == source, block, jnp.zeros_like(block))
    return lax.psum(block, axis)


def on_device(iterate, factor, inverses):
    highest = lax.Precision.HIGHEST
    row_dev, local_width = iterate.shape
    n_rows = lax.axis_size("row")
    n_cols = lax.axis_size("col")
    full_order = local_width * n_cols
    panel_width = inverses.shape[1]
    panels = inverses.shape[0]
    owners = panel_width // local_width
    row_index = lax.axis_index("row")
    col_index = lax.axis_index("col")
    scale_factor = 3.0 / (row_dev * n_rows)
    block_rows = full_order // n_rows
    gathered = lax.all_gather(iterate, "col", axis=1, tiled=True)
    summed = lax.psum_scatter(
        lax.dot_general(
            gathered,
            iterate,
            (((0,), (0,)), ((), ())),
            precision=highest,
            preferred_element_type=jnp.float32,
        ),
        "row",
        scatter_dimension=0,
        tiled=True,
    )
    row_ids = row_index * block_rows + jnp.arange(block_rows)[:, None]
    col_ids = col_index * local_width + jnp.arange(local_width)[None, :]
    gram_block = jnp.where(row_ids == col_ids, 1.0, 0.0).astype(jnp.float32) + scale_factor * summed
    offset = jnp.minimum(col_index * local_width, panel_width - local_width)
    empty = jnp.zeros((block_rows, panel_width), jnp.float32)
    placed = lax.dynamic_update_slice_in_dim(empty, gram_block, offset, 1)
    placed = jnp.where(col_index < owners, placed, 0.0)
    panel_rows = lax.psum(placed, "col")
    leading_rows = from_root(panel_rows, "row", 0)
    leading = jnp.linalg.cholesky(leading_rows)
    share_rows = block_rows // n_cols
    my_rows = lax.dynamic_slice_in_dim(panel_rows, col_index * share_rows, share_rows, 0)
    panel_factor = jax.scipy.linalg.solve_triangular(leading, my_rows.T, lower=True).T
    solved = solve(iterate, factor, inverses)
    return (gram_block, panel_factor, solved)


def solution(mesh):
    placed = (P("row", "col"), P(None, "col"), P())
    return jax.shard_map(
        on_device,
        mesh=mesh,
        in_specs=placed,
        out_specs=(P("row", "col"), P(("row", "col"), None), P("row", "col")),
        check_vma=False,
    )
```

```python
import functools

import jax
import jax.numpy as jnp
from jax import lax
from jax.experimental import pallas as pl
from jax.experimental.pallas import tpu as pltpu
from jax.sharding import PartitionSpec as P

ROUTES = (
    ((0, 1), (0, 3), (0, 4), (1, 2), (1, 5), (4, 7), (7, 6)),
    ((1, 2), (1, 5), (2, 3), (2, 6), (5, 4), (6, 7)),
    ((2, 3), (2, 6), (3, 7), (6, 5), (7, 4)),
    ((3, 7), (7, 4), (7, 6), (6, 5)),
    ((4, 5), (4, 7), (5, 6)),
    ((5, 6), (6, 7)),
    ((6, 7),),
    (),
)
CHIPS = 8
CHUNKS = 6
SLOTS = 5
LAG = 4
MESH = pl.DeviceIdType.MESH


def split(value):
    high = value.astype(jnp.bfloat16)
    return high, (value - high.astype(jnp.float32)).astype(jnp.bfloat16)


def dot3(left, right_high, right_low):
    high, low = split(left)
    dot = functools.partial(jnp.dot, preferred_element_type=jnp.float32)
    return dot(high, right_high) + (dot(high, right_low) + dot(low, right_high))


def gram_kernel(mine_ref, gram_ref, lead_ref, theirs, got, high, low, prod, land, slices, send, recv, push, landed, cut, cut_in, share, shared):
    row = lax.axis_index("row")
    col = lax.axis_index("col")
    n_rows = lax.axis_size("row")
    chip = col // 2
    core = col % 2
    x, y = chip % 4, chip // 4
    n, width = mine_ref.shape
    half = n // 2
    piece = width // n_rows
    scale = 3.0 / (n * n_rows)

    def at(dx, dy):
        return 4 * ((y + dy) % 2) + (x + dx) % 4

    left, right, partner, far = at(3, 0), at(1, 0), at(0, 1), at(2, 0)
    barrier = pltpu.get_barrier_semaphore()
    for other in (2 * left + core, 2 * right + core, 2 * partner + core, 2 * chip + 1 - core):
        pl.semaphore_signal(barrier, inc=1, device_id=(row, other), device_id_type=MESH)
    for step in range(1, n_rows):
        for other in range(2):
            pl.semaphore_signal(
                barrier, inc=1, device_id=((row + step) % n_rows, 2 * chip + other), device_id_type=MESH
            )
    pl.semaphore_wait(barrier, 4 + 2 * (n_rows - 1))

    def copy(source, target, out, arrival, device):
        return pltpu.make_async_remote_copy(
            src_ref=source, dst_ref=target, send_sem=out, recv_sem=arrival, device_id=device, device_id_type=MESH
        )

    top, low_half = pl.ds(0, half), pl.ds(half, half)
    at_right, at_left = (row, 2 * right + core), (row, 2 * left + core)
    at_partner, at_sibling = (row, 2 * partner + core), (row, 2 * chip + 1 - core)
    sends = [
        copy(mine_ref, theirs, send.at[8], recv.at[8], at_sibling),
        copy(mine_ref, got.at[chip], send.at[0], recv.at[0], at_right),
        copy(mine_ref, got.at[chip], send.at[1], recv.at[1], at_left),
        copy(mine_ref, got.at[chip], send.at[2], recv.at[2], at_partner),
        copy(got.at[left, top], got.at[left, top], send.at[3], recv.at[3], at_right),
        copy(got.at[right, low_half], got.at[right, low_half], send.at[4], recv.at[4], at_left),
        copy(got.at[partner], got.at[partner], send.at[5], recv.at[5], at_right),
        copy(got.at[partner], got.at[partner], send.at[6], recv.at[6], at_left),
        copy(got.at[far], got.at[far], send.at[7], recv.at[7], at_partner),
    ]
    for one in sends[:4]:
        one.start()
    got[chip] = mine_ref[...]
    own_high, own_low = split(mine_ref[...])
    high[core] = own_high
    low[core] = own_low
    sends[0].wait_recv()
    their_high, their_low = split(theirs[...])
    high[1 - core] = their_high
    low[1 - core] = their_low

    def order(idx):
        dx = jnp.where((idx == 1) | (idx == 5), 3, jnp.where((idx == 2) | (idx == 6), 1, jnp.where((idx == 4) | (idx == 7), 2, 0)))
        dy = jnp.where((idx == 3) | (idx > 4), 1, 0)
        return at(dx, dy)

    def away(block, to):
        return copy(
            prod.at[block, to], land.at[row, core], push.at[block, to], landed.at[row, core], (block, 2 * chip + to)
        )

    def slice_to(other):
        return copy(
            prod.at[0, :, pl.ds(pl.multiple_of(other * piece, piece), piece)],
            slices.at[row],
            cut.at[other],
            cut_in.at[row],
            (other, core),
        )

    def lead_rows(at_row, at_core):
        return lead_ref.at[pl.ds(pl.multiple_of(at_core * width + at_row * piece, piece), piece)]

    def share_to(step, to):
        return copy(
            lead_rows(row, core), lead_rows(row, core), share.at[step, to], shared.at[row, core],
            ((row + step) % n_rows, to),
        )

    def body(idx, carry):
        @pl.when(idx == 1)
        def _():
            for one in sends[1:4]:
                one.wait_recv()
            for one in sends[4:8]:
                one.start()

        @pl.when(idx == 4)
        def _():
            sends[4].wait_recv()
            sends[5].wait_recv()
            sends[8].start()

        @pl.when(idx > 4)
        def _():
            copy(mine_ref, got.at[chip], send.at[0], recv.at[idx], at_right).wait_recv()

        block = order(idx)
        left_high, left_low = split(got[block])
        dot = functools.partial(
            lax.dot_general, dimension_numbers=(((0,), (0,)), ((), ())), preferred_element_type=jnp.float32
        )
        for to in range(2):
            prod[block, to] = dot(left_high, high[to]) + (dot(left_high, low[to]) + dot(left_low, high[to]))

        @pl.when(block != row)
        def _():
            away(block, core).start()

        @pl.when(block == row)
        def _():
            land[row, core] = prod[block, core]

        away(block, 1 - core).start()

        @pl.when((idx == 0) & (chip == 0))
        def _():
            for step in range(1, n_rows):
                slice_to((row + step) % n_rows).start()
            slices[row] = prod[0, :, pl.ds(pl.multiple_of(row * piece, piece), piece)]

        @pl.when((idx == 3) & (chip == 0))
        def _():
            for step in range(1, n_rows):
                source = (row + step) % n_rows
                copy(
                    slices.at[row], slices.at[source], cut.at[source], cut_in.at[source], (source, core)
                ).wait_recv()
            total = slices[0]
            for other in range(1, n_rows):
                total = total + slices[other]
            whole = scale * jnp.concatenate([total[0], total[1]], axis=1)
            first = core * width + row * piece
            shape = (piece, 2 * width)
            there = lax.broadcasted_iota(jnp.int32, shape, 0) + first == lax.broadcasted_iota(jnp.int32, shape, 1)
            lead_rows(row, core)[...] = whole + jnp.where(there, 1.0, 0.0)
            for step in range(n_rows):
                for to in range(2):
                    if step:
                        share_to(step, to).start()
            share_to(0, 1 - core).start()

        return carry

    lax.fori_loop(0, CHIPS, body, 0)

    @pl.when(chip == 0)
    def _():
        for step in range(n_rows):
            for other in range(2):
                source = (row + step) % n_rows

                @pl.when((step > 0) | (core != other))
                def _():
                    rows = lead_rows(source, other)
                    copy(rows, rows, share.at[0, 0], shared.at[source, other], (source, 0)).wait_recv()

        for step in range(1, n_rows):
            slice_to((row + step) % n_rows).wait_send()
            for to in range(2):
                share_to(step, to).wait_send()
        share_to(0, 1 - core).wait_send()

    for other in range(2):
        for step in range(n_rows):
            source = (row + step) % n_rows

            @pl.when((step > 0) | (core != other))
            def _():
                copy(
                    prod.at[0, 0], land.at[source, other], push.at[0, 0], landed.at[source, other], at_sibling
                ).wait_recv()

        total = land[0, other]
        for source in range(1, n_rows):
            total = total + land[source, other]
        shape = (width, width)
        shift = (row * 2 + other - (2 * chip + core)) * width
        there = lax.broadcasted_iota(jnp.int32, shape, 0) + shift == lax.broadcasted_iota(jnp.int32, shape, 1)
        gram_ref[pl.ds(other * width, width)] = jnp.where(there, 1.0, 0.0) + scale * total

    for one in sends:
        one.wait_send()

    def drain(block, carry):
        pl.when(block != row)(lambda: away(block, core).wait_send())
        away(block, 1 - core).wait_send()
        return carry

    lax.fori_loop(0, CHIPS, drain, 0)


def gram(iterate):
    n, width = iterate.shape
    n_rows = lax.axis_size("row")
    vmem = pl.BlockSpec(memory_space=pltpu.VMEM)
    dma = pltpu.SemaphoreType.DMA
    return pl.pallas_call(
        gram_kernel,
        out_shape=(
            jax.ShapeDtypeStruct((2 * width, width), jnp.float32),
            jax.ShapeDtypeStruct((2 * width, 2 * width), jnp.float32),
        ),
        in_specs=[vmem],
        out_specs=(vmem, vmem),
        scratch_shapes=[
            pltpu.VMEM((n, width), jnp.float32),
            pltpu.VMEM((CHIPS, n, width), jnp.float32),
            pltpu.VMEM((2, n, width), jnp.bfloat16),
            pltpu.VMEM((2, n, width), jnp.bfloat16),
            pltpu.VMEM((CHIPS, 2, width, width), jnp.float32),
            pltpu.VMEM((n_rows, 2, width, width), jnp.float32),
            pltpu.VMEM((n_rows, 2, width // n_rows, width), jnp.float32),
            dma((9,)),
            dma((9,)),
            dma((CHIPS, 2)),
            dma((n_rows, 2)),
            dma((n_rows,)),
            dma((n_rows,)),
            dma((n_rows, 2)),
            dma((n_rows, 2)),
        ],
        compiler_params=pltpu.CompilerParams(
            collective_id=1, has_side_effects=True, vmem_limit_bytes=48 << 20
        ),
        cost_estimate=pl.CostEstimate(flops=5 * 10**9, bytes_accessed=10**7, transcendentals=0),
    )(iterate)


def factor_block(grid):
    base = grid.shape[0]
    for p in range(base // 8):
        rows = slice(8 * p, 8 * p + 8)
        panel = grid[rows]
        sub = lax.broadcasted_iota(jnp.int32, panel.shape, 0)
        columns = [jnp.broadcast_to(panel[:, 8 * p + c : 8 * p + c + 1], panel.shape) for c in range(8)]
        scales = jnp.zeros_like(panel)
        for j in range(8):
            pivot = jnp.broadcast_to(columns[j][j : j + 1], panel.shape)
            guess = lax.rsqrt(pivot)
            guess = guess * (1.5 - 0.5 * pivot * guess * guess)
            below = jnp.where(sub > j, columns[j] * (guess * guess), 0.0)
            scales = jnp.where(sub == j, guess, scales)
            for c in range(j + 1, 8):
                columns[c] = columns[c] - below * columns[c][j : j + 1]
            panel = panel - below * panel[j : j + 1]
        panel = panel * scales
        grid[rows] = panel
        if 8 * p + 8 < base:
            rest = slice(8 * p + 8, base)
            turned = panel[:, :base].T[8 * p + 8 :]
            value = grid[rest]
            for j in range(8):
                value = value - turned[:, j : j + 1] * panel[j : j + 1]
            grid[rest] = value


def panel_solve(work, grid, size):
    base = grid.shape[0]
    highest = lax.Precision.HIGHEST
    dims = (((1,), (1,)), ((), ()))

    def block(s, carry):
        span = pl.ds(pl.multiple_of(s * base, base), base)
        shape = (base, base)
        eye = lax.broadcasted_iota(jnp.int32, shape, 0) == lax.broadcasted_iota(jnp.int32, shape, 1)
        grid[:, :base] = work[span, span]
        grid[:, base:] = jnp.where(eye, 1.0, 0.0)
        factor_block(grid)
        done = lax.dot_general(
            work[:, span], grid[:, base:], dims, precision=highest, preferred_element_type=jnp.float32
        )
        below = lax.broadcasted_iota(jnp.int32, done.shape, 0) >= (s + 1) * base
        done = jnp.where(below, done, 0.0)
        work[...] = work[...] - lax.dot_general(
            done, done[:size], dims, precision=highest, preferred_element_type=jnp.float32
        )
        work[size:, span] = done[size:]
        return carry

    lax.fori_loop(0, size // base, block, 0)


def solve_kernel(
    base_ref, high_ref, low_ref, lead_ref, gram_ref, out_ref, panel_ref,
    panels, part, part_in, work, grid, side, send, recv, part_send, part_recv, side_send, side_recv, row_send, row_recv, row_own,
):
    row = lax.axis_index("row")
    col = lax.axis_index("col")
    chip = col // 2
    core = col % 2
    width = out_ref.shape[1]
    rows = out_ref.shape[0] // CHUNKS
    sibling = (row, 2 * chip + 1 - core)

    barrier = pltpu.get_barrier_semaphore()
    n_cols = lax.axis_size("col")
    for step in range(1, n_cols):
        pl.semaphore_signal(barrier, inc=1, device_id=(row, (col + step) % n_cols), device_id_type=MESH)
    pl.semaphore_wait(barrier, n_cols - 1)
    share = panel_ref.shape[0]

    def swap():
        return pltpu.make_async_remote_copy(
            src_ref=gram_ref.at[pl.ds(pl.multiple_of((1 - core) * width, width), width)],
            dst_ref=side,
            send_sem=side_send,
            recv_sem=side_recv,
            device_id=sibling,
            device_id_type=MESH,
        )

    def strip(m):
        return work.at[pl.ds(2 * width + m * share, share)]

    def hand_out(m):
        return pltpu.make_async_remote_copy(
            src_ref=strip(m),
            dst_ref=panel_ref,
            send_sem=row_send.at[m],
            recv_sem=row_recv,
            device_id=(row, CHIPS * core + m),
            device_id_type=MESH,
        )

    def leading():
        work[pl.ds(0, 2 * width)] = lead_ref[...]
        own = pl.ds(pl.multiple_of(core * width, width), width)
        other = pl.ds(pl.multiple_of((1 - core) * width, width), width)
        tail = pl.ds(2 * width, width)
        work[tail, own] = gram_ref[own]
        swap().wait_recv()
        work[tail, other] = side[...]
        panel_solve(work, grid, 2 * width)
        for m in range(CHIPS):
            if m:
                hand_out(m).start()
            else:
                pl.when(core == 1)(lambda: hand_out(0).start())
                pl.when(core == 0)(lambda: pltpu.make_async_copy(strip(0), panel_ref, row_own).start())

    def leading_sent():
        swap().wait_send()
        for m in range(CHIPS):
            if m:
                hand_out(m).wait_send()
            else:
                pl.when(core == 1)(lambda: hand_out(0).wait_send())
                pl.when(core == 0)(lambda: pltpu.make_async_copy(strip(0), panel_ref, row_own).wait())

    def run(me):
        onward = [[b for a, b in ROUTES[j] if a == me] for j in range(CHIPS)]
        slots = {}
        for j in range(CHIPS):
            for target in onward[j]:
                slots[j, target] = len(slots)
        early = 4 if me >= 4 else 0
        stages = [(0, [j for j in range(early) if j + 4 in (me, me - 1)])]
        stages.append((2, [j for j in range(early) if j not in stages[0][1] and onward[j]]))
        relayed = stages[0][1] + stages[1][1]
        lag = LAG if early else 0

        def window(t):
            return pl.ds(pl.multiple_of(t * rows, rows), rows)

        def transfer(j, target, t):
            source = out_ref.at[window(t)] if j == me else panels.at[j, window(t)]
            return pltpu.make_async_remote_copy(
                src_ref=source,
                dst_ref=panels.at[j, window(t)],
                send_sem=send.at[slots.get((j, target), 0), t],
                recv_sem=recv.at[j, t],
                device_id=(row, 2 * target + core),
                device_id_type=MESH,
            )

        def exchange(t):
            return pltpu.make_async_remote_copy(
                src_ref=part.at[t, 1 - core],
                dst_ref=part_in.at[t],
                send_sem=part_send.at[t],
                recv_sem=part_recv.at[t],
                device_id=sibling,
                device_id_type=MESH,
            )

        def arrive(j, t):
            transfer(j, (me + 1) % CHIPS, t).wait_recv()
            for target in onward[j]:
                transfer(j, target, t).start()

        def finish(t):
            total = base_ref[window(t)]
            for j in range(me):
                if j not in relayed:
                    arrive(j, t)
                span = pl.ds(j * width, width)
                total = total - dot3(panels[j, window(t)], high_ref[span], low_ref[span])
            part[t, 0] = total[:, :width]
            part[t, 1] = total[:, width:]
            exchange(t).start()
            exchange(t).wait_recv()
            out_ref[window(t)] = part[t, core] + part_in[t]
            for target in onward[me]:
                transfer(me, target, t).start()

        def step(tick, carry):
            for delay, sources in stages:
                if sources:

                    @pl.when((tick >= delay) & (tick < CHUNKS + delay))
                    def _():
                        for j in sources:
                            arrive(j, tick - delay)

            if lag:
                pl.when(tick >= lag)(lambda: finish(tick - lag))
            else:
                finish(tick)
            return carry

        if me == 0:
            swap().start()
        lax.fori_loop(0, CHUNKS + lag, step, 0)
        if me == 0:
            leading()

        def drain(t, carry):
            exchange(t).wait_send()
            for j, target in slots:
                transfer(j, target, t).wait_send()
            return carry

        lax.fori_loop(0, CHUNKS, drain, 0)
        if me == 0:
            leading_sent()

    for me in range(CHIPS):
        pl.when(chip == me)(functools.partial(run, me))
    pl.when(col > 0)(lambda: hand_out(0).wait_recv())


def solve(iterate, factor, inverses, lead, gram_block):
    n_rows, width = iterate.shape
    order, _ = factor.shape
    rows = n_rows // CHUNKS
    high = lax.Precision.HIGH
    chip = lax.axis_index("col") // 2
    core = lax.axis_index("col") % 2
    inverse = lax.dynamic_index_in_dim(inverses, chip, 0, keepdims=False)
    blocks = factor.reshape(CHIPS, 2, width, width)
    mine = lax.dynamic_index_in_dim(blocks, core, 1, keepdims=False).reshape(order // 2, width)
    theirs = lax.dynamic_index_in_dim(blocks, 1 - core, 1, keepdims=False).reshape(order // 2, width)
    pairs = [(c, c ^ 1) for c in range(2 * CHIPS)]
    theirs = lax.ppermute(theirs, "col", pairs)
    both = jnp.where(core == 0, jnp.concatenate([mine, theirs], 1), jnp.concatenate([theirs, mine], 1))
    coupling = jnp.dot(both, inverse, precision=high, preferred_element_type=jnp.float32)
    rounded = lax.reduce_precision(coupling, 8, 7)
    w_high = rounded.astype(jnp.bfloat16)
    w_low = (coupling - rounded).astype(jnp.bfloat16)
    half = lax.dynamic_slice_in_dim(inverse, core * width, width, 0)
    base = jnp.dot(iterate, half, precision=high, preferred_element_type=jnp.float32)
    vmem = pl.BlockSpec(memory_space=pltpu.VMEM)
    return pl.pallas_call(
        solve_kernel,
        out_shape=(
            jax.ShapeDtypeStruct((n_rows, width), jnp.float32),
            jax.ShapeDtypeStruct((width // CHIPS, 2 * width), jnp.float32),
        ),
        in_specs=[vmem] * 5,
        out_specs=(vmem, vmem),
        scratch_shapes=[
            pltpu.VMEM((CHIPS - 1, n_rows, width), jnp.float32),
            pltpu.VMEM((CHUNKS, 2, rows, width), jnp.float32),
            pltpu.VMEM((CHUNKS, rows, width), jnp.float32),
            pltpu.VMEM((3 * width, 2 * width), jnp.float32),
            pltpu.VMEM((width // 2, width), jnp.float32),
            pltpu.VMEM((width, width), jnp.float32),
            pltpu.SemaphoreType.DMA((SLOTS, CHUNKS)),
            pltpu.SemaphoreType.DMA((CHIPS, CHUNKS)),
            pltpu.SemaphoreType.DMA((CHUNKS,)),
            pltpu.SemaphoreType.DMA((CHUNKS,)),
            pltpu.SemaphoreType.DMA,
            pltpu.SemaphoreType.DMA,
            pltpu.SemaphoreType.DMA((CHIPS,)),
            pltpu.SemaphoreType.DMA,
            pltpu.SemaphoreType.DMA,
        ],
        compiler_params=pltpu.CompilerParams(
            collective_id=0, has_side_effects=True, vmem_limit_bytes=40 << 20
        ),
        cost_estimate=pl.CostEstimate(flops=3 * 10**9, bytes_accessed=10**7, transcendentals=0),
    )(base, w_high, w_low, lead, gram_block)


def on_device(iterate, factor, inverses):
    gram_block, lead = gram(iterate)
    solved, panel = solve(iterate, factor, inverses, lead, gram_block)
    return (gram_block, panel, solved)


def solution(mesh):
    placed = (P("row", "col"), P(None, "col"), P())
    return jax.shard_map(
        on_device,
        mesh=mesh,
        in_specs=placed,
        out_specs=(P("row", "col"), P(("row", "col"), None), P("row", "col")),
        check_vma=False,
    )
```

```python
import functools
import types

import jax
import jax.numpy as jnp
from jax import lax
from jax.experimental import pallas as pl
from jax.experimental.pallas import tpu as pltpu
from jax.sharding import PartitionSpec as P

CHIPS = 8
RING = 4
MESH = pl.DeviceIdType.MESH


def split(value):
    high = value.astype(jnp.bfloat16)
    return high, (value - high.astype(jnp.float32)).astype(jnp.bfloat16)


def dot3(left, right):
    dot = functools.partial(jnp.dot, preferred_element_type=jnp.float32)
    return dot(left[0], right[0]) + (dot(left[0], right[1]) + dot(left[1], right[0]))


def dot3_turned(left, right):
    dot = functools.partial(
        lax.dot_general, dimension_numbers=(((0,), (0,)), ((), ())), preferred_element_type=jnp.float32
    )
    return dot(left[0], right[0]) + (dot(left[0], right[1]) + dot(left[1], right[0]))


def dot_exact_turned(left, right):
    return lax.dot_general(
        left, right, (((1,), (1,)), ((), ())), precision=lax.Precision.HIGHEST, preferred_element_type=jnp.float32
    )


def factor_block(grid):
    base = grid.shape[0]
    for p in range(base // 8):
        rows = slice(8 * p, 8 * p + 8)
        panel = grid[rows]
        sub = lax.broadcasted_iota(jnp.int32, panel.shape, 0)
        columns = [jnp.broadcast_to(panel[:, 8 * p + c : 8 * p + c + 1], panel.shape) for c in range(8)]
        scales = jnp.zeros_like(panel)
        for j in range(8):
            pivot = jnp.broadcast_to(columns[j][j : j + 1], panel.shape)
            guess = lax.rsqrt(pivot)
            guess = guess * (1.5 - 0.5 * pivot * guess * guess)
            below = jnp.where(sub > j, columns[j] * (guess * guess), 0.0)
            scales = jnp.where(sub == j, guess, scales)
            for c in range(j + 1, 8):
                columns[c] = columns[c] - below * columns[c][j : j + 1]
            panel = panel - below * panel[j : j + 1]
        panel = panel * scales
        grid[rows] = panel
        if 8 * p + 8 < base:
            rest = slice(8 * p + 8, base)
            turned = panel[:, :base].T[8 * p + 8 :]
            value = grid[rest]
            for j in range(8):
                value = value - turned[:, j : j + 1] * panel[j : j + 1]
            grid[rest] = value


def factor_step(work, grid, inverted, below, s):
    base = grid.shape[0]
    span = pl.ds(pl.multiple_of(s * base, base), base)
    shape = (base, base)
    eye = lax.broadcasted_iota(jnp.int32, shape, 0) == lax.broadcasted_iota(jnp.int32, shape, 1)
    grid[:, :base] = work[span, span]
    grid[:, base:] = jnp.where(eye, 1.0, 0.0)
    factor_block(grid)
    inverted[s] = grid[:, base:]
    done = dot_exact_turned(work[:, span], grid[:, base:])
    later = lax.broadcasted_iota(jnp.int32, done.shape, 0) >= (s + 1) * base
    done = jnp.where(later, done, 0.0)
    below[s] = done
    work[...] = work[...] - dot_exact_turned(done, done)


def solve_rows(rows_ref, inverted, below):
    blocks, base, _ = inverted.shape

    def step(s, carry):
        span = pl.ds(pl.multiple_of(s * base, base), base)
        done = dot_exact_turned(rows_ref[:, span], inverted[s])
        rows_ref[...] = rows_ref[...] - dot_exact_turned(done, below[s])
        rows_ref[:, span] = done
        return carry

    lax.fori_loop(0, blocks, step, 0)


def scratch_shapes(n, width, n_rows):
    f32, bf16 = jnp.float32, jnp.bfloat16
    vmem, dma = pltpu.VMEM, pltpu.SemaphoreType.DMA
    z_rows = width // RING
    return dict(
        theirs=vmem((n, width), f32),
        got=vmem((CHIPS, n, width), f32),
        high=vmem((2, n, width), bf16),
        low=vmem((2, n, width), bf16),
        prod=vmem((CHIPS, 2, width, width), f32),
        land=vmem((n_rows, 2, width, width), f32),
        slices=vmem((n_rows, 2, width // n_rows, width), f32),
        work=vmem((2 * width, 2 * width), f32),
        grid=vmem((width // 2, width), f32),
        inverted=vmem((4, width // 2, width // 2), f32),
        below=vmem((4, 2 * width, width // 2), f32),
        lead_in=vmem((2 * width, 2 * width), f32),
        first=vmem((width, 2 * width), f32),
        side=vmem((width, width), f32),
        their_factor=vmem((CHIPS, width, width), f32),
        inverse=vmem((2, width, 2 * width), f32),
        inverse_high=vmem((2, width, 2 * width), bf16),
        inverse_low=vmem((2, width, 2 * width), bf16),
        starts=vmem((CHIPS, 2, z_rows, width), f32),
        w_high=vmem((CHIPS - 1, width, 2 * width), bf16),
        w_low=vmem((CHIPS - 1, width, 2 * width), bf16),
        chain=vmem((CHIPS - 1, CHIPS - 1, 2, z_rows, width), f32),
        part=vmem((CHIPS, 2, 2, z_rows, width), f32),
        part_in=vmem((CHIPS, 2, z_rows, width), f32),
        own=vmem((CHIPS - 1, 2, z_rows, width), f32),
        cols=vmem((CHIPS - 1, 2, width, width), f32),
        total=vmem((2, n, width), f32),
        total_in=vmem((n, width), f32),
        send=dma((9,)),
        recv=dma((9,)),
        push=dma((CHIPS, 2)),
        landed=dma((n_rows, 2)),
        cut=dma((n_rows,)),
        cut_in=dma((n_rows,)),
        share=dma((n_rows, 2)),
        shared=dma((n_rows, 2)),
        local=dma((3,)),
        factor_send=dma,
        factor_recv=dma,
        part_send=dma((CHIPS,)),
        part_recv=dma((CHIPS,)),
        chain_send=dma((CHIPS, CHIPS)),
        chain_recv=dma((CHIPS, CHIPS)),
        col_send=dma((CHIPS, 5)),
        col_relay=dma((CHIPS, 2, 2)),
        col_recv=dma((CHIPS, 5, 2)),
        total_send=dma,
        total_recv=dma,
        side_send=dma,
        side_recv=dma,
        row_send=dma((CHIPS,)),
        row_recv=dma,
    )


def fused_kernel(names, mine_ref, factor_ref, inverses_ref, gram_ref, panel_ref, solved_ref, *scratch):
    v = types.SimpleNamespace(**dict(zip(names, scratch)))
    row = lax.axis_index("row")
    col = lax.axis_index("col")
    n_rows = lax.axis_size("row")
    n_cols = lax.axis_size("col")
    chip = col // 2
    core = col % 2
    x, y = chip % 4, chip // 4
    z, plane = row % RING, row // RING
    n, width = mine_ref.shape
    half = n // 2
    piece = width // n_rows
    z_rows = width // RING
    scale = 3.0 / (n * n_rows)
    sibling = (row, 2 * chip + 1 - core)

    barrier = pltpu.get_barrier_semaphore()
    for step in range(1, n_cols):
        pl.semaphore_signal(barrier, inc=1, device_id=(row, (col + step) % n_cols), device_id_type=MESH)
    for step in range(1, n_rows):
        for other in range(2):
            pl.semaphore_signal(
                barrier, inc=1, device_id=((row + step) % n_rows, 2 * chip + other), device_id_type=MESH
            )
    pl.semaphore_wait(barrier, n_cols - 1 + 2 * (n_rows - 1))

    def copy(source, target, out, arrival, device):
        return pltpu.make_async_remote_copy(
            src_ref=source, dst_ref=target, send_sem=out, recv_sem=arrival, device_id=device, device_id_type=MESH
        )

    def at(dx, dy):
        return 4 * ((y + dy) % 2) + (x + dx) % 4

    left, right, partner, far = at(3, 0), at(1, 0), at(0, 1), at(2, 0)
    top, low_half = pl.ds(0, half), pl.ds(half, half)
    at_right, at_left = (row, 2 * right + core), (row, 2 * left + core)
    at_partner = (row, 2 * partner + core)
    got = v.got
    sends = [
        copy(mine_ref, v.theirs, v.send.at[8], v.recv.at[8], sibling),
        copy(mine_ref, got.at[chip], v.send.at[0], v.recv.at[0], at_right),
        copy(mine_ref, got.at[chip], v.send.at[1], v.recv.at[1], at_left),
        copy(mine_ref, got.at[chip], v.send.at[2], v.recv.at[2], at_partner),
        copy(got.at[left, top], got.at[left, top], v.send.at[3], v.recv.at[3], at_right),
        copy(got.at[right, low_half], got.at[right, low_half], v.send.at[4], v.recv.at[4], at_left),
        copy(got.at[partner], got.at[partner], v.send.at[5], v.recv.at[5], at_right),
        copy(got.at[partner], got.at[partner], v.send.at[6], v.recv.at[6], at_left),
        copy(got.at[far], got.at[far], v.send.at[7], v.recv.at[7], at_partner),
    ]
    give_factor = copy(factor_ref.at[:, 1 - core], v.their_factor, v.factor_send, v.factor_recv, sibling)
    own_span = pl.ds(pl.multiple_of(core * width, width), width)
    fetch = [
        pltpu.make_async_copy(inverses_ref.at[chip, 0], v.inverse.at[0], v.local.at[0]),
        pltpu.make_async_copy(inverses_ref.at[chip, 1], v.inverse.at[1], v.local.at[1]),
        pltpu.make_async_copy(
            inverses_ref.at[:, :, pl.ds(pl.multiple_of(z * z_rows, z_rows), z_rows), own_span], v.starts, v.local.at[2]
        ),
    ]
    for one in sends[:4]:
        one.start()
    give_factor.start()
    for one in fetch:
        one.start()
    got[chip] = mine_ref[...]
    own_high, own_low = split(mine_ref[...])
    v.high[core] = own_high
    v.low[core] = own_low
    sends[0].wait_recv()
    their_high, their_low = split(v.theirs[...])
    v.high[1 - core] = their_high
    v.low[1 - core] = their_low

    def order(idx):
        dx = jnp.where(
            (idx == 1) | (idx == 5), 3, jnp.where((idx == 2) | (idx == 6), 1, jnp.where((idx == 4) | (idx == 7), 2, 0))
        )
        dy = jnp.where((idx == 3) | (idx > 4), 1, 0)
        return at(dx, dy)

    def away(block, to):
        return copy(
            v.prod.at[block, to],
            v.land.at[row, core],
            v.push.at[block, to],
            v.landed.at[row, core],
            (block, 2 * chip + to),
        )

    def product(idx):
        block = order(idx)
        lefts = split(got[block])
        for to in range(2):
            v.prod[block, to] = dot3_turned(lefts, (v.high[to], v.low[to]))

        @pl.when(block != row)
        def _():
            away(block, core).start()

        @pl.when(block == row)
        def _():
            v.land[row, core] = v.prod[block, core]

        away(block, 1 - core).start()

    def slice_to(other):
        return copy(
            v.prod.at[0, :, pl.ds(pl.multiple_of(other * piece, piece), piece)],
            v.slices.at[row],
            v.cut.at[other],
            v.cut_in.at[row],
            (other, core),
        )

    def lead_rows(at_row, at_core):
        return v.lead_in.at[pl.ds(pl.multiple_of(at_core * width + at_row * piece, piece), piece)]

    def share_to(step, to):
        rows = lead_rows(row, core)
        return copy(rows, rows, v.share.at[step, to], v.shared.at[row, core], ((row + step) % n_rows, to))

    def lead_slices():
        for step in range(1, n_rows):
            slice_to((row + step) % n_rows).start()
        v.slices[row] = v.prod[0, :, pl.ds(pl.multiple_of(row * piece, piece), piece)]
        for step in range(1, n_rows):
            source = (row + step) % n_rows
            copy(
                v.slices.at[row], v.slices.at[source], v.cut.at[source], v.cut_in.at[source], (source, core)
            ).wait_recv()
        total = v.slices[0]
        for other in range(1, n_rows):
            total = total + v.slices[other]
        whole = scale * jnp.concatenate([total[0], total[1]], axis=1)
        first = core * width + row * piece
        shape = (piece, 2 * width)
        there = lax.broadcasted_iota(jnp.int32, shape, 0) + first == lax.broadcasted_iota(jnp.int32, shape, 1)
        lead_rows(row, core)[...] = whole + jnp.where(there, 1.0, 0.0)
        for step in range(1, n_rows):
            for to in range(2):
                share_to(step, to).start()
        share_to(0, 1 - core).start()

    def lead_wait():
        for step in range(n_rows):
            for other in range(2):
                source = (row + step) % n_rows

                @pl.when((step > 0) | (core != other))
                def _():
                    rows = lead_rows(source, other)
                    copy(rows, rows, v.share.at[0, 0], v.shared.at[source, other], (source, 0)).wait_recv()

        v.work[...] = v.lead_in[...]

    def couple(j):
        pairs = [(v.inverse_high[side], v.inverse_low[side]) for side in (core, 1 - core)]
        value = dot3(split(factor_ref[j, core]), pairs[0]) + dot3(split(v.their_factor[j]), pairs[1])
        w_high, w_low = split(value)
        v.w_high[j] = w_high
        v.w_low[j] = w_low

    def trade(d):
        return copy(v.part.at[d, 1 - core], v.part_in.at[d], v.part_send.at[d], v.part_recv.at[d], sibling)

    def along(i, j, target):
        return copy(
            v.own.at[i], v.chain.at[i, j], v.chain_send.at[i, target], v.chain_recv.at[i, j], (row, 2 * target + core)
        )

    def z_span(at_z, start=0, size=z_rows):
        return pl.ds(pl.multiple_of(at_z * z_rows + start, size), size)

    def z_device(step, to):
        return (RING * plane + (z + step) % RING, 2 * chip + to)

    def spread(i):
        place = v.cols.at[i, core, z_span(z)]
        copies = [copy(v.own.at[i, 1 - core], place, v.col_send.at[i, 0], v.col_recv.at[i, 0, core], sibling)]
        for slot, step in ((1, 1), (2, RING - 1)):
            for to in range(2):
                copies.append(
                    copy(
                        v.own.at[i, to],
                        place,
                        v.col_send.at[i, 2 * slot - 1 + to],
                        v.col_recv.at[i, slot, core],
                        z_device(step, to),
                    )
                )
        return copies

    def onward(i, side, slot):
        step, start = ((1, 0), (RING - 1, z_rows // 2))[slot - 1]
        place = v.cols.at[i, side, z_span((z - step) % RING, start, z_rows // 2)]
        return copy(
            place, place, v.col_relay.at[i, side, slot - 1], v.col_recv.at[i, slot + 2, side], z_device(step, core)
        )

    def arrived(i, side, slot):
        rows = z_span(z) if slot < 3 else z_span(z, 0, z_rows // 2)
        place = v.cols.at[i, side, rows]
        return copy(place, place, v.col_send.at[i, 0], v.col_recv.at[i, slot, side], sibling)

    def chain_step(d):
        i = chip - d

        def term(left, j):
            left = left.reshape(2 * z_rows, width)
            return dot3(split(left), (v.w_high[j], v.w_low[j])).reshape(2, z_rows, 2 * width)

        def add(value):
            for side in range(2):
                v.part[d, side] = v.part[d, side] + value[:, :, side * width : (side + 1) * width]

        value = term(v.starts[i], i)
        for side in range(2):
            v.part[d, side] = value[:, :, side * width : (side + 1) * width]

        def more(j, carry):
            copy(v.own.at[i], v.chain.at[i, j], v.chain_send.at[i, 0], v.chain_recv.at[i, j], sibling).wait_recv()
            add(term(v.chain[i, j], j))
            return carry

        lax.fori_loop(i + 1, chip, more, 0)
        trade(d).start()
        trade(d).wait_recv()
        v.own[i] = -(v.part[d, core] + v.part_in[d])

        def tell(target, carry):
            along(i, chip, target).start()
            return carry

        lax.fori_loop(chip + 1, CHIPS, tell, 0)
        for one in spread(i):
            one.start()
        v.cols[i, core, z_span(z)] = v.own[i, core]
        pl.when(i > 0)(lambda: couple(i - 1))

    def relay(i):
        for side in range(2):
            for slot in (1, 2):
                arrived(i, side, slot).wait_recv()
                onward(i, side, slot).start()

    for one in fetch:
        one.wait()
    for side in range(2):
        high, low = split(v.inverse[side])
        v.inverse_high[side] = high
        v.inverse_low[side] = low

    def body(idx, carry):
        @pl.when(idx == 1)
        def _():
            for one in sends[1:4]:
                one.wait_recv()
            for one in sends[4:8]:
                one.start()

        @pl.when(idx == 4)
        def _():
            sends[4].wait_recv()
            sends[5].wait_recv()
            sends[8].start()

        @pl.when(idx > 4)
        def _():
            copy(mine_ref, got.at[chip], v.send.at[0], v.recv.at[idx], at_right).wait_recv()

        product(idx)

        @pl.when(idx == 0)
        def _():
            pl.when(chip == 0)(lead_slices)
            give_factor.wait_recv()
            pl.when(chip > 0)(lambda: couple(chip - 1))

        pl.when((idx < CHIPS - 1) & (chip > idx))(lambda: chain_step(idx + 1))
        pl.when((idx > 0) & (chip >= idx))(lambda: relay(chip - idx))

        @pl.when((idx >= 4) & (chip == 0))
        def _():
            pl.when(idx == 4)(lead_wait)
            factor_step(v.work, v.grid, v.inverted, v.below, idx - 4)

        return carry

    lax.fori_loop(0, CHIPS, body, 0)

    lefts = split(got[chip])
    for side in range(2):
        span = slice(side * width, (side + 1) * width)
        v.total[side] = dot3(lefts, (v.inverse_high[core, :, span], v.inverse_low[core, :, span]))

    def accumulate(step, carry):
        i = chip - 1 - step
        arrived(i, 1 - core, 0).wait_recv()
        for side in range(2):
            for slot in (3, 4):
                arrived(i, side, slot).wait_recv()
        lefts = split(got[i])
        for side in range(2):
            v.total[side] = v.total[side] + dot3(lefts, split(v.cols[i, side]))
        return carry

    lax.fori_loop(0, chip, accumulate, 0)
    give_total = copy(v.total.at[1 - core], v.total_in, v.total_send, v.total_recv, sibling)
    give_total.start()

    for other in range(2):
        for step in range(n_rows):
            source = (row + step) % n_rows

            @pl.when((step > 0) | (core != other))
            def _():
                copy(
                    v.prod.at[0, 0], v.land.at[source, other], v.push.at[0, 0], v.landed.at[source, other], sibling
                ).wait_recv()

        total = v.land[0, other]
        for source in range(1, n_rows):
            total = total + v.land[source, other]
        shape = (width, width)
        shift = (row * 2 + other - (2 * chip + core)) * width
        there = lax.broadcasted_iota(jnp.int32, shape, 0) + shift == lax.broadcasted_iota(jnp.int32, shape, 1)
        gram_ref[pl.ds(other * width, width)] = jnp.where(there, 1.0, 0.0) + scale * total

    share = panel_ref.shape[0]
    other_span = pl.ds(pl.multiple_of((1 - core) * width, width), width)
    swap = copy(gram_ref.at[other_span], v.side, v.side_send, v.side_recv, sibling)

    def hand_out(m):
        return copy(
            v.first.at[pl.ds(m * share, share)], panel_ref, v.row_send.at[m], v.row_recv, (row, CHIPS * core + m)
        )

    @pl.when(chip == 0)
    def _():
        swap.start()
        v.first[:, own_span] = gram_ref[own_span]
        swap.wait_recv()
        v.first[:, other_span] = v.side[...]
        solve_rows(v.first, v.inverted, v.below)
        for m in range(1, CHIPS):
            hand_out(m).start()
        pl.when(core == 1)(lambda: hand_out(0).start())

        @pl.when(core == 0)
        def _():
            panel_ref[...] = v.first[pl.ds(0, share)]

    give_total.wait_recv()
    solved_ref[...] = v.total[core] + v.total_in[...]
    pl.when(col > 0)(lambda: hand_out(0).wait_recv())

    @pl.when(chip == 0)
    def _():
        for step in range(1, n_rows):
            slice_to((row + step) % n_rows).wait_send()
            for to in range(2):
                share_to(step, to).wait_send()
        share_to(0, 1 - core).wait_send()
        swap.wait_send()
        for m in range(1, CHIPS):
            hand_out(m).wait_send()
        pl.when(core == 1)(lambda: hand_out(0).wait_send())

    for one in sends:
        one.wait_send()
    give_factor.wait_send()
    give_total.wait_send()

    def drain_push(block, carry):
        pl.when(block != row)(lambda: away(block, core).wait_send())
        away(block, 1 - core).wait_send()
        return carry

    lax.fori_loop(0, CHIPS, drain_push, 0)

    def drain_chain(i, carry):
        trade(chip - i).wait_send()

        def told(target, carry):
            along(i, chip, target).wait_send()
            return carry

        lax.fori_loop(chip + 1, CHIPS, told, 0)
        for one in spread(i):
            one.wait_send()
        for side in range(2):
            for slot in (1, 2):
                onward(i, side, slot).wait_send()
        return carry

    lax.fori_loop(0, chip, drain_chain, 0)


def on_device(iterate, factor, inverses):
    n, width = iterate.shape
    n_rows = lax.axis_size("row")
    n_cols = lax.axis_size("col")
    vmem = pl.BlockSpec(memory_space=pltpu.VMEM)
    scratch = scratch_shapes(n, width, n_rows)
    return pl.pallas_call(
        functools.partial(fused_kernel, tuple(scratch)),
        out_shape=(
            jax.ShapeDtypeStruct((2 * width, width), jnp.float32),
            jax.ShapeDtypeStruct((2 * width // n_cols, 2 * width), jnp.float32),
            jax.ShapeDtypeStruct((n, width), jnp.float32),
        ),
        in_specs=[vmem, vmem, pl.BlockSpec(memory_space=pl.ANY)],
        out_specs=(vmem, vmem, vmem),
        scratch_shapes=list(scratch.values()),
        compiler_params=pltpu.CompilerParams(
            collective_id=0, has_side_effects=True, vmem_limit_bytes=60 << 20
        ),
        cost_estimate=pl.CostEstimate(flops=10**10, bytes_accessed=2 * 10**7, transcendentals=0),
    )(iterate, factor.reshape(CHIPS, 2, width, width), inverses.reshape(CHIPS, 2, width, 2 * width))


def solution(mesh):
    placed = (P("row", "col"), P(None, "col"), P())
    return jax.shard_map(
        on_device,
        mesh=mesh,
        in_specs=placed,
        out_specs=(P("row", "col"), P(("row", "col"), None), P("row", "col")),
        check_vma=False,
    )
```

```python
import functools
import types

import jax
import jax.numpy as jnp
from jax import lax
from jax.experimental import pallas as pl
from jax.experimental.pallas import tpu as pltpu
from jax.sharding import PartitionSpec as P

CHIPS = 8
RING = 4
MESH = pl.DeviceIdType.MESH


def split(value):
    high = value.astype(jnp.bfloat16)
    return high, (value - high.astype(jnp.float32)).astype(jnp.bfloat16)


def dot3(left, right):
    dot = functools.partial(jnp.dot, preferred_element_type=jnp.float32)
    return dot(left[0], right[0]) + (dot(left[0], right[1]) + dot(left[1], right[0]))


def dot3_turned(left, right):
    dot = functools.partial(
        lax.dot_general, dimension_numbers=(((0,), (0,)), ((), ())), preferred_element_type=jnp.float32
    )
    return dot(left[0], right[0]) + (dot(left[0], right[1]) + dot(left[1], right[0]))


def dot_exact_turned(left, right):
    return lax.dot_general(
        left, right, (((1,), (1,)), ((), ())), precision=lax.Precision.HIGHEST, preferred_element_type=jnp.float32
    )


def factor_block(grid):
    base = grid.shape[0]
    for p in range(base // 8):
        rows = slice(8 * p, 8 * p + 8)
        panel = grid[rows]
        sub = lax.broadcasted_iota(jnp.int32, panel.shape, 0)
        columns = [jnp.broadcast_to(panel[:, 8 * p + c : 8 * p + c + 1], panel.shape) for c in range(8)]
        scales = jnp.zeros_like(panel)
        for j in range(8):
            pivot = jnp.broadcast_to(columns[j][j : j + 1], panel.shape)
            guess = lax.rsqrt(pivot)
            guess = guess * (1.5 - 0.5 * pivot * guess * guess)
            below = jnp.where(sub > j, columns[j] * (guess * guess), 0.0)
            scales = jnp.where(sub == j, guess, scales)
            for c in range(j + 1, 8):
                columns[c] = columns[c] - below * columns[c][j : j + 1]
            panel = panel - below * panel[j : j + 1]
        panel = panel * scales
        grid[rows] = panel
        if 8 * p + 8 < base:
            rest = slice(8 * p + 8, base)
            turned = panel[:, :base].T[8 * p + 8 :]
            value = grid[rest]
            for j in range(8):
                value = value - turned[:, j : j + 1] * panel[j : j + 1]
            grid[rest] = value


def factor_step(work, grid, inverted, below, s):
    base = grid.shape[0]
    span = pl.ds(pl.multiple_of(s * base, base), base)
    shape = (base, base)
    eye = lax.broadcasted_iota(jnp.int32, shape, 0) == lax.broadcasted_iota(jnp.int32, shape, 1)
    grid[:, :base] = work[span, span]
    grid[:, base:] = jnp.where(eye, 1.0, 0.0)
    factor_block(grid)
    inverted[s] = grid[:, base:]
    done = dot_exact_turned(work[:, span], grid[:, base:])
    later = lax.broadcasted_iota(jnp.int32, done.shape, 0) >= (s + 1) * base
    done = jnp.where(later, done, 0.0)
    below[s] = done
    work[...] = work[...] - dot_exact_turned(done, done)


def solve_rows(rows_ref, inverted, below):
    blocks, base, _ = inverted.shape

    def step(s, carry):
        span = pl.ds(pl.multiple_of(s * base, base), base)
        done = dot_exact_turned(rows_ref[:, span], inverted[s])
        rows_ref[...] = rows_ref[...] - dot_exact_turned(done, below[s])
        rows_ref[:, span] = done
        return carry

    lax.fori_loop(0, blocks, step, 0)


def scratch_shapes(n, width, n_rows):
    f32, bf16 = jnp.float32, jnp.bfloat16
    vmem, dma = pltpu.VMEM, pltpu.SemaphoreType.DMA
    z_rows = width // RING
    return dict(
        theirs=vmem((n, width), f32),
        got=vmem((CHIPS, n, width), f32),
        high=vmem((2, n, width), bf16),
        low=vmem((2, n, width), bf16),
        prod=vmem((CHIPS, 2, width, width), f32),
        hop=vmem((CHIPS, width, width), f32),
        land=vmem((2, 2, 2, width, width), f32),
        beside=vmem((2, width, width), f32),
        cross=vmem((2, width, width), f32),
        cross_in=vmem((2, width, width), f32),
        slices=vmem((n_rows, 2, width // n_rows, width), f32),
        work=vmem((2 * width, 2 * width), f32),
        grid=vmem((width // 2, width), f32),
        inverted=vmem((4, width // 2, width // 2), f32),
        below=vmem((4, 2 * width, width // 2), f32),
        lead_in=vmem((2 * width, 2 * width), f32),
        first=vmem((width, 2 * width), f32),
        side=vmem((width, width), f32),
        their_factor=vmem((CHIPS, width, width), f32),
        inverse=vmem((2, width, 2 * width), f32),
        inverse_high=vmem((2, width, 2 * width), bf16),
        inverse_low=vmem((2, width, 2 * width), bf16),
        starts=vmem((CHIPS, 2, z_rows, width), f32),
        w_high=vmem((CHIPS - 1, width, 2 * width), bf16),
        w_low=vmem((CHIPS - 1, width, 2 * width), bf16),
        chain=vmem((CHIPS - 1, CHIPS - 1, 2, z_rows, width), f32),
        part=vmem((CHIPS, 2, 2, z_rows, width), f32),
        part_in=vmem((CHIPS, 2, z_rows, width), f32),
        own=vmem((CHIPS - 1, 2, z_rows, width), f32),
        cols=vmem((CHIPS - 1, 2, width, width), f32),
        total=vmem((2, n, width), f32),
        total_in=vmem((n, width), f32),
        send=dma((9,)),
        recv=dma((9,)),
        push=dma((CHIPS, 2)),
        hop_send=dma((CHIPS, 2)),
        hop_recv=dma((CHIPS,)),
        landed=dma((2, 2, 2)),
        beside_recv=dma((2,)),
        cross_send=dma((2,)),
        cross_recv=dma((2,)),
        cut=dma((n_rows,)),
        cut_in=dma((n_rows,)),
        share=dma((n_rows, 2)),
        shared=dma((n_rows, 2)),
        local=dma((3,)),
        factor_send=dma,
        factor_recv=dma,
        part_send=dma((CHIPS,)),
        part_recv=dma((CHIPS,)),
        chain_send=dma((CHIPS, CHIPS)),
        chain_recv=dma((CHIPS, CHIPS)),
        col_send=dma((CHIPS, 5)),
        col_relay=dma((CHIPS, 2, 2)),
        col_recv=dma((CHIPS, 5, 2)),
        total_send=dma,
        total_recv=dma,
        side_send=dma,
        side_recv=dma,
        row_send=dma((CHIPS,)),
        row_recv=dma,
    )


def fused_kernel(names, mine_ref, factor_ref, inverses_ref, gram_ref, panel_ref, solved_ref, *scratch):
    v = types.SimpleNamespace(**dict(zip(names, scratch)))
    row = lax.axis_index("row")
    col = lax.axis_index("col")
    n_rows = lax.axis_size("row")
    n_cols = lax.axis_size("col")
    chip = col // 2
    core = col % 2
    x, y = chip % 4, chip // 4
    z, plane = row % RING, row // RING
    n, width = mine_ref.shape
    half = n // 2
    piece = width // n_rows
    z_rows = width // RING
    scale = 3.0 / (n * n_rows)
    sibling = (row, 2 * chip + 1 - core)

    barrier = pltpu.get_barrier_semaphore()
    for step in range(1, n_cols):
        pl.semaphore_signal(barrier, inc=1, device_id=(row, (col + step) % n_cols), device_id_type=MESH)
    for step in range(1, n_rows):
        for other in range(2):
            pl.semaphore_signal(
                barrier, inc=1, device_id=((row + step) % n_rows, 2 * chip + other), device_id_type=MESH
            )
    pl.semaphore_wait(barrier, n_cols - 1 + 2 * (n_rows - 1))

    def copy(source, target, out, arrival, device):
        return pltpu.make_async_remote_copy(
            src_ref=source, dst_ref=target, send_sem=out, recv_sem=arrival, device_id=device, device_id_type=MESH
        )

    def at(dx, dy):
        return 4 * ((y + dy) % 2) + (x + dx) % 4

    left, right, partner, far = at(3, 0), at(1, 0), at(0, 1), at(2, 0)
    top, low_half = pl.ds(0, half), pl.ds(half, half)
    at_right, at_left = (row, 2 * right + core), (row, 2 * left + core)
    at_partner = (row, 2 * partner + core)
    got = v.got
    sends = [
        copy(mine_ref, v.theirs, v.send.at[8], v.recv.at[8], sibling),
        copy(mine_ref, got.at[chip], v.send.at[0], v.recv.at[0], at_right),
        copy(mine_ref, got.at[chip], v.send.at[1], v.recv.at[1], at_left),
        copy(mine_ref, got.at[chip], v.send.at[2], v.recv.at[2], at_partner),
        copy(got.at[left, top], got.at[left, top], v.send.at[3], v.recv.at[3], at_right),
        copy(got.at[right, low_half], got.at[right, low_half], v.send.at[4], v.recv.at[4], at_left),
        copy(got.at[partner], got.at[partner], v.send.at[5], v.recv.at[5], at_right),
        copy(got.at[partner], got.at[partner], v.send.at[6], v.recv.at[6], at_left),
        copy(got.at[far], got.at[far], v.send.at[7], v.recv.at[7], at_partner),
    ]
    give_factor = copy(factor_ref.at[:, 1 - core], v.their_factor, v.factor_send, v.factor_recv, sibling)
    own_span = pl.ds(pl.multiple_of(core * width, width), width)
    fetch = [
        pltpu.make_async_copy(inverses_ref.at[chip, 0], v.inverse.at[0], v.local.at[0]),
        pltpu.make_async_copy(inverses_ref.at[chip, 1], v.inverse.at[1], v.local.at[1]),
        pltpu.make_async_copy(
            inverses_ref.at[:, :, pl.ds(pl.multiple_of(z * z_rows, z_rows), z_rows), own_span], v.starts, v.local.at[2]
        ),
    ]
    for one in sends[:4]:
        one.start()
    give_factor.start()
    for one in fetch:
        one.start()
    got[chip] = mine_ref[...]
    own_high, own_low = split(mine_ref[...])
    v.high[core] = own_high
    v.low[core] = own_low
    sends[0].wait_recv()
    their_high, their_low = split(v.theirs[...])
    v.high[1 - core] = their_high
    v.low[1 - core] = their_low

    def order(idx):
        dx = jnp.where(
            (idx == 1) | (idx == 5), 3, jnp.where((idx == 2) | (idx == 6), 1, jnp.where((idx == 4) | (idx == 7), 2, 0))
        )
        dy = jnp.where((idx == 3) | (idx > 4), 1, 0)
        return at(dx, dy)

    def ahead(block):
        return (block % RING - z + RING) % RING

    def z_peer(step, to):
        return (RING * plane + (z + step) % RING, 2 * chip + to)

    def hop_to(block, side):
        step = (1, RING - 1)[side]
        return copy(
            v.prod.at[block, side], v.hop.at[block], v.hop_send.at[block, side], v.hop_recv.at[block], z_peer(step, core)
        )

    def away(block, side, to):
        step = (1, RING - 1)[side]
        return copy(
            v.prod.at[block, to],
            v.land.at[side, block // RING, core],
            v.push.at[block, to],
            v.landed.at[side, block // RING, core],
            z_peer(step, to),
        )

    def hand_beside(block):
        return copy(
            v.prod.at[block, 1 - core],
            v.beside.at[block // RING],
            v.push.at[block, 1 - core],
            v.beside_recv.at[block // RING],
            sibling,
        )

    def product(idx):
        block = order(idx)
        lefts = split(got[block])
        for to in range(2):
            v.prod[block, to] = dot3_turned(lefts, (v.high[to], v.low[to]))
        pl.when(ahead(block) == 0)(lambda: hand_beside(block).start())
        pl.when(ahead(block) == 1)(lambda: away(block, 0, 1).start())
        pl.when(ahead(block) == RING - 1)(lambda: away(block, 1, 0).start())

        @pl.when(ahead(block) == 2)
        def _():
            hop_to(block, 0).start()
            hop_to(block, 1).start()

    def add_and_pass(idx):
        block = order(idx)
        for side in range(2):

            @pl.when(ahead(block) == (1, RING - 1)[side])
            def _():
                hop_to(block, side).wait_recv()
                v.prod[block, side] = v.prod[block, side] + v.hop[block]
                away(block, side, side).start()

    def plane_sum(to_plane, part):
        total = v.land[0, to_plane, part] + v.land[1, to_plane, part]
        mine = jnp.where(core == part, 1, 0)
        return total + jnp.where(mine == 1, v.prod[RING * to_plane + z, core], v.beside[to_plane])

    def cross_to(part):
        return copy(
            v.cross.at[part],
            v.cross_in.at[part],
            v.cross_send.at[part],
            v.cross_recv.at[part],
            (RING * (1 - plane) + z, col),
        )

    def arrivals(to_plane):
        copy(v.cross.at[0], v.beside.at[0], v.push.at[0, 0], v.beside_recv.at[to_plane], sibling).wait_recv()
        for part in range(2):
            for side in range(2):
                copy(
                    v.cross.at[0], v.cross_in.at[0], v.push.at[0, 0], v.landed.at[side, to_plane, part], sibling
                ).wait_recv()

    def cross():
        arrivals(1 - plane)
        for part in range(2):
            v.cross[part] = plane_sum(1 - plane, part)
            cross_to(part).start()

    def slice_to(other):
        return copy(
            v.prod.at[0, :, pl.ds(pl.multiple_of(other * piece, piece), piece)],
            v.slices.at[row],
            v.cut.at[other],
            v.cut_in.at[row],
            (other, core),
        )

    def lead_rows(at_row, at_core):
        return v.lead_in.at[pl.ds(pl.multiple_of(at_core * width + at_row * piece, piece), piece)]

    def share_to(step, to):
        rows = lead_rows(row, core)
        return copy(rows, rows, v.share.at[step, to], v.shared.at[row, core], ((row + step) % n_rows, to))

    def lead_slices():
        for step in range(1, n_rows):
            slice_to((row + step) % n_rows).start()
        v.slices[row] = v.prod[0, :, pl.ds(pl.multiple_of(row * piece, piece), piece)]
        for step in range(1, n_rows):
            source = (row + step) % n_rows
            copy(
                v.slices.at[row], v.slices.at[source], v.cut.at[source], v.cut_in.at[source], (source, core)
            ).wait_recv()
            slice_to(source).wait_send()
        total = v.slices[0]
        for other in range(1, n_rows):
            total = total + v.slices[other]
        whole = scale * jnp.concatenate([total[0], total[1]], axis=1)
        first = core * width + row * piece
        shape = (piece, 2 * width)
        there = lax.broadcasted_iota(jnp.int32, shape, 0) + first == lax.broadcasted_iota(jnp.int32, shape, 1)
        lead_rows(row, core)[...] = whole + jnp.where(there, 1.0, 0.0)
        for step in range(1, n_rows):
            for to in range(2):
                share_to(step, to).start()
        share_to(0, 1 - core).start()

    def lead_wait():
        for step in range(n_rows):
            for other in range(2):
                source = (row + step) % n_rows

                @pl.when((step > 0) | (core != other))
                def _():
                    rows = lead_rows(source, other)
                    copy(rows, rows, v.share.at[0, 0], v.shared.at[source, other], (source, 0)).wait_recv()

        v.work[...] = v.lead_in[...]

    def couple(j):
        pairs = [(v.inverse_high[side], v.inverse_low[side]) for side in (core, 1 - core)]
        value = dot3(split(factor_ref[j, core]), pairs[0]) + dot3(split(v.their_factor[j]), pairs[1])
        w_high, w_low = split(value)
        v.w_high[j] = w_high
        v.w_low[j] = w_low

    def trade(d):
        return copy(v.part.at[d, 1 - core], v.part_in.at[d], v.part_send.at[d], v.part_recv.at[d], sibling)

    def along(i, j, target):
        return copy(
            v.own.at[i], v.chain.at[i, j], v.chain_send.at[i, target], v.chain_recv.at[i, j], (row, 2 * target + core)
        )

    def z_span(at_z, start=0, size=z_rows):
        return pl.ds(pl.multiple_of(at_z * z_rows + start, size), size)

    def z_device(step, to):
        return (RING * plane + (z + step) % RING, 2 * chip + to)

    def spread(i):
        place = v.cols.at[i, core, z_span(z)]
        copies = [copy(v.own.at[i, 1 - core], place, v.col_send.at[i, 0], v.col_recv.at[i, 0, core], sibling)]
        for slot, step in ((1, 1), (2, RING - 1)):
            for to in range(2):
                copies.append(
                    copy(
                        v.own.at[i, to],
                        place,
                        v.col_send.at[i, 2 * slot - 1 + to],
                        v.col_recv.at[i, slot, core],
                        z_device(step, to),
                    )
                )
        return copies

    def onward(i, side, slot):
        step, start = ((1, 0), (RING - 1, z_rows // 2))[slot - 1]
        place = v.cols.at[i, side, z_span((z - step) % RING, start, z_rows // 2)]
        return copy(
            place, place, v.col_relay.at[i, side, slot - 1], v.col_recv.at[i, slot + 2, side], z_device(step, core)
        )

    def arrived(i, side, slot):
        rows = z_span(z) if slot < 3 else z_span(z, 0, z_rows // 2)
        place = v.cols.at[i, side, rows]
        return copy(place, place, v.col_send.at[i, 0], v.col_recv.at[i, slot, side], sibling)

    def chain_step(d):
        i = chip - d

        def term(left, j):
            left = left.reshape(2 * z_rows, width)
            return dot3(split(left), (v.w_high[j], v.w_low[j])).reshape(2, z_rows, 2 * width)

        def add(value):
            for side in range(2):
                v.part[d, side] = v.part[d, side] + value[:, :, side * width : (side + 1) * width]

        value = term(v.starts[i], i)
        for side in range(2):
            v.part[d, side] = value[:, :, side * width : (side + 1) * width]

        def more(j, carry):
            copy(v.own.at[i], v.chain.at[i, j], v.chain_send.at[i, 0], v.chain_recv.at[i, j], sibling).wait_recv()
            add(term(v.chain[i, j], j))
            return carry

        lax.fori_loop(i + 1, chip, more, 0)
        trade(d).start()
        trade(d).wait_recv()
        v.own[i] = -(v.part[d, core] + v.part_in[d])

        def tell(target, carry):
            along(i, chip, target).start()
            return carry

        lax.fori_loop(chip + 1, CHIPS, tell, 0)
        for one in spread(i):
            one.start()
        v.cols[i, core, z_span(z)] = v.own[i, core]
        pl.when(i > 0)(lambda: couple(i - 1))

    def relay(i):
        for side in range(2):
            for slot in (1, 2):
                arrived(i, side, slot).wait_recv()
                onward(i, side, slot).start()

    for one in fetch:
        one.wait()
    for side in range(2):
        high, low = split(v.inverse[side])
        v.inverse_high[side] = high
        v.inverse_low[side] = low

    def body(idx, carry):
        @pl.when(idx == 1)
        def _():
            for one in sends[1:4]:
                one.wait_recv()
            for one in sends[4:8]:
                one.start()

        @pl.when(idx == 4)
        def _():
            sends[4].wait_recv()
            sends[5].wait_recv()
            sends[8].start()

        @pl.when(idx > 4)
        def _():
            copy(mine_ref, got.at[chip], v.send.at[0], v.recv.at[idx], at_right).wait_recv()

        product(idx)
        pl.when(idx > 0)(lambda: add_and_pass(idx - 1))

        @pl.when(idx == 0)
        def _():
            pl.when(chip == 0)(lead_slices)
            give_factor.wait_recv()
            pl.when(chip > 0)(lambda: couple(chip - 1))

        pl.when((idx < CHIPS - 1) & (chip > idx))(lambda: chain_step(idx + 1))
        pl.when((idx > 0) & (chip >= idx))(lambda: relay(chip - idx))

        @pl.when((idx >= 4) & (chip == 0))
        def _():
            pl.when(idx == 4)(lead_wait)
            factor_step(v.work, v.grid, v.inverted, v.below, idx - 4)

        return carry

    lax.fori_loop(0, CHIPS, body, 0)
    add_and_pass(CHIPS - 1)

    lefts = split(got[chip])
    for side in range(2):
        span = slice(side * width, (side + 1) * width)
        v.total[side] = dot3(lefts, (v.inverse_high[core, :, span], v.inverse_low[core, :, span]))

    def accumulate(step, carry):
        i = chip - 1 - step
        arrived(i, 1 - core, 0).wait_recv()
        for side in range(2):
            for slot in (3, 4):
                arrived(i, side, slot).wait_recv()
        lefts = split(got[i])
        for side in range(2):
            v.total[side] = v.total[side] + dot3(lefts, split(v.cols[i, side]))
        return carry

    lax.fori_loop(0, chip, accumulate, 0)
    give_total = copy(v.total.at[1 - core], v.total_in, v.total_send, v.total_recv, sibling)
    give_total.start()

    cross()
    arrivals(plane)
    for part in range(2):
        cross_to(part).wait_recv()
        total = plane_sum(plane, part) + v.cross_in[part]
        shape = (width, width)
        shift = (row * 2 + part - (2 * chip + core)) * width
        there = lax.broadcasted_iota(jnp.int32, shape, 0) + shift == lax.broadcasted_iota(jnp.int32, shape, 1)
        gram_ref[pl.ds(part * width, width)] = jnp.where(there, 1.0, 0.0) + scale * total

    share = panel_ref.shape[0]
    other_span = pl.ds(pl.multiple_of((1 - core) * width, width), width)
    swap = copy(gram_ref.at[other_span], v.side, v.side_send, v.side_recv, sibling)

    def hand_out(m):
        return copy(
            v.first.at[pl.ds(m * share, share)], panel_ref, v.row_send.at[m], v.row_recv, (row, CHIPS * core + m)
        )

    @pl.when(chip == 0)
    def _():
        swap.start()
        v.first[:, own_span] = gram_ref[own_span]
        swap.wait_recv()
        v.first[:, other_span] = v.side[...]
        solve_rows(v.first, v.inverted, v.below)
        for m in range(1, CHIPS):
            hand_out(m).start()
        pl.when(core == 1)(lambda: hand_out(0).start())

        @pl.when(core == 0)
        def _():
            panel_ref[...] = v.first[pl.ds(0, share)]

    give_total.wait_recv()
    solved_ref[...] = v.total[core] + v.total_in[...]
    pl.when(col > 0)(lambda: hand_out(0).wait_recv())

    @pl.when(chip == 0)
    def _():
        for step in range(1, n_rows):
            for to in range(2):
                share_to(step, to).wait_send()
        share_to(0, 1 - core).wait_send()
        swap.wait_send()
        for m in range(1, CHIPS):
            hand_out(m).wait_send()
        pl.when(core == 1)(lambda: hand_out(0).wait_send())

    for one in sends:
        one.wait_send()
    give_factor.wait_send()
    give_total.wait_send()

    def drain_push(block, carry):
        pl.when(ahead(block) == 0)(lambda: hand_beside(block).wait_send())
        for side in range(2):
            pl.when(ahead(block) == 2)(lambda: hop_to(block, side).wait_send())
            for to in range(2):
                pl.when(ahead(block) == (1, RING - 1)[side])(lambda: away(block, side, to).wait_send())
        return carry

    for part in range(2):
        cross_to(part).wait_send()
    lax.fori_loop(0, CHIPS, drain_push, 0)

    def drain_chain(i, carry):
        trade(chip - i).wait_send()

        def told(target, carry):
            along(i, chip, target).wait_send()
            return carry

        lax.fori_loop(chip + 1, CHIPS, told, 0)
        for one in spread(i):
            one.wait_send()
        for side in range(2):
            for slot in (1, 2):
                onward(i, side, slot).wait_send()
        return carry

    lax.fori_loop(0, chip, drain_chain, 0)


def on_device(iterate, factor, inverses):
    n, width = iterate.shape
    n_rows = lax.axis_size("row")
    n_cols = lax.axis_size("col")
    vmem = pl.BlockSpec(memory_space=pltpu.VMEM)
    scratch = scratch_shapes(n, width, n_rows)
    return pl.pallas_call(
        functools.partial(fused_kernel, tuple(scratch)),
        out_shape=(
            jax.ShapeDtypeStruct((2 * width, width), jnp.float32),
            jax.ShapeDtypeStruct((2 * width // n_cols, 2 * width), jnp.float32),
            jax.ShapeDtypeStruct((n, width), jnp.float32),
        ),
        in_specs=[vmem, vmem, pl.BlockSpec(memory_space=pl.ANY)],
        out_specs=(vmem, vmem, vmem),
        scratch_shapes=list(scratch.values()),
        compiler_params=pltpu.CompilerParams(
            collective_id=0, has_side_effects=True, vmem_limit_bytes=60 << 20
        ),
        cost_estimate=pl.CostEstimate(flops=10**10, bytes_accessed=2 * 10**7, transcendentals=0),
    )(iterate, factor.reshape(CHIPS, 2, width, width), inverses.reshape(CHIPS, 2, width, 2 * width))


def solution(mesh):
    placed = (P("row", "col"), P(None, "col"), P())
    return jax.shard_map(
        on_device,
        mesh=mesh,
        in_specs=placed,
        out_specs=(P("row", "col"), P(("row", "col"), None), P("row", "col")),
        check_vma=False,
    )
```

```python
import functools
import types

import jax
import jax.numpy as jnp
from jax import lax
from jax.experimental import pallas as pl
from jax.experimental.pallas import tpu as pltpu
from jax.sharding import PartitionSpec as P

CHIPS = 8
RING = 4
MESH = pl.DeviceIdType.MESH


def split(value):
    high = value.astype(jnp.bfloat16)
    return high, (value - high.astype(jnp.float32)).astype(jnp.bfloat16)


def dot3(left, right):
    dot = functools.partial(jnp.dot, preferred_element_type=jnp.float32)
    return dot(left[0], right[0]) + (dot(left[0], right[1]) + dot(left[1], right[0]))


def dot3_turned(left, right):
    dot = functools.partial(
        lax.dot_general, dimension_numbers=(((0,), (0,)), ((), ())), preferred_element_type=jnp.float32
    )
    return dot(left[0], right[0]) + (dot(left[0], right[1]) + dot(left[1], right[0]))


def dot_exact_turned(left, right):
    return lax.dot_general(
        left, right, (((1,), (1,)), ((), ())), precision=lax.Precision.HIGHEST, preferred_element_type=jnp.float32
    )


def factor_block(grid, first, last):
    base = grid.shape[0]
    for p in range(first, last):
        rows = slice(8 * p, 8 * p + 8)
        panel = grid[rows]
        sub = lax.broadcasted_iota(jnp.int32, panel.shape, 0)
        columns = [jnp.broadcast_to(panel[:, 8 * p + c : 8 * p + c + 1], panel.shape) for c in range(8)]
        scales = jnp.zeros_like(panel)
        for j in range(8):
            pivot = jnp.broadcast_to(columns[j][j : j + 1], panel.shape)
            guess = lax.rsqrt(pivot)
            guess = guess * (1.5 - 0.5 * pivot * guess * guess)
            below = jnp.where(sub > j, columns[j] * (guess * guess), 0.0)
            scales = jnp.where(sub == j, guess, scales)
            for c in range(j + 1, 8):
                columns[c] = columns[c] - below * columns[c][j : j + 1]
            panel = panel - below * panel[j : j + 1]
        panel = panel * scales
        grid[rows] = panel
        if 8 * p + 8 < base:
            rest = slice(8 * p + 8, base)
            turned = panel[:, :base].T[8 * p + 8 :]
            value = grid[rest]
            for j in range(8):
                value = value - turned[:, j : j + 1] * panel[j : j + 1]
            grid[rest] = value


def factor_part(work, grid, inverted, below, s, part):
    base = grid.shape[0]
    span = pl.ds(pl.multiple_of(s * base, base), base)
    panels = base // 8

    @pl.when(part == 0)
    def _():
        shape = (base, base)
        eye = lax.broadcasted_iota(jnp.int32, shape, 0) == lax.broadcasted_iota(jnp.int32, shape, 1)
        grid[:, :base] = work[span, span]
        grid[:, base:] = jnp.where(eye, 1.0, 0.0)
        factor_block(grid, 0, panels * 2 // 5)

    pl.when(part == 1)(lambda: factor_block(grid, panels * 2 // 5, panels))

    @pl.when(part == 2)
    def _():
        inverted[s] = grid[:, base:]
        done = dot_exact_turned(work[:, span], grid[:, base:])
        later = lax.broadcasted_iota(jnp.int32, done.shape, 0) >= (s + 1) * base
        done = jnp.where(later, done, 0.0)
        below[s] = done
        work[...] = work[...] - dot_exact_turned(done, done)


def solve_rows(rows_ref, inverted, below):
    blocks, base, _ = inverted.shape

    def step(s, carry):
        span = pl.ds(pl.multiple_of(s * base, base), base)
        done = dot_exact_turned(rows_ref[:, span], inverted[s])
        rows_ref[...] = rows_ref[...] - dot_exact_turned(done, below[s])
        rows_ref[:, span] = done
        return carry

    lax.fori_loop(0, blocks, step, 0)


def scratch_shapes(n, width, n_rows):
    f32, bf16 = jnp.float32, jnp.bfloat16
    vmem, dma = pltpu.VMEM, pltpu.SemaphoreType.DMA
    z_rows = width // RING
    return dict(
        theirs=vmem((n, width), f32),
        got=vmem((CHIPS, n, width), f32),
        high=vmem((2, n, width), bf16),
        low=vmem((2, n, width), bf16),
        prod=vmem((CHIPS, 2, width, width), f32),
        hop=vmem((CHIPS, width, width), f32),
        land=vmem((2, 2, 2, width, width), f32),
        beside=vmem((2, width, width), f32),
        cross=vmem((2, width, width), f32),
        cross_in=vmem((2, width, width), f32),
        slices=vmem((n_rows, 2, width // n_rows, width), f32),
        work=vmem((2 * width, 2 * width), f32),
        grid=vmem((width // 2, width), f32),
        inverted=vmem((4, width // 2, width // 2), f32),
        below=vmem((4, 2 * width, width // 2), f32),
        lead_in=vmem((2 * width, 2 * width), f32),
        first=vmem((width, 2 * width), f32),
        side=vmem((width, width), f32),
        their_factor=vmem((CHIPS, width, width), f32),
        inverse=vmem((2, width, 2 * width), f32),
        inverse_high=vmem((2, width, 2 * width), bf16),
        inverse_low=vmem((2, width, 2 * width), bf16),
        starts=vmem((CHIPS, 2, z_rows, width), f32),
        w_high=vmem((CHIPS - 1, width, 2 * width), bf16),
        w_low=vmem((CHIPS - 1, width, 2 * width), bf16),
        chain=vmem((CHIPS - 1, CHIPS - 1, 2, z_rows, width), f32),
        part=vmem((CHIPS, 2, 2, z_rows, width), f32),
        part_in=vmem((CHIPS, 2, z_rows, width), f32),
        own=vmem((CHIPS - 1, 2, z_rows, width), f32),
        cols=vmem((CHIPS - 1, 2, width, width), f32),
        total=vmem((2, n, width), f32),
        total_in=vmem((n, width), f32),
        send=dma((13,)),
        recv=dma((13,)),
        theirs_send=dma,
        theirs_recv=dma,
        push=dma((CHIPS, 2)),
        hop_send=dma((CHIPS, 2)),
        hop_recv=dma((CHIPS,)),
        landed=dma((2, 2, 2)),
        beside_recv=dma((2,)),
        cross_send=dma((2,)),
        cross_recv=dma((2,)),
        cut=dma((n_rows,)),
        cut_in=dma((n_rows,)),
        share=dma((n_rows, 2)),
        shared=dma((n_rows, 2)),
        local=dma((3,)),
        factor_send=dma,
        factor_recv=dma,
        part_send=dma((CHIPS,)),
        part_recv=dma((CHIPS,)),
        chain_send=dma((CHIPS, CHIPS)),
        chain_recv=dma((CHIPS, CHIPS)),
        col_send=dma((CHIPS, 5)),
        col_relay=dma((CHIPS, 2, 2)),
        col_recv=dma((CHIPS, 5, 2)),
        total_send=dma,
        total_recv=dma,
        side_send=dma,
        side_recv=dma,
        row_send=dma((CHIPS,)),
        row_recv=dma,
    )


def fused_kernel(names, mine_ref, factor_ref, inverses_ref, gram_ref, panel_ref, solved_ref, *scratch):
    v = types.SimpleNamespace(**dict(zip(names, scratch)))
    row = lax.axis_index("row")
    col = lax.axis_index("col")
    n_rows = lax.axis_size("row")
    n_cols = lax.axis_size("col")
    chip = col // 2
    core = col % 2
    x, y = chip % 4, chip // 4
    z, plane = row % RING, row // RING
    n, width = mine_ref.shape
    piece = width // n_rows
    z_rows = width // RING
    scale = 3.0 / (n * n_rows)
    sibling = (row, 2 * chip + 1 - core)

    barrier = pltpu.get_barrier_semaphore()
    for step in range(1, n_cols):
        pl.semaphore_signal(barrier, inc=1, device_id=(row, (col + step) % n_cols), device_id_type=MESH)
    for step in range(1, n_rows):
        for other in range(2):
            pl.semaphore_signal(
                barrier, inc=1, device_id=((row + step) % n_rows, 2 * chip + other), device_id_type=MESH
            )
    pl.semaphore_wait(barrier, n_cols - 1 + 2 * (n_rows - 1))

    def copy(source, target, out, arrival, device):
        return pltpu.make_async_remote_copy(
            src_ref=source, dst_ref=target, send_sem=out, recv_sem=arrival, device_id=device, device_id_type=MESH
        )

    def at(dx, dy):
        return 4 * ((y + dy) % 2) + (x + dx) % 4

    left, right, partner, far = at(3, 0), at(1, 0), at(0, 1), at(2, 0)
    at_right, at_left = (row, 2 * right + core), (row, 2 * left + core)
    at_partner = (row, 2 * partner + core)
    got = v.got
    top, low_half = pl.ds(0, n // 2), pl.ds(n // 2, n // 2)

    def block_copy(block, span, k, device, source=None):
        place = got.at[block] if span is None else got.at[block, span]
        return copy(place if source is None else source, place, v.send.at[k], v.recv.at[k], device)

    own_sends = [
        block_copy(chip, None, 0, at_right, mine_ref),
        block_copy(chip, None, 1, at_left, mine_ref),
        block_copy(chip, None, 2, at_partner, mine_ref),
    ]
    half_sends = [block_copy(left, top, 3, at_right), block_copy(right, low_half, 4, at_left)]
    thirds = [pl.ds(0, n * 3 // 8), pl.ds(n * 3 // 8, n * 3 // 8), pl.ds(n * 3 // 4, n // 4)]
    partner_sends = [
        [block_copy(partner, span, 5 + k, at_right), block_copy(partner, span, 8 + k, at_left)]
        for k, span in enumerate(thirds)
    ]
    far_sends = [block_copy(far, top, 11, at_partner), block_copy(far, low_half, 12, at_partner)]

    give_mine = copy(mine_ref, v.theirs, v.theirs_send, v.theirs_recv, sibling)
    give_factor = copy(factor_ref.at[:, 1 - core], v.their_factor, v.factor_send, v.factor_recv, sibling)
    own_span = pl.ds(pl.multiple_of(core * width, width), width)
    fetch = [
        pltpu.make_async_copy(inverses_ref.at[chip, 0], v.inverse.at[0], v.local.at[0]),
        pltpu.make_async_copy(inverses_ref.at[chip, 1], v.inverse.at[1], v.local.at[1]),
        pltpu.make_async_copy(
            inverses_ref.at[:, :, pl.ds(pl.multiple_of(z * z_rows, z_rows), z_rows), own_span], v.starts, v.local.at[2]
        ),
    ]
    give_mine.start()
    own_sends[0].start()
    own_sends[1].start()
    own_sends[2].start()
    give_factor.start()
    for one in fetch:
        one.start()
    got[chip] = mine_ref[...]
    own_high, own_low = split(mine_ref[...])
    v.high[core] = own_high
    v.low[core] = own_low
    give_mine.wait_recv()
    their_high, their_low = split(v.theirs[...])
    v.high[1 - core] = their_high
    v.low[1 - core] = their_low

    def order(idx):
        dx = jnp.where(
            (idx == 1) | (idx == 5), 3, jnp.where((idx == 2) | (idx == 6), 1, jnp.where((idx == 4) | (idx == 7), 2, 0))
        )
        dy = jnp.where((idx == 3) | (idx > 4), 1, 0)
        return at(dx, dy)

    def ahead(block):
        return (block % RING - z + RING) % RING

    def z_peer(step, to):
        return (RING * plane + (z + step) % RING, 2 * chip + to)

    def hop_to(block, side):
        step = (1, RING - 1)[side]
        return copy(
            v.prod.at[block, side], v.hop.at[block], v.hop_send.at[block, side], v.hop_recv.at[block], z_peer(step, core)
        )

    def away(block, side, to):
        step = (1, RING - 1)[side]
        return copy(
            v.prod.at[block, to],
            v.land.at[side, block // RING, core],
            v.push.at[block, to],
            v.landed.at[side, block // RING, core],
            z_peer(step, to),
        )

    def hand_beside(block):
        return copy(
            v.prod.at[block, 1 - core],
            v.beside.at[block // RING],
            v.push.at[block, 1 - core],
            v.beside_recv.at[block // RING],
            sibling,
        )

    def product(idx):
        block = order(idx)
        lefts = split(got[block])
        for to in range(2):
            v.prod[block, to] = dot3_turned(lefts, (v.high[to], v.low[to]))
        pl.when(ahead(block) == 0)(lambda: hand_beside(block).start())
        pl.when(ahead(block) == 1)(lambda: away(block, 0, 1).start())
        pl.when(ahead(block) == RING - 1)(lambda: away(block, 1, 0).start())

        @pl.when(ahead(block) == 2)
        def _():
            hop_to(block, 0).start()
            hop_to(block, 1).start()

    def add_and_pass(idx):
        block = order(idx)
        for side in range(2):

            @pl.when(ahead(block) == (1, RING - 1)[side])
            def _():
                hop_to(block, side).wait_recv()
                v.prod[block, side] = v.prod[block, side] + v.hop[block]
                away(block, side, side).start()

    def plane_sum(to_plane, part):
        total = v.land[0, to_plane, part] + v.land[1, to_plane, part]
        mine = jnp.where(core == part, 1, 0)
        return total + jnp.where(mine == 1, v.prod[RING * to_plane + z, core], v.beside[to_plane])

    def cross_to(part):
        return copy(
            v.cross.at[part],
            v.cross_in.at[part],
            v.cross_send.at[part],
            v.cross_recv.at[part],
            (RING * (1 - plane) + z, col),
        )

    def arrivals(to_plane):
        copy(v.cross.at[0], v.beside.at[0], v.push.at[0, 0], v.beside_recv.at[to_plane], sibling).wait_recv()
        for part in range(2):
            for side in range(2):
                copy(
                    v.cross.at[0], v.cross_in.at[0], v.push.at[0, 0], v.landed.at[side, to_plane, part], sibling
                ).wait_recv()

    def cross():
        arrivals(1 - plane)
        for part in range(2):
            v.cross[part] = plane_sum(1 - plane, part)
            cross_to(part).start()

    def slice_to(other):
        return copy(
            v.prod.at[0, :, pl.ds(pl.multiple_of(other * piece, piece), piece)],
            v.slices.at[row],
            v.cut.at[other],
            v.cut_in.at[row],
            (other, core),
        )

    def lead_rows(at_row, at_core):
        return v.lead_in.at[pl.ds(pl.multiple_of(at_core * width + at_row * piece, piece), piece)]

    def share_to(step, to):
        rows = lead_rows(row, core)
        return copy(rows, rows, v.share.at[step, to], v.shared.at[row, core], ((row + step) % n_rows, to))

    def lead_push():
        for step in range(1, n_rows):
            slice_to((row + step) % n_rows).start()
        v.slices[row] = v.prod[0, :, pl.ds(pl.multiple_of(row * piece, piece), piece)]

    def lead_sum():
        for step in range(1, n_rows):
            source = (row + step) % n_rows
            copy(
                v.slices.at[row], v.slices.at[source], v.cut.at[source], v.cut_in.at[source], (source, core)
            ).wait_recv()
            slice_to(source).wait_send()
        total = v.slices[0]
        for other in range(1, n_rows):
            total = total + v.slices[other]
        whole = scale * jnp.concatenate([total[0], total[1]], axis=1)
        first = core * width + row * piece
        shape = (piece, 2 * width)
        there = lax.broadcasted_iota(jnp.int32, shape, 0) + first == lax.broadcasted_iota(jnp.int32, shape, 1)
        lead_rows(row, core)[...] = whole + jnp.where(there, 1.0, 0.0)
        for step in range(1, n_rows):
            for to in range(2):
                share_to(step, to).start()
        share_to(0, 1 - core).start()

    def lead_wait():
        for step in range(n_rows):
            for other in range(2):
                source = (row + step) % n_rows

                @pl.when((step > 0) | (core != other))
                def _():
                    rows = lead_rows(source, other)
                    copy(rows, rows, v.share.at[0, 0], v.shared.at[source, other], (source, 0)).wait_recv()

        v.work[...] = v.lead_in[...]

    def couple(j):
        pairs = [(v.inverse_high[side], v.inverse_low[side]) for side in (core, 1 - core)]
        value = dot3(split(factor_ref[j, core]), pairs[0]) + dot3(split(v.their_factor[j]), pairs[1])
        w_high, w_low = split(value)
        v.w_high[j] = w_high
        v.w_low[j] = w_low

    def trade(d):
        return copy(v.part.at[d, 1 - core], v.part_in.at[d], v.part_send.at[d], v.part_recv.at[d], sibling)

    def along(i, j, target):
        return copy(
            v.own.at[i], v.chain.at[i, j], v.chain_send.at[i, target], v.chain_recv.at[i, j], (row, 2 * target + core)
        )

    def z_span(at_z, start=0, size=z_rows):
        return pl.ds(pl.multiple_of(at_z * z_rows + start, size), size)

    def z_device(step, to):
        return (RING * plane + (z + step) % RING, 2 * chip + to)

    def spread(i):
        place = v.cols.at[i, core, z_span(z)]
        copies = [copy(v.own.at[i, 1 - core], place, v.col_send.at[i, 0], v.col_recv.at[i, 0, core], sibling)]
        for slot, step in ((1, 1), (2, RING - 1)):
            for to in range(2):
                copies.append(
                    copy(
                        v.own.at[i, to],
                        place,
                        v.col_send.at[i, 2 * slot - 1 + to],
                        v.col_recv.at[i, slot, core],
                        z_device(step, to),
                    )
                )
        return copies

    def onward(i, side, slot):
        step, start = ((1, 0), (RING - 1, z_rows // 2))[slot - 1]
        place = v.cols.at[i, side, z_span((z - step) % RING, start, z_rows // 2)]
        return copy(
            place, place, v.col_relay.at[i, side, slot - 1], v.col_recv.at[i, slot + 2, side], z_device(step, core)
        )

    def arrived(i, side, slot):
        rows = z_span(z) if slot < 3 else z_span(z, 0, z_rows // 2)
        place = v.cols.at[i, side, rows]
        return copy(place, place, v.col_send.at[i, 0], v.col_recv.at[i, slot, side], sibling)

    def chain_step(d):
        i = chip - d

        def term(left, j):
            left = left.reshape(2 * z_rows, width)
            return dot3(split(left), (v.w_high[j], v.w_low[j])).reshape(2, z_rows, 2 * width)

        def add(value):
            for side in range(2):
                v.part[d, side] = v.part[d, side] + value[:, :, side * width : (side + 1) * width]

        value = term(v.starts[i], i)
        for side in range(2):
            v.part[d, side] = value[:, :, side * width : (side + 1) * width]

        def more(j, carry):
            copy(v.own.at[i], v.chain.at[i, j], v.chain_send.at[i, 0], v.chain_recv.at[i, j], sibling).wait_recv()
            add(term(v.chain[i, j], j))
            return carry

        lax.fori_loop(i + 1, chip, more, 0)
        trade(d).start()
        trade(d).wait_recv()
        v.own[i] = -(v.part[d, core] + v.part_in[d])

        def tell(target, carry):
            along(i, chip, target).start()
            return carry

        lax.fori_loop(chip + 1, CHIPS, tell, 0)
        for one in spread(i):
            one.start()
        v.cols[i, core, z_span(z)] = v.own[i, core]

    def relay(i):
        for side in range(2):
            for slot in (1, 2):
                arrived(i, side, slot).wait_recv()
                onward(i, side, slot).start()

    for one in fetch:
        one.wait()
    for side in range(2):
        high, low = split(v.inverse[side])
        v.inverse_high[side] = high
        v.inverse_low[side] = low

    def accumulate(idx):
        i = order(idx)

        @pl.when(i < chip)
        def _():
            arrived(i, 1 - core, 0).wait_recv()
            for side in range(2):
                for slot in (3, 4):
                    arrived(i, side, slot).wait_recv()
            lefts = split(got[i])
            for side in range(2):
                v.total[side] = v.total[side] + dot3(lefts, split(v.cols[i, side]))

    product(0)
    pl.when(chip == 0)(lead_push)
    give_factor.wait_recv()

    def couple_one(j, carry):
        couple(j)
        return carry

    lax.fori_loop(0, chip, couple_one, 0)
    lefts = split(got[chip])
    for side in range(2):
        span = slice(side * width, (side + 1) * width)
        v.total[side] = dot3(lefts, (v.inverse_high[core, :, span], v.inverse_low[core, :, span]))

    def one_solved(idx, carry):
        accumulate(idx)
        return carry

    def by_stage(stage, table):
        first, last = 0, 0
        for key, (low, high) in table.items():
            first = jnp.where(stage == key, low, first)
            last = jnp.where(stage == key, high, last)
        return first, last

    def body(stage, carry):
        @pl.when(stage == 1)
        def _():
            for one in own_sends[:2]:
                one.wait_recv()
            for one in half_sends:
                one.start()

        @pl.when(stage == 2)
        def _():
            for one in half_sends:
                one.wait_recv()
            for one in far_sends:
                one.start()

        pl.when(chip > stage)(lambda: chain_step(stage + 1))

        @pl.when(stage == 1)
        def _():
            own_sends[2].wait_recv()

        for k in range(3):

            @pl.when(stage == k + 1)
            def _():
                for one in partner_sends[k]:
                    one.start()

        @pl.when(stage == 4)
        def _():
            for one in sum(partner_sends, far_sends):
                one.wait_recv()

        def one_product(idx, carry):
            product(idx)
            return carry

        def one_pass(idx, carry):
            add_and_pass(idx)
            return carry

        def one_part(step, carry):
            pl.when(step == 0)(lead_wait)
            factor_part(v.work, v.grid, v.inverted, v.below, step // 3, step % 3)
            return carry

        lax.fori_loop(*by_stage(stage, {1: (1, 4), 2: (4, 5), 4: (5, 8)}), one_product, 0)
        pl.when((stage > 0) & (chip >= stage))(lambda: relay(chip - stage))
        lax.fori_loop(*by_stage(stage, {2: (0, 4), 3: (4, 5), 5: (5, 8)}), one_pass, 0)

        @pl.when(chip == 0)
        def _():
            pl.when(stage == 1)(lead_sum)
            lax.fori_loop(*by_stage(stage, {2: (0, 3), 3: (3, 6), 4: (6, 9), 5: (9, 12)}), one_part, 0)

        lax.fori_loop(*by_stage(stage, {5: (1, 3), 6: (3, 5)}), one_solved, 0)

        return carry

    lax.fori_loop(0, CHIPS - 1, body, 0)
    pl.when(chip == CHIPS - 1)(lambda: relay(0))
    cross()

    lax.fori_loop(5, CHIPS, one_solved, 0)
    give_total = copy(v.total.at[1 - core], v.total_in, v.total_send, v.total_recv, sibling)
    give_total.start()

    @pl.when(chip == 0)
    def _():
        shape = (2 * width, 2 * width)
        eye = lax.broadcasted_iota(jnp.int32, shape, 0) == lax.broadcasted_iota(jnp.int32, shape, 1)
        v.work[...] = jnp.where(eye, 1.0, 0.0)
        solve_rows(v.work, v.inverted, v.below)

    arrivals(plane)
    for part in range(2):
        cross_to(part).wait_recv()
        total = plane_sum(plane, part) + v.cross_in[part]
        shape = (width, width)
        shift = (row * 2 + part - (2 * chip + core)) * width
        there = lax.broadcasted_iota(jnp.int32, shape, 0) + shift == lax.broadcasted_iota(jnp.int32, shape, 1)
        gram_ref[pl.ds(part * width, width)] = jnp.where(there, 1.0, 0.0) + scale * total

    share = panel_ref.shape[0]
    other_span = pl.ds(pl.multiple_of((1 - core) * width, width), width)
    swap = copy(gram_ref.at[other_span], v.side, v.side_send, v.side_recv, sibling)

    def hand_out(m):
        return copy(
            v.first.at[pl.ds(m * share, share)], panel_ref, v.row_send.at[m], v.row_recv, (row, CHIPS * core + m)
        )

    @pl.when(chip == 0)
    def _():
        swap.start()
        v.first[:, own_span] = gram_ref[own_span]
        swap.wait_recv()
        v.first[:, other_span] = v.side[...]
        v.first[...] = jnp.dot(
            v.first[...], v.work[...], precision=lax.Precision.HIGHEST, preferred_element_type=jnp.float32
        )
        for m in range(1, CHIPS):
            hand_out(m).start()
        pl.when(core == 1)(lambda: hand_out(0).start())

        @pl.when(core == 0)
        def _():
            panel_ref[...] = v.first[pl.ds(0, share)]

    give_total.wait_recv()
    solved_ref[...] = v.total[core] + v.total_in[...]
    pl.when(col > 0)(lambda: hand_out(0).wait_recv())

    @pl.when(chip == 0)
    def _():
        for step in range(1, n_rows):
            for to in range(2):
                share_to(step, to).wait_send()
        share_to(0, 1 - core).wait_send()
        swap.wait_send()
        for m in range(1, CHIPS):
            hand_out(m).wait_send()
        pl.when(core == 1)(lambda: hand_out(0).wait_send())

    for one in sum(partner_sends, own_sends + half_sends + far_sends):
        one.wait_send()
    give_mine.wait_send()
    give_factor.wait_send()
    give_total.wait_send()

    def drain_push(block, carry):
        pl.when(ahead(block) == 0)(lambda: hand_beside(block).wait_send())
        for side in range(2):
            pl.when(ahead(block) == 2)(lambda: hop_to(block, side).wait_send())
            for to in range(2):
                pl.when(ahead(block) == (1, RING - 1)[side])(lambda: away(block, side, to).wait_send())
        return carry

    for part in range(2):
        cross_to(part).wait_send()
    lax.fori_loop(0, CHIPS, drain_push, 0)

    def drain_chain(i, carry):
        trade(chip - i).wait_send()

        def told(target, carry):
            along(i, chip, target).wait_send()
            return carry

        lax.fori_loop(chip + 1, CHIPS, told, 0)
        for one in spread(i):
            one.wait_send()
        for side in range(2):
            for slot in (1, 2):
                onward(i, side, slot).wait_send()
        return carry

    lax.fori_loop(0, chip, drain_chain, 0)


def finish_kernel(*refs):
    for source, target in zip(refs[:3], refs[3:]):
        target[...] = source[...]


def finish(values):
    vmem = pl.BlockSpec(memory_space=pltpu.VMEM)
    return pl.pallas_call(
        finish_kernel,
        out_shape=tuple(jax.ShapeDtypeStruct(a.shape, a.dtype) for a in values),
        in_specs=[vmem] * 3,
        out_specs=(vmem,) * 3,
    )(*values)


def on_device(iterate, factor, inverses):
    n, width = iterate.shape
    n_rows = lax.axis_size("row")
    n_cols = lax.axis_size("col")
    vmem = pl.BlockSpec(memory_space=pltpu.VMEM)
    scratch = scratch_shapes(n, width, n_rows)
    values = pl.pallas_call(
        functools.partial(fused_kernel, tuple(scratch)),
        out_shape=(
            jax.ShapeDtypeStruct((2 * width, width), jnp.float32),
            jax.ShapeDtypeStruct((2 * width // n_cols, 2 * width), jnp.float32),
            jax.ShapeDtypeStruct((n, width), jnp.float32),
        ),
        in_specs=[vmem, vmem, pl.BlockSpec(memory_space=pl.ANY)],
        out_specs=(vmem, vmem, vmem),
        scratch_shapes=list(scratch.values()),
        compiler_params=pltpu.CompilerParams(
            collective_id=0, has_side_effects=True, vmem_limit_bytes=60 << 20
        ),
        cost_estimate=pl.CostEstimate(flops=10**10, bytes_accessed=2 * 10**7, transcendentals=0),
    )(iterate, factor.reshape(CHIPS, 2, width, width), inverses.reshape(CHIPS, 2, width, 2 * width))
    return finish(values)


def solution(mesh):
    placed = (P("row", "col"), P(None, "col"), P())
    return jax.shard_map(
        on_device,
        mesh=mesh,
        in_specs=placed,
        out_specs=(P("row", "col"), P(("row", "col"), None), P("row", "col")),
        check_vma=False,
    )
```

```python
import functools
import types

import jax
import jax.numpy as jnp
from jax import lax
from jax.experimental import pallas as pl
from jax.experimental.pallas import tpu as pltpu
from jax.sharding import PartitionSpec as P

CHIPS = 8
RING = 4
MESH = pl.DeviceIdType.MESH


def split(value):
    high = value.astype(jnp.bfloat16)
    return high, (value - high.astype(jnp.float32)).astype(jnp.bfloat16)


def dot3(left, right):
    dot = functools.partial(jnp.dot, preferred_element_type=jnp.float32)
    return dot(left[0], right[0]) + (dot(left[0], right[1]) + dot(left[1], right[0]))


def dot3_turned(left, right):
    dot = functools.partial(
        lax.dot_general, dimension_numbers=(((0,), (0,)), ((), ())), preferred_element_type=jnp.float32
    )
    return dot(left[0], right[0]) + (dot(left[0], right[1]) + dot(left[1], right[0]))


def dot_exact_turned(left, right):
    return lax.dot_general(
        left, right, (((1,), (1,)), ((), ())), precision=lax.Precision.HIGHEST, preferred_element_type=jnp.float32
    )


def factor_block(grid, first, last):
    base = grid.shape[0]
    for p in range(first, last):
        rows = slice(8 * p, 8 * p + 8)
        panel = grid[rows]
        sub = lax.broadcasted_iota(jnp.int32, panel.shape, 0)
        columns = [jnp.broadcast_to(panel[:, 8 * p + c : 8 * p + c + 1], panel.shape) for c in range(8)]
        scales = jnp.ones_like(panel)
        for j in range(8):
            pivot = jnp.broadcast_to(columns[j][j : j + 1], panel.shape)
            below = jnp.where(sub > j, columns[j], 0.0) / pivot
            scales = jnp.where(sub == j, pivot, scales)
            for c in range(j + 1, 8):
                columns[c] = columns[c] - below * columns[c][j : j + 1]
            panel = panel - below * panel[j : j + 1]
        panel = panel / jnp.sqrt(scales)
        grid[rows] = panel
        if 8 * p + 8 < base:
            rest = slice(8 * p + 8, base)
            turned = panel[:, :base].T[8 * p + 8 :]
            value = grid[rest]
            for j in range(8):
                value = value - turned[:, j : j + 1] * panel[j : j + 1]
            grid[rest] = value


def factor_part(work, grid, inverted, below, s, part):
    base = grid.shape[0]
    span = pl.ds(pl.multiple_of(s * base, base), base)
    panels = base // 8

    @pl.when(part == 0)
    def _():
        shape = (base, base)
        eye = lax.broadcasted_iota(jnp.int32, shape, 0) == lax.broadcasted_iota(jnp.int32, shape, 1)
        grid[:, :base] = work[span, span]
        grid[:, base:] = jnp.where(eye, 1.0, 0.0)
        factor_block(grid, 0, panels * 2 // 5)

    pl.when(part == 1)(lambda: factor_block(grid, panels * 2 // 5, panels))

    @pl.when(part == 2)
    def _():
        inverted[s] = grid[:, base:]

        @pl.when((s + 1) * base == work.shape[0])
        def _():
            below[s] = jnp.zeros(below.shape[1:], jnp.float32)

        @pl.when((s + 1) * base < work.shape[0])
        def _():
            done = dot_exact_turned(work[:, span], grid[:, base:])
            later = lax.broadcasted_iota(jnp.int32, done.shape, 0) >= (s + 1) * base
            done = jnp.where(later, done, 0.0)
            below[s] = done
            work[...] = work[...] - dot_exact_turned(done, done)


def solve_rows(rows_ref, inverted, below):
    blocks, base, _ = inverted.shape

    def step(s, carry):
        span = pl.ds(pl.multiple_of(s * base, base), base)
        done = dot_exact_turned(rows_ref[:, span], inverted[s])
        rows_ref[...] = rows_ref[...] - dot_exact_turned(done, below[s])
        rows_ref[:, span] = done
        return carry

    lax.fori_loop(0, blocks, step, 0)


def scratch_shapes(n, width, n_rows):
    f32, bf16 = jnp.float32, jnp.bfloat16
    vmem, dma = pltpu.VMEM, pltpu.SemaphoreType.DMA
    z_rows = width // RING
    return dict(
        theirs=vmem((n, width), f32),
        got=vmem((CHIPS, n, width), f32),
        high=vmem((2, n, width), bf16),
        low=vmem((2, n, width), bf16),
        prod=vmem((CHIPS, 2, width, width), f32),
        hop=vmem((CHIPS, width, width), f32),
        land=vmem((2, 2, 2, width, width), f32),
        beside=vmem((2, width, width), f32),
        cross=vmem((2, width, width), f32),
        cross_in=vmem((2, width, width), f32),
        slices=vmem((n_rows, 2, width // n_rows, width), f32),
        work=vmem((2 * width, 2 * width), f32),
        grid=vmem((width // 2, width), f32),
        inverted=vmem((4, width // 2, width // 2), f32),
        below=vmem((4, 2 * width, width // 2), f32),
        lead_in=vmem((2 * width, 2 * width), f32),
        first=vmem((width, 2 * width), f32),
        side=vmem((width, width), f32),
        their_factor=vmem((CHIPS, width, width), f32),
        inverse=vmem((2, width, 2 * width), f32),
        inverse_high=vmem((2, width, 2 * width), bf16),
        inverse_low=vmem((2, width, 2 * width), bf16),
        starts=vmem((CHIPS, 2, z_rows, width), f32),
        w_high=vmem((CHIPS - 1, width, 2 * width), bf16),
        w_low=vmem((CHIPS - 1, width, 2 * width), bf16),
        chain=vmem((CHIPS - 1, CHIPS - 1, 2, z_rows, width), f32),
        part=vmem((CHIPS, 2, 2, z_rows, width), f32),
        part_in=vmem((CHIPS, 2, z_rows, width), f32),
        own=vmem((CHIPS - 1, 2, z_rows, width), f32),
        cols=vmem((CHIPS - 1, 2, width, width), f32),
        total=vmem((2, n, width), f32),
        total_in=vmem((n, width), f32),
        send=dma((13,)),
        recv=dma((13,)),
        theirs_send=dma,
        theirs_recv=dma,
        push=dma((CHIPS, 2, 2)),
        hop_send=dma((CHIPS, 2, 2)),
        hop_recv=dma((CHIPS, 2)),
        landed=dma((2, 2, 2, 2)),
        beside_recv=dma((2,)),
        cross_send=dma((2, 2)),
        cross_recv=dma((2, 2)),
        cut=dma((n_rows,)),
        cut_in=dma((n_rows,)),
        share=dma((n_rows, 2)),
        shared=dma((n_rows, 2)),
        local=dma((3,)),
        factor_send=dma,
        factor_recv=dma,
        part_send=dma((CHIPS,)),
        part_recv=dma((CHIPS,)),
        chain_send=dma((CHIPS, CHIPS)),
        chain_recv=dma((CHIPS, CHIPS)),
        col_send=dma((CHIPS, 5)),
        col_relay=dma((CHIPS, 2, 2)),
        col_recv=dma((CHIPS, 5, 2)),
        total_send=dma,
        total_recv=dma,
        side_send=dma,
        side_recv=dma,
        row_send=dma((CHIPS,)),
        row_recv=dma,
    )


def fused_kernel(names, mine_ref, factor_ref, inverses_ref, gram_ref, panel_ref, solved_ref, *scratch):
    v = types.SimpleNamespace(**dict(zip(names, scratch)))
    row = lax.axis_index("row")
    col = lax.axis_index("col")
    n_rows = lax.axis_size("row")
    n_cols = lax.axis_size("col")
    chip = col // 2
    core = col % 2
    x, y = chip % 4, chip // 4
    z, plane = row % RING, row // RING
    n, width = mine_ref.shape
    piece = width // n_rows
    z_rows = width // RING
    scale = 3.0 / (n * n_rows)
    sibling = (row, 2 * chip + 1 - core)

    barrier = pltpu.get_barrier_semaphore()
    for step in range(1, n_cols):
        pl.semaphore_signal(barrier, inc=1, device_id=(row, (col + step) % n_cols), device_id_type=MESH)
    for step in range(1, n_rows):
        for other in range(2):
            pl.semaphore_signal(
                barrier, inc=1, device_id=((row + step) % n_rows, 2 * chip + other), device_id_type=MESH
            )
    pl.semaphore_wait(barrier, n_cols - 1 + 2 * (n_rows - 1))

    def copy(source, target, out, arrival, device):
        return pltpu.make_async_remote_copy(
            src_ref=source, dst_ref=target, send_sem=out, recv_sem=arrival, device_id=device, device_id_type=MESH
        )

    def at(dx, dy):
        return 4 * ((y + dy) % 2) + (x + dx) % 4

    left, right, partner, far = at(3, 0), at(1, 0), at(0, 1), at(2, 0)
    at_right, at_left = (row, 2 * right + core), (row, 2 * left + core)
    at_partner = (row, 2 * partner + core)
    got = v.got
    top, low_half = pl.ds(0, n // 2), pl.ds(n // 2, n // 2)

    def block_copy(block, span, k, device, source=None):
        place = got.at[block] if span is None else got.at[block, span]
        return copy(place if source is None else source, place, v.send.at[k], v.recv.at[k], device)

    own_sends = [
        block_copy(chip, None, 0, at_right, mine_ref),
        block_copy(chip, None, 1, at_left, mine_ref),
        block_copy(chip, None, 2, at_partner, mine_ref),
    ]
    half_sends = [block_copy(left, top, 3, at_right), block_copy(right, low_half, 4, at_left)]
    thirds = [pl.ds(0, n * 3 // 8), pl.ds(n * 3 // 8, n * 3 // 8), pl.ds(n * 3 // 4, n // 4)]
    partner_sends = [
        [block_copy(partner, span, 5 + k, at_right), block_copy(partner, span, 8 + k, at_left)]
        for k, span in enumerate(thirds)
    ]
    far_sends = [block_copy(far, top, 11, at_partner), block_copy(far, low_half, 12, at_partner)]

    give_mine = copy(mine_ref, v.theirs, v.theirs_send, v.theirs_recv, sibling)
    give_factor = copy(factor_ref.at[:, 1 - core], v.their_factor, v.factor_send, v.factor_recv, sibling)
    own_span = pl.ds(pl.multiple_of(core * width, width), width)
    fetch = [
        pltpu.make_async_copy(inverses_ref.at[chip, 0], v.inverse.at[0], v.local.at[0]),
        pltpu.make_async_copy(inverses_ref.at[chip, 1], v.inverse.at[1], v.local.at[1]),
        pltpu.make_async_copy(
            inverses_ref.at[:, :, pl.ds(pl.multiple_of(z * z_rows, z_rows), z_rows), own_span], v.starts, v.local.at[2]
        ),
    ]
    give_mine.start()
    own_sends[0].start()
    own_sends[1].start()
    own_sends[2].start()
    give_factor.start()
    for one in fetch:
        one.start()
    got[chip] = mine_ref[...]
    own_high, own_low = split(mine_ref[...])
    v.high[core] = own_high
    v.low[core] = own_low
    give_mine.wait_recv()
    their_high, their_low = split(v.theirs[...])
    v.high[1 - core] = their_high
    v.low[1 - core] = their_low

    def order(idx):
        dx = jnp.where(
            (idx == 1) | (idx == 5), 3, jnp.where((idx == 2) | (idx == 6), 1, jnp.where((idx == 4) | (idx == 7), 2, 0))
        )
        dy = jnp.where((idx == 3) | (idx > 4), 1, 0)
        return at(dx, dy)

    def ahead(block):
        return (block % RING - z + RING) % RING

    def z_peer(step, to):
        return (RING * plane + (z + step) % RING, 2 * chip + to)

    halves = [pl.ds(0, width // 2), pl.ds(width // 2, width // 2)]

    def hop_to(block, side, c):
        step = (1, RING - 1)[side]
        return copy(
            v.prod.at[block, side, halves[c]],
            v.hop.at[block, halves[c]],
            v.hop_send.at[block, side, c],
            v.hop_recv.at[block, c],
            z_peer(step, core),
        )

    def away(block, side, to, c):
        step = (1, RING - 1)[side]
        return copy(
            v.prod.at[block, to, halves[c]],
            v.land.at[side, block // RING, core, halves[c]],
            v.push.at[block, to, c],
            v.landed.at[side, block // RING, core, c],
            z_peer(step, to),
        )

    def hand_beside(block):
        return copy(
            v.prod.at[block, 1 - core],
            v.beside.at[block // RING],
            v.push.at[block, 1 - core, 0],
            v.beside_recv.at[block // RING],
            sibling,
        )

    def product(idx):
        block = order(idx)
        lefts = split(got[block])
        for to in range(2):
            v.prod[block, to] = dot3_turned(lefts, (v.high[to], v.low[to]))
        pl.when(ahead(block) == 0)(lambda: hand_beside(block).start())

        @pl.when(ahead(block) == 2)
        def _():
            for c in range(2):
                for side in range(2):
                    hop_to(block, side, c).start()

        for side in range(2):

            @pl.when(ahead(block) == (1, RING - 1)[side])
            def _():
                for c in range(2):
                    away(block, side, 1 - side, c).start()

    def add_and_pass(idx):
        block = order(idx)
        for side in range(2):

            @pl.when(ahead(block) == (1, RING - 1)[side])
            def _():
                for c in range(2):
                    rows = halves[c]
                    hop_to(block, side, c).wait_recv()
                    v.prod[block, side, rows] = v.prod[block, side, rows] + v.hop[block, rows]
                    away(block, side, side, c).start()

    def plane_sum(to_plane, part, c):
        rows = halves[c]
        total = v.land[0, to_plane, part, rows] + v.land[1, to_plane, part, rows]
        mine = jnp.where(core == part, 1, 0)
        return total + jnp.where(mine == 1, v.prod[RING * to_plane + z, core, rows], v.beside[to_plane, rows])

    def cross_to(part, c):
        return copy(
            v.cross.at[part, halves[c]],
            v.cross_in.at[part, halves[c]],
            v.cross_send.at[part, c],
            v.cross_recv.at[part, c],
            (RING * (1 - plane) + z, col),
        )

    def arrivals(to_plane, c):
        if c == 0:
            copy(v.cross.at[0], v.beside.at[0], v.push.at[0, 0, 0], v.beside_recv.at[to_plane], sibling).wait_recv()
        for part in range(2):
            for side in range(2):
                copy(
                    v.cross.at[0, halves[0]],
                    v.cross_in.at[0, halves[0]],
                    v.push.at[0, 0, 0],
                    v.landed.at[side, to_plane, part, c],
                    sibling,
                ).wait_recv()

    def cross():
        for c in range(2):
            arrivals(1 - plane, c)
            for part in range(2):
                v.cross[part, halves[c]] = plane_sum(1 - plane, part, c)
                cross_to(part, c).start()

    def slice_to(other):
        return copy(
            v.prod.at[0, :, pl.ds(pl.multiple_of(other * piece, piece), piece)],
            v.slices.at[row],
            v.cut.at[other],
            v.cut_in.at[row],
            (other, core),
        )

    def lead_rows(at_row, at_core):
        return v.lead_in.at[pl.ds(pl.multiple_of(at_core * width + at_row * piece, piece), piece)]

    def share_to(step, to):
        rows = lead_rows(row, core)
        return copy(rows, rows, v.share.at[step, to], v.shared.at[row, core], ((row + step) % n_rows, to))

    def lead_push():
        for step in range(1, n_rows):
            slice_to((row + step) % n_rows).start()
        v.slices[row] = v.prod[0, :, pl.ds(pl.multiple_of(row * piece, piece), piece)]

    def lead_sum():
        for step in range(1, n_rows):
            source = (row + step) % n_rows
            copy(
                v.slices.at[row], v.slices.at[source], v.cut.at[source], v.cut_in.at[source], (source, core)
            ).wait_recv()
            slice_to(source).wait_send()
        total = v.slices[0]
        for other in range(1, n_rows):
            total = total + v.slices[other]
        whole = scale * jnp.concatenate([total[0], total[1]], axis=1)
        first = core * width + row * piece
        shape = (piece, 2 * width)
        there = lax.broadcasted_iota(jnp.int32, shape, 0) + first == lax.broadcasted_iota(jnp.int32, shape, 1)
        lead_rows(row, core)[...] = whole + jnp.where(there, 1.0, 0.0)
        for step in range(1, n_rows):
            for to in range(2):
                share_to(step, to).start()
        share_to(0, 1 - core).start()

    def lead_wait():
        for step in range(n_rows):
            for other in range(2):
                source = (row + step) % n_rows

                @pl.when((step > 0) | (core != other))
                def _():
                    rows = lead_rows(source, other)
                    copy(rows, rows, v.share.at[0, 0], v.shared.at[source, other], (source, 0)).wait_recv()

        v.work[...] = v.lead_in[...]

    def couple(j):
        pairs = [(v.inverse_high[side], v.inverse_low[side]) for side in (core, 1 - core)]
        value = dot3(split(factor_ref[j, core]), pairs[0]) + dot3(split(v.their_factor[j]), pairs[1])
        w_high, w_low = split(value)
        v.w_high[j] = w_high
        v.w_low[j] = w_low

    def trade(d):
        return copy(v.part.at[d, 1 - core], v.part_in.at[d], v.part_send.at[d], v.part_recv.at[d], sibling)

    def along(i, j, target):
        return copy(
            v.own.at[i], v.chain.at[i, j], v.chain_send.at[i, target], v.chain_recv.at[i, j], (row, 2 * target + core)
        )

    def z_span(at_z, start=0, size=z_rows):
        return pl.ds(pl.multiple_of(at_z * z_rows + start, size), size)

    def z_device(step, to):
        return (RING * plane + (z + step) % RING, 2 * chip + to)

    def spread(i):
        place = v.cols.at[i, core, z_span(z)]
        copies = [copy(v.own.at[i, 1 - core], place, v.col_send.at[i, 0], v.col_recv.at[i, 0, core], sibling)]
        for slot, step in ((1, 1), (2, RING - 1)):
            for to in range(2):
                copies.append(
                    copy(
                        v.own.at[i, to],
                        place,
                        v.col_send.at[i, 2 * slot - 1 + to],
                        v.col_recv.at[i, slot, core],
                        z_device(step, to),
                    )
                )
        return copies

    def onward(i, side, slot):
        step, start = ((1, 0), (RING - 1, z_rows // 2))[slot - 1]
        place = v.cols.at[i, side, z_span((z - step) % RING, start, z_rows // 2)]
        return copy(
            place, place, v.col_relay.at[i, side, slot - 1], v.col_recv.at[i, slot + 2, side], z_device(step, core)
        )

    def arrived(i, side, slot):
        rows = z_span(z) if slot < 3 else z_span(z, 0, z_rows // 2)
        place = v.cols.at[i, side, rows]
        return copy(place, place, v.col_send.at[i, 0], v.col_recv.at[i, slot, side], sibling)

    def chain_step(d):
        i = chip - d

        def term(left, j):
            left = left.reshape(2 * z_rows, width)
            return dot3(split(left), (v.w_high[j], v.w_low[j])).reshape(2, z_rows, 2 * width)

        def add(value):
            for side in range(2):
                v.part[d, side] = v.part[d, side] + value[:, :, side * width : (side + 1) * width]

        value = term(v.starts[i], i)
        for side in range(2):
            v.part[d, side] = value[:, :, side * width : (side + 1) * width]

        def more(j, carry):
            copy(v.own.at[i], v.chain.at[i, j], v.chain_send.at[i, 0], v.chain_recv.at[i, j], sibling).wait_recv()
            add(term(v.chain[i, j], j))
            return carry

        lax.fori_loop(i + 1, chip, more, 0)
        trade(d).start()
        trade(d).wait_recv()
        v.own[i] = -(v.part[d, core] + v.part_in[d])

        def tell(target, carry):
            along(i, chip, target).start()
            return carry

        lax.fori_loop(chip + 1, CHIPS, tell, 0)
        for one in spread(i):
            one.start()
        v.cols[i, core, z_span(z)] = v.own[i, core]

    def relay(i):
        for side in range(2):
            for slot in (1, 2):
                arrived(i, side, slot).wait_recv()
                onward(i, side, slot).start()

    for one in fetch:
        one.wait()
    for side in range(2):
        high, low = split(v.inverse[side])
        v.inverse_high[side] = high
        v.inverse_low[side] = low

    def accumulate(idx):
        i = order(idx)

        @pl.when(i < chip)
        def _():
            arrived(i, 1 - core, 0).wait_recv()
            for side in range(2):
                for slot in (3, 4):
                    arrived(i, side, slot).wait_recv()
            lefts = split(got[i])
            for side in range(2):
                v.total[side] = v.total[side] + dot3(lefts, split(v.cols[i, side]))

    product(0)
    pl.when(chip == 0)(lead_push)
    give_factor.wait_recv()

    def couple_one(j, carry):
        couple(j)
        return carry

    lax.fori_loop(0, chip, couple_one, 0)
    lefts = split(got[chip])
    for side in range(2):
        span = slice(side * width, (side + 1) * width)
        v.total[side] = dot3(lefts, (v.inverse_high[core, :, span], v.inverse_low[core, :, span]))

    def one_solved(idx, carry):
        accumulate(idx)
        return carry

    def by_stage(stage, table):
        first, last = 0, 0
        for key, (low, high) in table.items():
            first = jnp.where(stage == key, low, first)
            last = jnp.where(stage == key, high, last)
        return first, last

    def body(stage, carry):
        @pl.when(stage == 1)
        def _():
            for one in own_sends[:2]:
                one.wait_recv()
            for one in half_sends:
                one.start()

        @pl.when(stage == 2)
        def _():
            for one in half_sends:
                one.wait_recv()
            for one in far_sends:
                one.start()

        pl.when(chip > stage)(lambda: chain_step(stage + 1))

        @pl.when(stage == 1)
        def _():
            own_sends[2].wait_recv()

        for k in range(3):

            @pl.when(stage == k + 1)
            def _():
                for one in partner_sends[k]:
                    one.start()

        @pl.when(stage == 4)
        def _():
            for one in sum(partner_sends, far_sends):
                one.wait_recv()

        def one_product(idx, carry):
            product(idx)
            return carry

        def one_pass(idx, carry):
            add_and_pass(idx)
            return carry

        def one_part(step, carry):
            pl.when(step == 0)(lead_wait)
            factor_part(v.work, v.grid, v.inverted, v.below, step // 3, step % 3)
            return carry

        lax.fori_loop(*by_stage(stage, {1: (1, 4), 2: (4, 5), 4: (5, 8)}), one_product, 0)
        pl.when((stage > 0) & (chip >= stage))(lambda: relay(chip - stage))
        lax.fori_loop(*by_stage(stage, {2: (0, 4), 3: (4, 5), 5: (5, 8)}), one_pass, 0)

        @pl.when(chip == 0)
        def _():
            pl.when(stage == 1)(lead_sum)
            lax.fori_loop(*by_stage(stage, {2: (0, 2), 3: (2, 5), 4: (5, 9), 5: (9, 12)}), one_part, 0)

        lax.fori_loop(*by_stage(stage, {5: (1, 3), 6: (3, 5)}), one_solved, 0)

        return carry

    lax.fori_loop(0, CHIPS - 1, body, 0)
    pl.when(chip == CHIPS - 1)(lambda: relay(0))
    cross()

    lax.fori_loop(5, CHIPS, one_solved, 0)
    give_total = copy(v.total.at[1 - core], v.total_in, v.total_send, v.total_recv, sibling)
    give_total.start()

    @pl.when(chip == 0)
    def _():
        shape = (2 * width, 2 * width)
        eye = lax.broadcasted_iota(jnp.int32, shape, 0) == lax.broadcasted_iota(jnp.int32, shape, 1)
        v.work[...] = jnp.where(eye, 1.0, 0.0)
        solve_rows(v.work, v.inverted, v.below)

    for c in range(2):
        arrivals(plane, c)
        for part in range(2):
            cross_to(part, c).wait_recv()
            total = plane_sum(plane, part, c) + v.cross_in[part, halves[c]]
            shift = (row * 2 + part - (2 * chip + core)) * width + c * (width // 2)
            there = lax.broadcasted_iota(jnp.int32, total.shape, 0) + shift == lax.broadcasted_iota(
                jnp.int32, total.shape, 1
            )
            rows = pl.ds(part * width + c * (width // 2), width // 2)
            gram_ref[rows] = jnp.where(there, 1.0, 0.0) + scale * total

    share = panel_ref.shape[0]
    other_span = pl.ds(pl.multiple_of((1 - core) * width, width), width)
    swap = copy(gram_ref.at[other_span], v.side, v.side_send, v.side_recv, sibling)

    def hand_out(m):
        return copy(
            v.first.at[pl.ds(m * share, share)], panel_ref, v.row_send.at[m], v.row_recv, (row, CHIPS * core + m)
        )

    @pl.when(chip == 0)
    def _():
        swap.start()
        v.first[:, own_span] = gram_ref[own_span]
        swap.wait_recv()
        v.first[:, other_span] = v.side[...]
        v.first[...] = jnp.dot(
            v.first[...], v.work[...], precision=lax.Precision.HIGHEST, preferred_element_type=jnp.float32
        )
        for m in range(1, CHIPS):
            hand_out(m).start()
        pl.when(core == 1)(lambda: hand_out(0).start())

        @pl.when(core == 0)
        def _():
            panel_ref[...] = v.first[pl.ds(0, share)]

    give_total.wait_recv()
    solved_ref[...] = v.total[core] + v.total_in[...]
    pl.when(col > 0)(lambda: hand_out(0).wait_recv())

    @pl.when(chip == 0)
    def _():
        for step in range(1, n_rows):
            for to in range(2):
                share_to(step, to).wait_send()
        share_to(0, 1 - core).wait_send()
        swap.wait_send()
        for m in range(1, CHIPS):
            hand_out(m).wait_send()
        pl.when(core == 1)(lambda: hand_out(0).wait_send())

    for one in sum(partner_sends, own_sends + half_sends + far_sends):
        one.wait_send()
    give_mine.wait_send()
    give_factor.wait_send()
    give_total.wait_send()

    def drain_push(block, carry):
        pl.when(ahead(block) == 0)(lambda: hand_beside(block).wait_send())
        for c in range(2):
            for side in range(2):
                pl.when(ahead(block) == 2)(lambda: hop_to(block, side, c).wait_send())
                for to in range(2):
                    pl.when(ahead(block) == (1, RING - 1)[side])(lambda: away(block, side, to, c).wait_send())
        return carry

    for part in range(2):
        for c in range(2):
            cross_to(part, c).wait_send()
    lax.fori_loop(0, CHIPS, drain_push, 0)

    def drain_chain(i, carry):
        trade(chip - i).wait_send()

        def told(target, carry):
            along(i, chip, target).wait_send()
            return carry

        lax.fori_loop(chip + 1, CHIPS, told, 0)
        for one in spread(i):
            one.wait_send()
        for side in range(2):
            for slot in (1, 2):
                onward(i, side, slot).wait_send()
        return carry

    lax.fori_loop(0, chip, drain_chain, 0)


def finish_kernel(*refs):
    for source, target in zip(refs[:3], refs[3:]):
        target[...] = source[...]


def finish(values):
    vmem = pl.BlockSpec(memory_space=pltpu.VMEM)
    return pl.pallas_call(
        finish_kernel,
        out_shape=tuple(jax.ShapeDtypeStruct(a.shape, a.dtype) for a in values),
        in_specs=[vmem] * 3,
        out_specs=(vmem,) * 3,
    )(*values)


def on_device(iterate, factor, inverses):
    n, width = iterate.shape
    n_rows = lax.axis_size("row")
    n_cols = lax.axis_size("col")
    vmem = pl.BlockSpec(memory_space=pltpu.VMEM)
    scratch = scratch_shapes(n, width, n_rows)
    values = pl.pallas_call(
        functools.partial(fused_kernel, tuple(scratch)),
        out_shape=(
            jax.ShapeDtypeStruct((2 * width, width), jnp.float32),
            jax.ShapeDtypeStruct((2 * width // n_cols, 2 * width), jnp.float32),
            jax.ShapeDtypeStruct((n, width), jnp.float32),
        ),
        in_specs=[vmem, vmem, pl.BlockSpec(memory_space=pl.ANY)],
        out_specs=(vmem, vmem, vmem),
        scratch_shapes=list(scratch.values()),
        compiler_params=pltpu.CompilerParams(
            collective_id=0, has_side_effects=True, vmem_limit_bytes=60 << 20
        ),
        cost_estimate=pl.CostEstimate(flops=10**10, bytes_accessed=2 * 10**7, transcendentals=0),
    )(iterate, factor.reshape(CHIPS, 2, width, width), inverses.reshape(CHIPS, 2, width, 2 * width))
    return finish(values)


def solution(mesh):
    placed = (P("row", "col"), P(None, "col"), P())
    return jax.shard_map(
        on_device,
        mesh=mesh,
        in_specs=placed,
        out_specs=(P("row", "col"), P(("row", "col"), None), P("row", "col")),
        check_vma=False,
    )
```

```python
import functools
import types

import jax
import jax.numpy as jnp
from jax import lax
from jax.experimental import pallas as pl
from jax.experimental.pallas import tpu as pltpu
from jax.sharding import PartitionSpec as P

CHIPS = 8
RING = 4
MESH = pl.DeviceIdType.MESH


def split(value):
    high = value.astype(jnp.bfloat16)
    return high, (value - high.astype(jnp.float32)).astype(jnp.bfloat16)


def dot3(left, right):
    dot = functools.partial(jnp.dot, preferred_element_type=jnp.float32)
    return dot(left[0], right[0]) + (dot(left[0], right[1]) + dot(left[1], right[0]))


def dot3_turned(left, right):
    dot = functools.partial(
        lax.dot_general, dimension_numbers=(((0,), (0,)), ((), ())), preferred_element_type=jnp.float32
    )
    return dot(left[0], right[0]) + (dot(left[0], right[1]) + dot(left[1], right[0]))


def dot_exact_turned(left, right):
    return lax.dot_general(
        left, right, (((1,), (1,)), ((), ())), precision=lax.Precision.HIGHEST, preferred_element_type=jnp.float32
    )


def factor_block(grid, first, last):
    base = grid.shape[0]
    for p in range(first, last):
        rows = slice(8 * p, 8 * p + 8)
        panel = grid[rows]
        sub = lax.broadcasted_iota(jnp.int32, panel.shape, 0)
        columns = [jnp.broadcast_to(panel[:, 8 * p + c : 8 * p + c + 1], panel.shape) for c in range(8)]
        scales = jnp.ones_like(panel)
        for j in range(8):
            pivot = jnp.broadcast_to(columns[j][j : j + 1], panel.shape)
            below = jnp.where(sub > j, columns[j], 0.0) / pivot
            scales = jnp.where(sub == j, pivot, scales)
            for c in range(j + 1, 8):
                columns[c] = columns[c] - below * columns[c][j : j + 1]
            panel = panel - below * panel[j : j + 1]
        panel = panel / jnp.sqrt(scales)
        grid[rows] = panel
        if 8 * p + 8 < base:
            rest = slice(8 * p + 8, base)
            turned = panel[:, :base].T[8 * p + 8 :]
            value = grid[rest]
            for j in range(8):
                value = value - turned[:, j : j + 1] * panel[j : j + 1]
            grid[rest] = value


def factor_part(work, grid, inverted, below, s, part):
    base = grid.shape[0]
    span = pl.ds(pl.multiple_of(s * base, base), base)
    panels = base // 8

    @pl.when(part == 0)
    def _():
        shape = (base, base)
        eye = lax.broadcasted_iota(jnp.int32, shape, 0) == lax.broadcasted_iota(jnp.int32, shape, 1)
        grid[:, :base] = work[span, span]
        grid[:, base:] = jnp.where(eye, 1.0, 0.0)
        factor_block(grid, 0, panels * 2 // 5)

    pl.when(part == 1)(lambda: factor_block(grid, panels * 2 // 5, panels))

    @pl.when(part == 2)
    def _():
        inverted[s] = grid[:, base:]

        @pl.when((s + 1) * base == work.shape[0])
        def _():
            below[s] = jnp.zeros(below.shape[1:], jnp.float32)

        @pl.when((s + 1) * base < work.shape[0])
        def _():
            done = dot_exact_turned(work[:, span], grid[:, base:])
            later = lax.broadcasted_iota(jnp.int32, done.shape, 0) >= (s + 1) * base
            done = jnp.where(later, done, 0.0)
            below[s] = done
            work[...] = work[...] - dot_exact_turned(done, done)


def solve_rows(rows_ref, inverted, below):
    blocks, base, _ = inverted.shape

    def step(s, carry):
        span = pl.ds(pl.multiple_of(s * base, base), base)
        done = dot_exact_turned(rows_ref[:, span], inverted[s])
        rows_ref[...] = rows_ref[...] - dot_exact_turned(done, below[s])
        rows_ref[:, span] = done
        return carry

    lax.fori_loop(0, blocks, step, 0)


def scratch_shapes(n, width, n_rows):
    f32, bf16 = jnp.float32, jnp.bfloat16
    vmem, dma = pltpu.VMEM, pltpu.SemaphoreType.DMA
    z_rows = width // RING
    return dict(
        theirs=vmem((n, width), f32),
        got=vmem((CHIPS, n, width), f32),
        high=vmem((2, n, width), bf16),
        low=vmem((2, n, width), bf16),
        prod=vmem((CHIPS, 2, width, width), f32),
        hop=vmem((CHIPS, width, width), f32),
        land=vmem((2, 2, 2, width, width), f32),
        beside=vmem((2, width, width), f32),
        cross=vmem((2, width, width), f32),
        cross_in=vmem((2, width, width), f32),
        slices=vmem((n_rows, 2, width // n_rows, width), f32),
        work=vmem((2 * width, 2 * width), f32),
        grid=vmem((width // 2, width), f32),
        inverted=vmem((4, width // 2, width // 2), f32),
        below=vmem((4, 2 * width, width // 2), f32),
        lead_in=vmem((2 * width, 2 * width), f32),
        first=vmem((width, 2 * width), f32),
        side=vmem((width, width), f32),
        their_factor=vmem((CHIPS, width, width), f32),
        inverse=vmem((2, width, 2 * width), f32),
        inverse_high=vmem((2, width, 2 * width), bf16),
        inverse_low=vmem((2, width, 2 * width), bf16),
        starts=vmem((CHIPS, z_rows, width), f32),
        w_high=vmem((CHIPS - 1, width, 2 * width), bf16),
        w_low=vmem((CHIPS - 1, width, 2 * width), bf16),
        chain=vmem((CHIPS - 1, CHIPS - 1, z_rows, width), f32),
        part=vmem((CHIPS, 2, z_rows, width), f32),
        part_in=vmem((CHIPS, z_rows, width), f32),
        own=vmem((CHIPS - 1, z_rows, width), f32),
        cols=vmem((CHIPS - 1, 2, width, width), f32),
        total=vmem((2, n, width), f32),
        total_in=vmem((n, width), f32),
        send=dma((13,)),
        recv=dma((13,)),
        theirs_send=dma,
        theirs_recv=dma,
        push=dma((CHIPS, 2, 2)),
        hop_send=dma((CHIPS, 2, 2)),
        hop_recv=dma((CHIPS, 2)),
        landed=dma((2, 2, 2, 2)),
        beside_recv=dma((2,)),
        cross_send=dma((2, 2)),
        cross_recv=dma((2, 2)),
        cut=dma((n_rows,)),
        cut_in=dma((n_rows,)),
        share=dma((n_rows, 2)),
        shared=dma((n_rows, 2)),
        local=dma((3,)),
        factor_send=dma,
        factor_recv=dma,
        part_send=dma((CHIPS,)),
        part_recv=dma((CHIPS,)),
        chain_send=dma((CHIPS, CHIPS)),
        chain_recv=dma((CHIPS, CHIPS)),
        seed_send=dma((CHIPS, 2)),
        seed_recv=dma((CHIPS, 2)),
        near_send=dma((CHIPS, 2, 2)),
        col_relay=dma((CHIPS, 2, 2)),
        col_recv=dma((CHIPS, 5, 2)),
        total_send=dma,
        total_recv=dma,
        side_send=dma,
        side_recv=dma,
        row_send=dma((CHIPS,)),
        row_recv=dma,
    )


def fused_kernel(names, mine_ref, factor_ref, inverses_ref, gram_ref, panel_ref, solved_ref, *scratch):
    v = types.SimpleNamespace(**dict(zip(names, scratch)))
    row = lax.axis_index("row")
    col = lax.axis_index("col")
    n_rows = lax.axis_size("row")
    n_cols = lax.axis_size("col")
    chip = col // 2
    core = col % 2
    x, y = chip % 4, chip // 4
    z, plane = row % RING, row // RING
    n, width = mine_ref.shape
    piece = width // n_rows
    z_rows = width // RING
    scale = 3.0 / (n * n_rows)
    sibling = (row, 2 * chip + 1 - core)

    barrier = pltpu.get_barrier_semaphore()
    for step in range(1, n_cols):
        pl.semaphore_signal(barrier, inc=1, device_id=(row, (col + step) % n_cols), device_id_type=MESH)
    for step in range(1, n_rows):
        for other in range(2):
            pl.semaphore_signal(
                barrier, inc=1, device_id=((row + step) % n_rows, 2 * chip + other), device_id_type=MESH
            )
    pl.semaphore_wait(barrier, n_cols - 1 + 2 * (n_rows - 1))

    def copy(source, target, out, arrival, device):
        return pltpu.make_async_remote_copy(
            src_ref=source, dst_ref=target, send_sem=out, recv_sem=arrival, device_id=device, device_id_type=MESH
        )

    def at(dx, dy):
        return 4 * ((y + dy) % 2) + (x + dx) % 4

    left, right, partner, far = at(3, 0), at(1, 0), at(0, 1), at(2, 0)
    at_right, at_left = (row, 2 * right + core), (row, 2 * left + core)
    at_partner = (row, 2 * partner + core)
    got = v.got
    top, low_half = pl.ds(0, n // 2), pl.ds(n // 2, n // 2)

    def block_copy(block, span, k, device, source=None):
        place = got.at[block] if span is None else got.at[block, span]
        return copy(place if source is None else source, place, v.send.at[k], v.recv.at[k], device)

    own_sends = [
        block_copy(chip, None, 0, at_right, mine_ref),
        block_copy(chip, None, 1, at_left, mine_ref),
        block_copy(chip, None, 2, at_partner, mine_ref),
    ]
    half_sends = [block_copy(left, top, 3, at_right), block_copy(right, low_half, 4, at_left)]
    thirds = [pl.ds(0, n * 3 // 8), pl.ds(n * 3 // 8, n * 3 // 8), pl.ds(n * 3 // 4, n // 4)]
    partner_sends = [
        [block_copy(partner, span, 5 + k, at_right), block_copy(partner, span, 8 + k, at_left)]
        for k, span in enumerate(thirds)
    ]
    far_sends = [block_copy(far, top, 11, at_partner), block_copy(far, low_half, 12, at_partner)]

    give_mine = copy(mine_ref, v.theirs, v.theirs_send, v.theirs_recv, sibling)
    give_factor = copy(factor_ref.at[:, 1 - core], v.their_factor, v.factor_send, v.factor_recv, sibling)
    own_span = pl.ds(pl.multiple_of(core * width, width), width)
    fetch = [
        pltpu.make_async_copy(inverses_ref.at[chip, 0], v.inverse.at[0], v.local.at[0]),
        pltpu.make_async_copy(inverses_ref.at[chip, 1], v.inverse.at[1], v.local.at[1]),
        pltpu.make_async_copy(
            inverses_ref.at[:, plane, pl.ds(pl.multiple_of(z * z_rows, z_rows), z_rows), own_span], v.starts, v.local.at[2]
        ),
    ]
    give_mine.start()
    own_sends[0].start()
    own_sends[1].start()
    own_sends[2].start()
    give_factor.start()
    for one in fetch:
        one.start()
    got[chip] = mine_ref[...]
    own_high, own_low = split(mine_ref[...])
    v.high[core] = own_high
    v.low[core] = own_low
    give_mine.wait_recv()
    their_high, their_low = split(v.theirs[...])
    v.high[1 - core] = their_high
    v.low[1 - core] = their_low

    def order(idx):
        dx = jnp.where(
            (idx == 1) | (idx == 5), 3, jnp.where((idx == 2) | (idx == 6), 1, jnp.where((idx == 4) | (idx == 7), 2, 0))
        )
        dy = jnp.where((idx == 3) | (idx > 4), 1, 0)
        return at(dx, dy)

    def ahead(block):
        return (block % RING - z + RING) % RING

    def z_peer(step, to):
        return (RING * plane + (z + step) % RING, 2 * chip + to)

    halves = [pl.ds(0, width // 2), pl.ds(width // 2, width // 2)]

    def hop_to(block, side, c):
        step = (1, RING - 1)[side]
        return copy(
            v.prod.at[block, side, halves[c]],
            v.hop.at[block, halves[c]],
            v.hop_send.at[block, side, c],
            v.hop_recv.at[block, c],
            z_peer(step, core),
        )

    def away(block, side, to, c):
        step = (1, RING - 1)[side]
        return copy(
            v.prod.at[block, to, halves[c]],
            v.land.at[side, block // RING, core, halves[c]],
            v.push.at[block, to, c],
            v.landed.at[side, block // RING, core, c],
            z_peer(step, to),
        )

    def hand_beside(block):
        return copy(
            v.prod.at[block, 1 - core],
            v.beside.at[block // RING],
            v.push.at[block, 1 - core, 0],
            v.beside_recv.at[block // RING],
            sibling,
        )

    def product(idx):
        block = order(idx)
        lefts = split(got[block])
        for to in range(2):
            v.prod[block, to] = dot3_turned(lefts, (v.high[to], v.low[to]))
        pl.when(ahead(block) == 0)(lambda: hand_beside(block).start())

        @pl.when(ahead(block) == 2)
        def _():
            for c in range(2):
                for side in range(2):
                    hop_to(block, side, c).start()

        for side in range(2):

            @pl.when(ahead(block) == (1, RING - 1)[side])
            def _():
                for c in range(2):
                    away(block, side, 1 - side, c).start()

    def add_and_pass(idx):
        block = order(idx)
        for side in range(2):

            @pl.when(ahead(block) == (1, RING - 1)[side])
            def _():
                for c in range(2):
                    rows = halves[c]
                    hop_to(block, side, c).wait_recv()
                    v.prod[block, side, rows] = v.prod[block, side, rows] + v.hop[block, rows]
                    away(block, side, side, c).start()

    def plane_sum(to_plane, part, c):
        rows = halves[c]
        total = v.land[0, to_plane, part, rows] + v.land[1, to_plane, part, rows]
        mine = jnp.where(core == part, 1, 0)
        return total + jnp.where(mine == 1, v.prod[RING * to_plane + z, core, rows], v.beside[to_plane, rows])

    def cross_to(part, c):
        return copy(
            v.cross.at[part, halves[c]],
            v.cross_in.at[part, halves[c]],
            v.cross_send.at[part, c],
            v.cross_recv.at[part, c],
            (RING * (1 - plane) + z, col),
        )

    def arrivals(to_plane, c):
        if c == 0:
            copy(v.cross.at[0], v.beside.at[0], v.push.at[0, 0, 0], v.beside_recv.at[to_plane], sibling).wait_recv()
        for part in range(2):
            for side in range(2):
                copy(
                    v.cross.at[0, halves[0]],
                    v.cross_in.at[0, halves[0]],
                    v.push.at[0, 0, 0],
                    v.landed.at[side, to_plane, part, c],
                    sibling,
                ).wait_recv()

    def cross():
        for c in range(2):
            arrivals(1 - plane, c)
            for part in range(2):
                v.cross[part, halves[c]] = plane_sum(1 - plane, part, c)
                cross_to(part, c).start()

    def slice_to(other):
        return copy(
            v.prod.at[0, :, pl.ds(pl.multiple_of(other * piece, piece), piece)],
            v.slices.at[row],
            v.cut.at[other],
            v.cut_in.at[row],
            (other, core),
        )

    def lead_rows(at_row, at_core):
        return v.lead_in.at[pl.ds(pl.multiple_of(at_core * width + at_row * piece, piece), piece)]

    def share_to(step, to):
        rows = lead_rows(row, core)
        return copy(rows, rows, v.share.at[step, to], v.shared.at[row, core], ((row + step) % n_rows, to))

    def lead_push():
        for step in range(1, n_rows):
            slice_to((row + step) % n_rows).start()
        v.slices[row] = v.prod[0, :, pl.ds(pl.multiple_of(row * piece, piece), piece)]

    def lead_sum():
        for step in range(1, n_rows):
            source = (row + step) % n_rows
            copy(
                v.slices.at[row], v.slices.at[source], v.cut.at[source], v.cut_in.at[source], (source, core)
            ).wait_recv()
            slice_to(source).wait_send()
        total = v.slices[0]
        for other in range(1, n_rows):
            total = total + v.slices[other]
        whole = scale * jnp.concatenate([total[0], total[1]], axis=1)
        first = core * width + row * piece
        shape = (piece, 2 * width)
        there = lax.broadcasted_iota(jnp.int32, shape, 0) + first == lax.broadcasted_iota(jnp.int32, shape, 1)
        lead_rows(row, core)[...] = whole + jnp.where(there, 1.0, 0.0)
        for step in range(1, n_rows):
            for to in range(2):
                share_to(step, to).start()
        share_to(0, 1 - core).start()

    def lead_wait():
        for step in range(n_rows):
            for other in range(2):
                source = (row + step) % n_rows

                @pl.when((step > 0) | (core != other))
                def _():
                    rows = lead_rows(source, other)
                    copy(rows, rows, v.share.at[0, 0], v.shared.at[source, other], (source, 0)).wait_recv()

        v.work[...] = v.lead_in[...]

    def couple(j):
        pairs = [(v.inverse_high[side], v.inverse_low[side]) for side in (core, 1 - core)]
        value = dot3(split(factor_ref[j, core]), pairs[0]) + dot3(split(v.their_factor[j]), pairs[1])
        w_high, w_low = split(value)
        v.w_high[j] = w_high
        v.w_low[j] = w_low

    def trade(d):
        return copy(v.part.at[d, 1 - core], v.part_in.at[d], v.part_send.at[d], v.part_recv.at[d], sibling)

    def along(i, j, target):
        return copy(
            v.own.at[i], v.chain.at[i, j], v.chain_send.at[i, target], v.chain_recv.at[i, j], (row, 2 * target + core)
        )

    def z_span(at_z, start=0, size=z_rows):
        return pl.ds(pl.multiple_of(at_z * z_rows + start, size), size)

    def z_device(step, to):
        return (RING * plane + (z + step) % RING, 2 * chip + to)

    def seed_beside(i):
        place = v.cols.at[i, core, z_span(z)]
        return copy(v.own.at[i], place, v.seed_send.at[i, 0], v.seed_recv.at[i, core], sibling)

    def seed_across(i):
        place = v.cols.at[i, core, z_span(z)]
        device = (RING * (1 - plane) + z, 2 * chip + plane)
        return copy(v.own.at[i], place, v.seed_send.at[i, 1], v.seed_recv.at[i, core], device)

    def near(i, side, slot):
        place = v.cols.at[i, side, z_span(z)]
        step = (1, RING - 1)[slot - 1]
        return copy(
            place, place, v.near_send.at[i, side, slot - 1], v.col_recv.at[i, slot, side], z_device(step, core)
        )

    def plant(i):
        seed_across(i).start()
        pl.when(core != plane)(lambda: seed_beside(i).start())

        @pl.when(core == plane)
        def _():
            v.cols[i, core, z_span(z)] = v.own[i]

    def relay_near(i):
        for side in range(2):

            @pl.when((core != plane) | (core != side))
            def _():
                place = v.cols.at[i, side, z_span(z)]
                copy(place, place, v.seed_send.at[i, 0], v.seed_recv.at[i, side], sibling).wait_recv()

            for slot in (1, 2):
                near(i, side, slot).start()

    def onward(i, side, slot):
        step, start = ((1, 0), (RING - 1, z_rows // 2))[slot - 1]
        place = v.cols.at[i, side, z_span((z - step) % RING, start, z_rows // 2)]
        return copy(
            place, place, v.col_relay.at[i, side, slot - 1], v.col_recv.at[i, slot + 2, side], z_device(step, core)
        )

    def arrived(i, side, slot):
        rows = z_span(z) if slot < 3 else z_span(z, 0, z_rows // 2)
        place = v.cols.at[i, side, rows]
        return copy(place, place, v.seed_send.at[i, 0], v.col_recv.at[i, slot, side], sibling)

    def chain_step(d):
        i = chip - d

        def term(left, j):
            return dot3(split(left), (v.w_high[j], v.w_low[j]))

        def add(value):
            for side in range(2):
                v.part[d, side] = v.part[d, side] + value[:, side * width : (side + 1) * width]

        value = term(v.starts[i], i)
        for side in range(2):
            v.part[d, side] = value[:, side * width : (side + 1) * width]

        def more(j, carry):
            copy(v.own.at[i], v.chain.at[i, j], v.chain_send.at[i, 0], v.chain_recv.at[i, j], sibling).wait_recv()
            add(term(v.chain[i, j], j))
            return carry

        lax.fori_loop(i + 1, chip, more, 0)
        trade(d).start()
        trade(d).wait_recv()
        v.own[i] = -(v.part[d, core] + v.part_in[d])

        def tell(target, carry):
            along(i, chip, target).start()
            return carry

        lax.fori_loop(chip + 1, CHIPS, tell, 0)
        plant(i)

    def relay_far(i):
        for side in range(2):
            for slot in (1, 2):
                arrived(i, side, slot).wait_recv()
                onward(i, side, slot).start()

    for one in fetch:
        one.wait()
    for side in range(2):
        high, low = split(v.inverse[side])
        v.inverse_high[side] = high
        v.inverse_low[side] = low

    def accumulate(idx):
        i = order(idx)

        @pl.when(i < chip)
        def _():
            for side in range(2):
                for slot in (3, 4):
                    arrived(i, side, slot).wait_recv()
            lefts = split(got[i])
            for side in range(2):
                v.total[side] = v.total[side] + dot3(lefts, split(v.cols[i, side]))

    product(0)
    pl.when(chip == 0)(lead_push)
    give_factor.wait_recv()

    def couple_one(j, carry):
        couple(j)
        return carry

    lax.fori_loop(0, chip, couple_one, 0)
    lefts = split(got[chip])
    for side in range(2):
        span = slice(side * width, (side + 1) * width)
        v.total[side] = dot3(lefts, (v.inverse_high[core, :, span], v.inverse_low[core, :, span]))

    def one_solved(idx, carry):
        accumulate(idx)
        return carry

    def by_stage(stage, table):
        first, last = 0, 0
        for key, (low, high) in table.items():
            first = jnp.where(stage == key, low, first)
            last = jnp.where(stage == key, high, last)
        return first, last

    def body(stage, carry):
        @pl.when(stage == 1)
        def _():
            for one in own_sends[:2]:
                one.wait_recv()
            for one in half_sends:
                one.start()

        @pl.when(stage == 2)
        def _():
            for one in half_sends:
                one.wait_recv()
            for one in far_sends:
                one.start()

        pl.when(chip > stage)(lambda: chain_step(stage + 1))

        @pl.when(stage == 1)
        def _():
            own_sends[2].wait_recv()

        for k in range(3):

            @pl.when(stage == k + 1)
            def _():
                for one in partner_sends[k]:
                    one.start()

        @pl.when(stage == 4)
        def _():
            for one in sum(partner_sends, far_sends):
                one.wait_recv()

        def one_product(idx, carry):
            product(idx)
            return carry

        def one_pass(idx, carry):
            add_and_pass(idx)
            return carry

        def one_part(step, carry):
            pl.when(step == 0)(lead_wait)
            factor_part(v.work, v.grid, v.inverted, v.below, step // 3, step % 3)
            return carry

        lax.fori_loop(*by_stage(stage, {1: (1, 4), 2: (4, 5), 4: (5, 8)}), one_product, 0)
        pl.when((stage > 0) & (chip >= stage))(lambda: relay_near(chip - stage))
        pl.when((stage > 1) & (chip >= stage - 1))(lambda: relay_far(chip - stage + 1))
        lax.fori_loop(*by_stage(stage, {2: (0, 4), 3: (4, 5), 5: (5, 8)}), one_pass, 0)

        @pl.when(chip == 0)
        def _():
            pl.when(stage == 1)(lead_sum)
            lax.fori_loop(*by_stage(stage, {2: (0, 2), 3: (2, 5), 4: (5, 9), 5: (9, 12)}), one_part, 0)

        lax.fori_loop(*by_stage(stage, {5: (1, 3), 6: (3, 5)}), one_solved, 0)

        return carry

    lax.fori_loop(0, CHIPS - 1, body, 0)
    pl.when(chip == CHIPS - 1)(lambda: relay_near(0))
    pl.when(chip >= CHIPS - 2)(lambda: relay_far(chip - CHIPS + 2))
    pl.when(chip == CHIPS - 1)(lambda: relay_far(0))
    cross()

    lax.fori_loop(5, CHIPS, one_solved, 0)
    give_total = copy(v.total.at[1 - core], v.total_in, v.total_send, v.total_recv, sibling)
    give_total.start()

    @pl.when(chip == 0)
    def _():
        shape = (2 * width, 2 * width)
        eye = lax.broadcasted_iota(jnp.int32, shape, 0) == lax.broadcasted_iota(jnp.int32, shape, 1)
        v.work[...] = jnp.where(eye, 1.0, 0.0)
        solve_rows(v.work, v.inverted, v.below)

    for c in range(2):
        arrivals(plane, c)
        for part in range(2):
            cross_to(part, c).wait_recv()
            total = plane_sum(plane, part, c) + v.cross_in[part, halves[c]]
            shift = (row * 2 + part - (2 * chip + core)) * width + c * (width // 2)
            there = lax.broadcasted_iota(jnp.int32, total.shape, 0) + shift == lax.broadcasted_iota(
                jnp.int32, total.shape, 1
            )
            rows = pl.ds(part * width + c * (width // 2), width // 2)
            gram_ref[rows] = jnp.where(there, 1.0, 0.0) + scale * total

    share = panel_ref.shape[0]
    other_span = pl.ds(pl.multiple_of((1 - core) * width, width), width)
    swap = copy(gram_ref.at[other_span], v.side, v.side_send, v.side_recv, sibling)

    def hand_out(m):
        return copy(
            v.first.at[pl.ds(m * share, share)], panel_ref, v.row_send.at[m], v.row_recv, (row, CHIPS * core + m)
        )

    @pl.when(chip == 0)
    def _():
        swap.start()
        v.first[:, own_span] = gram_ref[own_span]
        swap.wait_recv()
        v.first[:, other_span] = v.side[...]
        v.first[...] = jnp.dot(
            v.first[...], v.work[...], precision=lax.Precision.HIGHEST, preferred_element_type=jnp.float32
        )
        for m in range(1, CHIPS):
            hand_out(m).start()
        pl.when(core == 1)(lambda: hand_out(0).start())

        @pl.when(core == 0)
        def _():
            panel_ref[...] = v.first[pl.ds(0, share)]

    give_total.wait_recv()
    solved_ref[...] = v.total[core] + v.total_in[...]
    pl.when(col > 0)(lambda: hand_out(0).wait_recv())

    @pl.when(chip == 0)
    def _():
        for step in range(1, n_rows):
            for to in range(2):
                share_to(step, to).wait_send()
        share_to(0, 1 - core).wait_send()
        swap.wait_send()
        for m in range(1, CHIPS):
            hand_out(m).wait_send()
        pl.when(core == 1)(lambda: hand_out(0).wait_send())

    for one in sum(partner_sends, own_sends + half_sends + far_sends):
        one.wait_send()
    give_mine.wait_send()
    give_factor.wait_send()
    give_total.wait_send()

    def drain_push(block, carry):
        pl.when(ahead(block) == 0)(lambda: hand_beside(block).wait_send())
        for c in range(2):
            for side in range(2):
                pl.when(ahead(block) == 2)(lambda: hop_to(block, side, c).wait_send())
                for to in range(2):
                    pl.when(ahead(block) == (1, RING - 1)[side])(lambda: away(block, side, to, c).wait_send())
        return carry

    for part in range(2):
        for c in range(2):
            cross_to(part, c).wait_send()
    lax.fori_loop(0, CHIPS, drain_push, 0)

    def drain_chain(i, carry):
        trade(chip - i).wait_send()

        def told(target, carry):
            along(i, chip, target).wait_send()
            return carry

        lax.fori_loop(chip + 1, CHIPS, told, 0)
        seed_across(i).wait_send()
        pl.when(core != plane)(lambda: seed_beside(i).wait_send())
        for side in range(2):
            for slot in (1, 2):
                near(i, side, slot).wait_send()
                onward(i, side, slot).wait_send()
        return carry

    lax.fori_loop(0, chip, drain_chain, 0)


def finish_kernel(*refs):
    for source, target in zip(refs[:3], refs[3:]):
        target[...] = source[...]


def finish(values):
    vmem = pl.BlockSpec(memory_space=pltpu.VMEM)
    return pl.pallas_call(
        finish_kernel,
        out_shape=tuple(jax.ShapeDtypeStruct(a.shape, a.dtype) for a in values),
        in_specs=[vmem] * 3,
        out_specs=(vmem,) * 3,
    )(*values)


def on_device(iterate, factor, inverses):
    n, width = iterate.shape
    n_rows = lax.axis_size("row")
    n_cols = lax.axis_size("col")
    vmem = pl.BlockSpec(memory_space=pltpu.VMEM)
    scratch = scratch_shapes(n, width, n_rows)
    values = pl.pallas_call(
        functools.partial(fused_kernel, tuple(scratch)),
        out_shape=(
            jax.ShapeDtypeStruct((2 * width, width), jnp.float32),
            jax.ShapeDtypeStruct((2 * width // n_cols, 2 * width), jnp.float32),
            jax.ShapeDtypeStruct((n, width), jnp.float32),
        ),
        in_specs=[vmem, vmem, pl.BlockSpec(memory_space=pl.ANY)],
        out_specs=(vmem, vmem, vmem),
        scratch_shapes=list(scratch.values()),
        compiler_params=pltpu.CompilerParams(
            collective_id=0, has_side_effects=True, vmem_limit_bytes=60 << 20
        ),
        cost_estimate=pl.CostEstimate(flops=10**10, bytes_accessed=2 * 10**7, transcendentals=0),
    )(iterate, factor.reshape(CHIPS, 2, width, width), inverses.reshape(CHIPS, 2, width, 2 * width))
    return finish(values)


def solution(mesh):
    placed = (P("row", "col"), P(None, "col"), P())
    return jax.shard_map(
        on_device,
        mesh=mesh,
        in_specs=placed,
        out_specs=(P("row", "col"), P(("row", "col"), None), P("row", "col")),
        check_vma=False,
    )
```

```python
import functools
import types

import jax
import jax.numpy as jnp
from jax import lax
from jax.experimental import pallas as pl
from jax.experimental.pallas import tpu as pltpu
from jax.sharding import PartitionSpec as P

CHIPS = 8
RING = 4
MESH = pl.DeviceIdType.MESH


def split(value):
    high = value.astype(jnp.bfloat16)
    return high, (value - high.astype(jnp.float32)).astype(jnp.bfloat16)


def dot3(left, right):
    dot = functools.partial(jnp.dot, preferred_element_type=jnp.float32)
    return dot(left[0], right[0]) + (dot(left[0], right[1]) + dot(left[1], right[0]))


def dot3_turned(left, right):
    dot = functools.partial(
        lax.dot_general, dimension_numbers=(((0,), (0,)), ((), ())), preferred_element_type=jnp.float32
    )
    return dot(left[0], right[0]) + (dot(left[0], right[1]) + dot(left[1], right[0]))


def dot_exact_turned(left, right):
    return lax.dot_general(
        left, right, (((1,), (1,)), ((), ())), precision=lax.Precision.HIGHEST, preferred_element_type=jnp.float32
    )


def factor_block(grid, first, last):
    base = grid.shape[0]
    for p in range(first, last):
        rows = slice(8 * p, 8 * p + 8)
        panel = grid[rows]
        sub = lax.broadcasted_iota(jnp.int32, panel.shape, 0)
        columns = [jnp.broadcast_to(panel[:, 8 * p + c : 8 * p + c + 1], panel.shape) for c in range(8)]
        scales = jnp.ones_like(panel)
        for j in range(8):
            pivot = jnp.broadcast_to(columns[j][j : j + 1], panel.shape)
            below = jnp.where(sub > j, columns[j], 0.0) / pivot
            scales = jnp.where(sub == j, pivot, scales)
            for c in range(j + 1, 8):
                columns[c] = columns[c] - below * columns[c][j : j + 1]
            panel = panel - below * panel[j : j + 1]
        panel = panel / jnp.sqrt(scales)
        grid[rows] = panel
        if 8 * p + 8 < base:
            rest = slice(8 * p + 8, base)
            turned = panel[:, :base].T[8 * p + 8 :]
            value = grid[rest]
            for j in range(8):
                value = value - turned[:, j : j + 1] * panel[j : j + 1]
            grid[rest] = value


def factor_part(work, grid, inverted, below, s, part):
    base = grid.shape[0]
    span = pl.ds(pl.multiple_of(s * base, base), base)
    panels = base // 8

    @pl.when(part == 0)
    def _():
        shape = (base, base)
        eye = lax.broadcasted_iota(jnp.int32, shape, 0) == lax.broadcasted_iota(jnp.int32, shape, 1)
        grid[:, :base] = work[span, span]
        grid[:, base:] = jnp.where(eye, 1.0, 0.0)
        factor_block(grid, 0, panels * 2 // 5)

    pl.when(part == 1)(lambda: factor_block(grid, panels * 2 // 5, panels))

    @pl.when(part == 2)
    def _():
        inverted[s] = grid[:, base:]

        @pl.when((s + 1) * base == work.shape[0])
        def _():
            below[s] = jnp.zeros(below.shape[1:], jnp.float32)

        @pl.when((s + 1) * base < work.shape[0])
        def _():
            done = dot_exact_turned(work[:, span], grid[:, base:])
            later = lax.broadcasted_iota(jnp.int32, done.shape, 0) >= (s + 1) * base
            done = jnp.where(later, done, 0.0)
            below[s] = done
            work[...] = work[...] - dot_exact_turned(done, done)


def solve_rows(rows_ref, inverted, below):
    blocks, base, _ = inverted.shape

    def step(s, carry):
        span = pl.ds(pl.multiple_of(s * base, base), base)
        done = dot_exact_turned(rows_ref[:, span], inverted[s])
        rows_ref[...] = rows_ref[...] - dot_exact_turned(done, below[s])
        rows_ref[:, span] = done
        return carry

    lax.fori_loop(0, blocks, step, 0)


def scratch_shapes(n, width, n_rows):
    f32, bf16 = jnp.float32, jnp.bfloat16
    vmem, dma = pltpu.VMEM, pltpu.SemaphoreType.DMA
    z_rows = width // RING
    return dict(
        theirs=vmem((n, width), f32),
        got=vmem((CHIPS, n, width), f32),
        high=vmem((2, n, width), bf16),
        low=vmem((2, n, width), bf16),
        prod=vmem((CHIPS, 2, width, width), f32),
        hop=vmem((CHIPS, width, width), f32),
        land=vmem((2, 2, 2, width, width), f32),
        beside=vmem((2, width, width), f32),
        cross=vmem((2, width, width), f32),
        cross_in=vmem((2, width, width), f32),
        slices=vmem((n_rows, 2, width // n_rows, width), f32),
        work=vmem((2 * width, 2 * width), f32),
        grid=vmem((width // 2, width), f32),
        inverted=vmem((4, width // 2, width // 2), f32),
        below=vmem((4, 2 * width, width // 2), f32),
        lead_in=vmem((2 * width, 2 * width), f32),
        first=vmem((width, 2 * width), f32),
        side=vmem((width, width), f32),
        my_factor=vmem((CHIPS, width, width), f32),
        their_factor=vmem((CHIPS, width, width), f32),
        inverse=vmem((2, width, 2 * width), f32),
        inverse_high=vmem((2, width, 2 * width), bf16),
        inverse_low=vmem((2, width, 2 * width), bf16),
        starts=vmem((CHIPS, z_rows, width), f32),
        w_high=vmem((CHIPS - 1, width, 2 * width), bf16),
        w_low=vmem((CHIPS - 1, width, 2 * width), bf16),
        chain=vmem((CHIPS - 1, CHIPS - 1, z_rows, width), f32),
        part=vmem((CHIPS, 2, z_rows, width), f32),
        part_in=vmem((CHIPS, z_rows, width), f32),
        own=vmem((CHIPS - 1, z_rows, width), f32),
        cols=vmem((CHIPS - 1, 2, width, width), f32),
        total=vmem((2, n, width), f32),
        total_in=vmem((n, width), f32),
        send=dma((13,)),
        recv=dma((13,)),
        theirs_send=dma,
        theirs_recv=dma,
        push=dma((CHIPS, 2, 2)),
        hop_send=dma((CHIPS, 2, 2)),
        hop_recv=dma((CHIPS, 2)),
        landed=dma((2, 2, 2, 2)),
        beside_recv=dma((2,)),
        cross_send=dma((2, 2)),
        cross_recv=dma((2, 2)),
        cut=dma((n_rows,)),
        cut_in=dma((n_rows,)),
        share=dma((n_rows, 2)),
        shared=dma((n_rows, 2)),
        local=dma((4,)),
        factor_send=dma,
        factor_recv=dma,
        part_send=dma((CHIPS,)),
        part_recv=dma((CHIPS,)),
        chain_send=dma((CHIPS, CHIPS)),
        chain_recv=dma((CHIPS, CHIPS)),
        seed_send=dma((CHIPS, 2)),
        seed_recv=dma((CHIPS, 2)),
        near_send=dma((CHIPS, 2, 2)),
        col_relay=dma((CHIPS, 2, 2)),
        col_recv=dma((CHIPS, 5, 2)),
        total_send=dma,
        total_recv=dma,
        side_send=dma,
        side_recv=dma,
        row_send=dma((CHIPS,)),
        row_recv=dma,
    )


def fused_kernel(names, mine_ref, factor_ref, inverses_ref, gram_ref, panel_ref, solved_ref, *scratch):
    v = types.SimpleNamespace(**dict(zip(names, scratch)))
    row = lax.axis_index("row")
    col = lax.axis_index("col")
    n_rows = lax.axis_size("row")
    n_cols = lax.axis_size("col")
    chip = col // 2
    core = col % 2
    x, y = chip % 4, chip // 4
    z, plane = row % RING, row // RING
    n, width = mine_ref.shape
    piece = width // n_rows
    z_rows = width // RING
    scale = 3.0 / (n * n_rows)
    sibling = (row, 2 * chip + 1 - core)

    barrier = pltpu.get_barrier_semaphore()
    for step in range(1, n_cols):
        pl.semaphore_signal(barrier, inc=1, device_id=(row, (col + step) % n_cols), device_id_type=MESH)
    for step in range(1, n_rows):
        for other in range(2):
            pl.semaphore_signal(
                barrier, inc=1, device_id=((row + step) % n_rows, 2 * chip + other), device_id_type=MESH
            )
    pl.semaphore_wait(barrier, n_cols - 1 + 2 * (n_rows - 1))

    def copy(source, target, out, arrival, device):
        return pltpu.make_async_remote_copy(
            src_ref=source, dst_ref=target, send_sem=out, recv_sem=arrival, device_id=device, device_id_type=MESH
        )

    def at(dx, dy):
        return 4 * ((y + dy) % 2) + (x + dx) % 4

    left, right, partner, far = at(3, 0), at(1, 0), at(0, 1), at(2, 0)
    at_right, at_left = (row, 2 * right + core), (row, 2 * left + core)
    at_partner = (row, 2 * partner + core)
    got = v.got
    top, low_half = pl.ds(0, n // 2), pl.ds(n // 2, n // 2)

    def block_copy(block, span, k, device, source=None):
        place = got.at[block] if span is None else got.at[block, span]
        return copy(place if source is None else source, place, v.send.at[k], v.recv.at[k], device)

    own_sends = [
        block_copy(chip, None, 0, at_right, mine_ref),
        block_copy(chip, None, 1, at_left, mine_ref),
        block_copy(chip, None, 2, at_partner, mine_ref),
    ]
    half_sends = [block_copy(left, top, 3, at_right), block_copy(right, low_half, 4, at_left)]
    thirds = [pl.ds(0, n * 3 // 8), pl.ds(n * 3 // 8, n * 3 // 8), pl.ds(n * 3 // 4, n // 4)]
    partner_sends = [
        [block_copy(partner, span, 5 + k, at_right), block_copy(partner, span, 8 + k, at_left)]
        for k, span in enumerate(thirds)
    ]
    far_sends = [block_copy(far, top, 11, at_partner), block_copy(far, low_half, 12, at_partner)]

    give_mine = copy(mine_ref, v.theirs, v.theirs_send, v.theirs_recv, sibling)
    give_factor = copy(factor_ref.at[:, 1 - core], v.their_factor, v.factor_send, v.factor_recv, sibling)
    own_span = pl.ds(pl.multiple_of(core * width, width), width)
    fetch = [
        pltpu.make_async_copy(factor_ref.at[:, core], v.my_factor, v.local.at[3]),
        pltpu.make_async_copy(inverses_ref.at[chip, 0], v.inverse.at[0], v.local.at[0]),
        pltpu.make_async_copy(inverses_ref.at[chip, 1], v.inverse.at[1], v.local.at[1]),
        pltpu.make_async_copy(
            inverses_ref.at[:, plane, pl.ds(pl.multiple_of(z * z_rows, z_rows), z_rows), own_span], v.starts, v.local.at[2]
        ),
    ]
    give_mine.start()
    own_sends[0].start()
    own_sends[1].start()
    own_sends[2].start()
    give_factor.start()
    for one in fetch:
        one.start()
    got[chip] = mine_ref[...]
    own_high, own_low = split(mine_ref[...])
    v.high[core] = own_high
    v.low[core] = own_low
    give_mine.wait_recv()
    their_high, their_low = split(v.theirs[...])
    v.high[1 - core] = their_high
    v.low[1 - core] = their_low

    def order(idx):
        dx = jnp.where(
            (idx == 1) | (idx == 5), 3, jnp.where((idx == 2) | (idx == 6), 1, jnp.where((idx == 4) | (idx == 7), 2, 0))
        )
        dy = jnp.where((idx == 3) | (idx > 4), 1, 0)
        return at(dx, dy)

    def ahead(block):
        return (block % RING - z + RING) % RING

    def z_peer(step, to):
        return (RING * plane + (z + step) % RING, 2 * chip + to)

    halves = [pl.ds(0, width // 2), pl.ds(width // 2, width // 2)]

    def hop_to(block, side, c):
        step = (1, RING - 1)[side]
        return copy(
            v.prod.at[block, side, halves[c]],
            v.hop.at[block, halves[c]],
            v.hop_send.at[block, side, c],
            v.hop_recv.at[block, c],
            z_peer(step, core),
        )

    def away(block, side, to, c):
        step = (1, RING - 1)[side]
        return copy(
            v.prod.at[block, to, halves[c]],
            v.land.at[side, block // RING, core, halves[c]],
            v.push.at[block, to, c],
            v.landed.at[side, block // RING, core, c],
            z_peer(step, to),
        )

    def hand_beside(block):
        return copy(
            v.prod.at[block, 1 - core],
            v.beside.at[block // RING],
            v.push.at[block, 1 - core, 0],
            v.beside_recv.at[block // RING],
            sibling,
        )

    def product(idx):
        block = order(idx)
        lefts = split(got[block])
        for to in range(2):
            v.prod[block, to] = dot3_turned(lefts, (v.high[to], v.low[to]))
        pl.when(ahead(block) == 0)(lambda: hand_beside(block).start())

        @pl.when(ahead(block) == 2)
        def _():
            for c in range(2):
                for side in range(2):
                    hop_to(block, side, c).start()

        for side in range(2):

            @pl.when(ahead(block) == (1, RING - 1)[side])
            def _():
                for c in range(2):
                    away(block, side, 1 - side, c).start()

    def add_and_pass(idx):
        block = order(idx)
        for side in range(2):

            @pl.when(ahead(block) == (1, RING - 1)[side])
            def _():
                for c in range(2):
                    rows = halves[c]
                    hop_to(block, side, c).wait_recv()
                    v.prod[block, side, rows] = v.prod[block, side, rows] + v.hop[block, rows]
                    away(block, side, side, c).start()

    def plane_sum(to_plane, part, c):
        rows = halves[c]
        total = v.land[0, to_plane, part, rows] + v.land[1, to_plane, part, rows]
        mine = jnp.where(core == part, 1, 0)
        return total + jnp.where(mine == 1, v.prod[RING * to_plane + z, core, rows], v.beside[to_plane, rows])

    def cross_to(part, c):
        return copy(
            v.cross.at[part, halves[c]],
            v.cross_in.at[part, halves[c]],
            v.cross_send.at[part, c],
            v.cross_recv.at[part, c],
            (RING * (1 - plane) + z, col),
        )

    def arrivals(to_plane, c):
        if c == 0:
            copy(v.cross.at[0], v.beside.at[0], v.push.at[0, 0, 0], v.beside_recv.at[to_plane], sibling).wait_recv()
        for part in range(2):
            for side in range(2):
                copy(
                    v.cross.at[0, halves[0]],
                    v.cross_in.at[0, halves[0]],
                    v.push.at[0, 0, 0],
                    v.landed.at[side, to_plane, part, c],
                    sibling,
                ).wait_recv()

    def cross():
        for c in range(2):
            arrivals(1 - plane, c)
            for part in range(2):
                v.cross[part, halves[c]] = plane_sum(1 - plane, part, c)
                cross_to(part, c).start()

    def slice_to(other):
        return copy(
            v.prod.at[0, :, pl.ds(pl.multiple_of(other * piece, piece), piece)],
            v.slices.at[row],
            v.cut.at[other],
            v.cut_in.at[row],
            (other, core),
        )

    def lead_rows(at_row, at_core):
        return v.lead_in.at[pl.ds(pl.multiple_of(at_core * width + at_row * piece, piece), piece)]

    def share_to(step, to):
        rows = lead_rows(row, core)
        return copy(rows, rows, v.share.at[step, to], v.shared.at[row, core], ((row + step) % n_rows, to))

    def lead_push():
        for step in range(1, n_rows):
            slice_to((row + step) % n_rows).start()
        v.slices[row] = v.prod[0, :, pl.ds(pl.multiple_of(row * piece, piece), piece)]

    def lead_sum():
        for step in range(1, n_rows):
            source = (row + step) % n_rows
            copy(
                v.slices.at[row], v.slices.at[source], v.cut.at[source], v.cut_in.at[source], (source, core)
            ).wait_recv()
            slice_to(source).wait_send()
        total = v.slices[0]
        for other in range(1, n_rows):
            total = total + v.slices[other]
        whole = scale * jnp.concatenate([total[0], total[1]], axis=1)
        first = core * width + row * piece
        shape = (piece, 2 * width)
        there = lax.broadcasted_iota(jnp.int32, shape, 0) + first == lax.broadcasted_iota(jnp.int32, shape, 1)
        lead_rows(row, core)[...] = whole + jnp.where(there, 1.0, 0.0)
        for step in range(1, n_rows):
            for to in range(2):
                share_to(step, to).start()
        share_to(0, 1 - core).start()

    def lead_wait():
        for step in range(n_rows):
            for other in range(2):
                source = (row + step) % n_rows

                @pl.when((step > 0) | (core != other))
                def _():
                    rows = lead_rows(source, other)
                    copy(rows, rows, v.share.at[0, 0], v.shared.at[source, other], (source, 0)).wait_recv()

        v.work[...] = v.lead_in[...]

    def couple(j):
        pairs = [(v.inverse_high[side], v.inverse_low[side]) for side in (core, 1 - core)]
        value = dot3(split(v.my_factor[j]), pairs[0]) + dot3(split(v.their_factor[j]), pairs[1])
        w_high, w_low = split(value)
        v.w_high[j] = w_high
        v.w_low[j] = w_low

    def trade(d):
        return copy(v.part.at[d, 1 - core], v.part_in.at[d], v.part_send.at[d], v.part_recv.at[d], sibling)

    def along(i, j, target):
        return copy(
            v.own.at[i], v.chain.at[i, j], v.chain_send.at[i, target], v.chain_recv.at[i, j], (row, 2 * target + core)
        )

    def z_span(at_z, start=0, size=z_rows):
        return pl.ds(pl.multiple_of(at_z * z_rows + start, size), size)

    def z_device(step, to):
        return (RING * plane + (z + step) % RING, 2 * chip + to)

    def seed_beside(i):
        place = v.cols.at[i, core, z_span(z)]
        return copy(v.own.at[i], place, v.seed_send.at[i, 0], v.seed_recv.at[i, core], sibling)

    def seed_across(i):
        place = v.cols.at[i, core, z_span(z)]
        device = (RING * (1 - plane) + z, 2 * chip + plane)
        return copy(v.own.at[i], place, v.seed_send.at[i, 1], v.seed_recv.at[i, core], device)

    def near(i, side, slot):
        place = v.cols.at[i, side, z_span(z)]
        step = (1, RING - 1)[slot - 1]
        return copy(
            place, place, v.near_send.at[i, side, slot - 1], v.col_recv.at[i, slot, side], z_device(step, core)
        )

    def plant(i):
        seed_across(i).start()
        pl.when(core != plane)(lambda: seed_beside(i).start())

        @pl.when(core == plane)
        def _():
            v.cols[i, core, z_span(z)] = v.own[i]

    def relay_near(i):
        for side in range(2):

            @pl.when((core != plane) | (core != side))
            def _():
                place = v.cols.at[i, side, z_span(z)]
                copy(place, place, v.seed_send.at[i, 0], v.seed_recv.at[i, side], sibling).wait_recv()

            for slot in (1, 2):
                near(i, side, slot).start()

    def onward(i, side, slot):
        step, start = ((1, 0), (RING - 1, z_rows // 2))[slot - 1]
        place = v.cols.at[i, side, z_span((z - step) % RING, start, z_rows // 2)]
        return copy(
            place, place, v.col_relay.at[i, side, slot - 1], v.col_recv.at[i, slot + 2, side], z_device(step, core)
        )

    def arrived(i, side, slot):
        rows = z_span(z) if slot < 3 else z_span(z, 0, z_rows // 2)
        place = v.cols.at[i, side, rows]
        return copy(place, place, v.seed_send.at[i, 0], v.col_recv.at[i, slot, side], sibling)

    def chain_step(d):
        i = chip - d

        def term(left, j):
            return dot3(split(left), (v.w_high[j], v.w_low[j]))

        def add(value):
            for side in range(2):
                v.part[d, side] = v.part[d, side] + value[:, side * width : (side + 1) * width]

        value = term(v.starts[i], i)
        for side in range(2):
            v.part[d, side] = value[:, side * width : (side + 1) * width]

        def more(j, carry):
            copy(v.own.at[i], v.chain.at[i, j], v.chain_send.at[i, 0], v.chain_recv.at[i, j], sibling).wait_recv()
            add(term(v.chain[i, j], j))
            return carry

        lax.fori_loop(i + 1, chip, more, 0)
        trade(d).start()
        trade(d).wait_recv()
        v.own[i] = -(v.part[d, core] + v.part_in[d])

        def tell(target, carry):
            along(i, chip, target).start()
            return carry

        lax.fori_loop(chip + 1, CHIPS, tell, 0)
        plant(i)

    def relay_far(i):
        for side in range(2):
            for slot in (1, 2):
                arrived(i, side, slot).wait_recv()
                onward(i, side, slot).start()

    for one in fetch:
        one.wait()
    for side in range(2):
        high, low = split(v.inverse[side])
        v.inverse_high[side] = high
        v.inverse_low[side] = low

    def accumulate(idx):
        i = order(idx)

        @pl.when(i < chip)
        def _():
            for side in range(2):
                for slot in (3, 4):
                    arrived(i, side, slot).wait_recv()
            lefts = split(got[i])
            for side in range(2):
                v.total[side] = v.total[side] + dot3(lefts, split(v.cols[i, side]))

    product(0)
    pl.when(chip == 0)(lead_push)
    give_factor.wait_recv()

    def couple_one(j, carry):
        couple(j)
        return carry

    lax.fori_loop(0, chip, couple_one, 0)
    lefts = split(got[chip])
    for side in range(2):
        span = slice(side * width, (side + 1) * width)
        v.total[side] = dot3(lefts, (v.inverse_high[core, :, span], v.inverse_low[core, :, span]))

    def one_solved(idx, carry):
        accumulate(idx)
        return carry

    def by_stage(stage, table):
        first, last = 0, 0
        for key, (low, high) in table.items():
            first = jnp.where(stage == key, low, first)
            last = jnp.where(stage == key, high, last)
        return first, last

    def body(stage, carry):
        @pl.when(stage == 1)
        def _():
            for one in own_sends[:2]:
                one.wait_recv()
            for one in half_sends:
                one.start()

        @pl.when(stage == 2)
        def _():
            for one in half_sends:
                one.wait_recv()
            for one in far_sends:
                one.start()

        pl.when(chip > stage)(lambda: chain_step(stage + 1))

        @pl.when(stage == 1)
        def _():
            own_sends[2].wait_recv()

        for k in range(3):

            @pl.when(stage == k + 1)
            def _():
                for one in partner_sends[k]:
                    one.start()

        @pl.when(stage == 4)
        def _():
            for one in sum(partner_sends, far_sends):
                one.wait_recv()

        def one_product(idx, carry):
            product(idx)
            return carry

        def one_pass(idx, carry):
            add_and_pass(idx)
            return carry

        def one_part(step, carry):
            pl.when(step == 0)(lead_wait)
            factor_part(v.work, v.grid, v.inverted, v.below, step // 3, step % 3)
            return carry

        lax.fori_loop(*by_stage(stage, {1: (1, 4), 2: (4, 5), 4: (5, 8)}), one_product, 0)
        pl.when((stage > 0) & (chip >= stage))(lambda: relay_near(chip - stage))
        pl.when((stage > 1) & (chip >= stage - 1))(lambda: relay_far(chip - stage + 1))
        lax.fori_loop(*by_stage(stage, {2: (0, 4), 3: (4, 5), 5: (5, 8)}), one_pass, 0)

        @pl.when(chip == 0)
        def _():
            pl.when(stage == 1)(lead_sum)
            lax.fori_loop(*by_stage(stage, {2: (0, 2), 3: (2, 5), 4: (5, 9), 5: (9, 12)}), one_part, 0)

        lax.fori_loop(*by_stage(stage, {5: (1, 3), 6: (3, 5)}), one_solved, 0)

        return carry

    lax.fori_loop(0, CHIPS - 1, body, 0)
    pl.when(chip == CHIPS - 1)(lambda: relay_near(0))
    pl.when(chip >= CHIPS - 2)(lambda: relay_far(chip - CHIPS + 2))
    pl.when(chip == CHIPS - 1)(lambda: relay_far(0))
    cross()

    lax.fori_loop(5, CHIPS, one_solved, 0)
    give_total = copy(v.total.at[1 - core], v.total_in, v.total_send, v.total_recv, sibling)
    give_total.start()

    @pl.when(chip == 0)
    def _():
        shape = (2 * width, 2 * width)
        eye = lax.broadcasted_iota(jnp.int32, shape, 0) == lax.broadcasted_iota(jnp.int32, shape, 1)
        v.work[...] = jnp.where(eye, 1.0, 0.0)
        solve_rows(v.work, v.inverted, v.below)

    for c in range(2):
        arrivals(plane, c)
        for part in range(2):
            cross_to(part, c).wait_recv()
            total = plane_sum(plane, part, c) + v.cross_in[part, halves[c]]
            shift = (row * 2 + part - (2 * chip + core)) * width + c * (width // 2)
            there = lax.broadcasted_iota(jnp.int32, total.shape, 0) + shift == lax.broadcasted_iota(
                jnp.int32, total.shape, 1
            )
            rows = pl.ds(part * width + c * (width // 2), width // 2)
            gram_ref[rows] = jnp.where(there, 1.0, 0.0) + scale * total

    share = panel_ref.shape[0]
    other_span = pl.ds(pl.multiple_of((1 - core) * width, width), width)
    swap = copy(gram_ref.at[other_span], v.side, v.side_send, v.side_recv, sibling)

    def hand_out(m):
        return copy(
            v.first.at[pl.ds(m * share, share)], panel_ref, v.row_send.at[m], v.row_recv, (row, CHIPS * core + m)
        )

    @pl.when(chip == 0)
    def _():
        swap.start()
        v.first[:, own_span] = gram_ref[own_span]
        swap.wait_recv()
        v.first[:, other_span] = v.side[...]
        v.first[...] = jnp.dot(
            v.first[...], v.work[...], precision=lax.Precision.HIGHEST, preferred_element_type=jnp.float32
        )
        for m in range(1, CHIPS):
            hand_out(m).start()
        pl.when(core == 1)(lambda: hand_out(0).start())

        @pl.when(core == 0)
        def _():
            panel_ref[...] = v.first[pl.ds(0, share)]

    give_total.wait_recv()
    solved_ref[...] = v.total[core] + v.total_in[...]
    pl.when(col > 0)(lambda: hand_out(0).wait_recv())

    @pl.when(chip == 0)
    def _():
        for step in range(1, n_rows):
            for to in range(2):
                share_to(step, to).wait_send()
        share_to(0, 1 - core).wait_send()
        swap.wait_send()
        for m in range(1, CHIPS):
            hand_out(m).wait_send()
        pl.when(core == 1)(lambda: hand_out(0).wait_send())

    for one in sum(partner_sends, own_sends + half_sends + far_sends):
        one.wait_send()
    give_mine.wait_send()
    give_factor.wait_send()
    give_total.wait_send()

    def drain_push(block, carry):
        pl.when(ahead(block) == 0)(lambda: hand_beside(block).wait_send())
        for c in range(2):
            for side in range(2):
                pl.when(ahead(block) == 2)(lambda: hop_to(block, side, c).wait_send())
                for to in range(2):
                    pl.when(ahead(block) == (1, RING - 1)[side])(lambda: away(block, side, to, c).wait_send())
        return carry

    for part in range(2):
        for c in range(2):
            cross_to(part, c).wait_send()
    lax.fori_loop(0, CHIPS, drain_push, 0)

    def drain_chain(i, carry):
        trade(chip - i).wait_send()

        def told(target, carry):
            along(i, chip, target).wait_send()
            return carry

        lax.fori_loop(chip + 1, CHIPS, told, 0)
        seed_across(i).wait_send()
        pl.when(core != plane)(lambda: seed_beside(i).wait_send())
        for side in range(2):
            for slot in (1, 2):
                near(i, side, slot).wait_send()
                onward(i, side, slot).wait_send()
        return carry

    lax.fori_loop(0, chip, drain_chain, 0)


def finish_kernel(*refs):
    for source, target in zip(refs[:3], refs[3:]):
        target[...] = source[...]


def finish(values):
    vmem = pl.BlockSpec(memory_space=pltpu.VMEM)
    return pl.pallas_call(
        finish_kernel,
        out_shape=tuple(jax.ShapeDtypeStruct(a.shape, a.dtype) for a in values),
        in_specs=[vmem] * 3,
        out_specs=(vmem,) * 3,
    )(*values)


def on_device(iterate, factor, inverses):
    n, width = iterate.shape
    n_rows = lax.axis_size("row")
    n_cols = lax.axis_size("col")
    vmem = pl.BlockSpec(memory_space=pltpu.VMEM)
    scratch = scratch_shapes(n, width, n_rows)
    values = pl.pallas_call(
        functools.partial(fused_kernel, tuple(scratch)),
        out_shape=(
            jax.ShapeDtypeStruct((2 * width, width), jnp.float32),
            jax.ShapeDtypeStruct((2 * width // n_cols, 2 * width), jnp.float32),
            jax.ShapeDtypeStruct((n, width), jnp.float32),
        ),
        in_specs=[vmem, pl.BlockSpec(memory_space=pl.ANY), pl.BlockSpec(memory_space=pl.ANY)],
        out_specs=(vmem, vmem, vmem),
        scratch_shapes=list(scratch.values()),
        compiler_params=pltpu.CompilerParams(
            collective_id=0, has_side_effects=True, vmem_limit_bytes=60 << 20
        ),
        cost_estimate=pl.CostEstimate(flops=10**10, bytes_accessed=2 * 10**7, transcendentals=0),
    )(iterate, factor.reshape(CHIPS, 2, width, width), inverses.reshape(CHIPS, 2, width, 2 * width))
    return finish(values)


def solution(mesh):
    placed = (P("row", "col"), P(None, "col"), P())
    return jax.shard_map(
        on_device,
        mesh=mesh,
        in_specs=placed,
        out_specs=(P("row", "col"), P(("row", "col"), None), P("row", "col")),
        check_vma=False,
    )
```

```python
import functools
import types

import jax
import jax.numpy as jnp
from jax import lax
from jax.experimental import pallas as pl
from jax.experimental.pallas import tpu as pltpu
from jax.sharding import PartitionSpec as P

CHIPS = 8
RING = 4
MESH = pl.DeviceIdType.MESH


def split(value):
    high = value.astype(jnp.bfloat16)
    return high, (value - high.astype(jnp.float32)).astype(jnp.bfloat16)


def dot3(left, right):
    dot = functools.partial(jnp.dot, preferred_element_type=jnp.float32)
    return dot(left[0], right[0]) + (dot(left[0], right[1]) + dot(left[1], right[0]))


def dot3_turned(left, right):
    dot = functools.partial(
        lax.dot_general, dimension_numbers=(((0,), (0,)), ((), ())), preferred_element_type=jnp.float32
    )
    return dot(left[0], right[0]) + (dot(left[0], right[1]) + dot(left[1], right[0]))


def dot_exact_turned(left, right):
    return lax.dot_general(
        left, right, (((1,), (1,)), ((), ())), precision=lax.Precision.HIGHEST, preferred_element_type=jnp.float32
    )


def factor_block(grid, first, last):
    base = grid.shape[0]
    for p in range(first, last):
        rows = slice(8 * p, 8 * p + 8)
        panel = grid[rows]
        sub = lax.broadcasted_iota(jnp.int32, panel.shape, 0)
        columns = [jnp.broadcast_to(panel[:, 8 * p + c : 8 * p + c + 1], panel.shape) for c in range(8)]
        scales = jnp.ones_like(panel)
        for j in range(8):
            pivot = jnp.broadcast_to(columns[j][j : j + 1], panel.shape)
            below = jnp.where(sub > j, columns[j], 0.0) / pivot
            scales = jnp.where(sub == j, pivot, scales)
            for c in range(j + 1, 8):
                columns[c] = columns[c] - below * columns[c][j : j + 1]
            panel = panel - below * panel[j : j + 1]
        panel = panel / jnp.sqrt(scales)
        grid[rows] = panel
        if 8 * p + 8 < base:
            rest = slice(8 * p + 8, base)
            turned = panel[:, :base].T[8 * p + 8 :]
            value = grid[rest]
            for j in range(8):
                value = value - turned[:, j : j + 1] * panel[j : j + 1]
            grid[rest] = value


def factor_part(work, grid, inverted, below, s, part):
    base = grid.shape[0]
    span = pl.ds(pl.multiple_of(s * base, base), base)
    panels = base // 8

    @pl.when(part == 0)
    def _():
        shape = (base, base)
        eye = lax.broadcasted_iota(jnp.int32, shape, 0) == lax.broadcasted_iota(jnp.int32, shape, 1)
        grid[:, :base] = work[span, span]
        grid[:, base:] = jnp.where(eye, 1.0, 0.0)
        factor_block(grid, 0, panels * 2 // 5)

    pl.when(part == 1)(lambda: factor_block(grid, panels * 2 // 5, panels))

    @pl.when(part == 2)
    def _():
        inverted[s] = grid[:, base:]

        @pl.when((s + 1) * base == work.shape[0])
        def _():
            below[s] = jnp.zeros(below.shape[1:], jnp.float32)

        @pl.when((s + 1) * base < work.shape[0])
        def _():
            done = dot_exact_turned(work[:, span], grid[:, base:])
            later = lax.broadcasted_iota(jnp.int32, done.shape, 0) >= (s + 1) * base
            done = jnp.where(later, done, 0.0)
            below[s] = done
            work[...] = work[...] - dot_exact_turned(done, done)


def solve_rows(rows_ref, inverted, below):
    blocks, base, _ = inverted.shape

    def step(s, carry):
        span = pl.ds(pl.multiple_of(s * base, base), base)
        done = dot_exact_turned(rows_ref[:, span], inverted[s])
        rows_ref[...] = rows_ref[...] - dot_exact_turned(done, below[s])
        rows_ref[:, span] = done
        return carry

    lax.fori_loop(0, blocks, step, 0)


def scratch_shapes(n, width, n_rows):
    f32, bf16 = jnp.float32, jnp.bfloat16
    vmem, dma = pltpu.VMEM, pltpu.SemaphoreType.DMA
    z_rows = width // RING
    return dict(
        theirs=vmem((n, width), f32),
        got=vmem((CHIPS, n, width), f32),
        high=vmem((2, n, width), bf16),
        low=vmem((2, n, width), bf16),
        prod=vmem((CHIPS, 2, width, width), f32),
        hop=vmem((CHIPS, width, width), f32),
        land=vmem((2, 2, 2, width, width), f32),
        beside=vmem((2, width, width), f32),
        cross=vmem((2, width, width), f32),
        cross_in=vmem((2, width, width), f32),
        slices=vmem((n_rows, 2, width // n_rows, width), f32),
        work=vmem((2 * width, 2 * width), f32),
        grid=vmem((width // 2, width), f32),
        inverted=vmem((4, width // 2, width // 2), f32),
        below=vmem((4, 2 * width, width // 2), f32),
        lead_in=vmem((2 * width, 2 * width), f32),
        first=vmem((width, 2 * width), f32),
        side=vmem((width, width), f32),
        my_factor=vmem((CHIPS, width, width), f32),
        their_factor=vmem((CHIPS, width, width), f32),
        inverse=vmem((2, width, 2 * width), f32),
        inverse_high=vmem((2, width, 2 * width), bf16),
        inverse_low=vmem((2, width, 2 * width), bf16),
        starts=vmem((CHIPS, z_rows, width), f32),
        w_high=vmem((CHIPS - 1, width, 2 * width), bf16),
        w_low=vmem((CHIPS - 1, width, 2 * width), bf16),
        chain=vmem((CHIPS - 1, CHIPS - 1, z_rows, width), f32),
        part=vmem((CHIPS, 2, z_rows, width), f32),
        part_in=vmem((CHIPS, z_rows, width), f32),
        own=vmem((CHIPS - 1, z_rows, width), f32),
        cols=vmem((CHIPS - 1, 2, width, width), f32),
        total=vmem((2, n, width), f32),
        total_in=vmem((n, width), f32),
        send=dma((13,)),
        recv=dma((13,)),
        theirs_send=dma,
        theirs_recv=dma,
        push=dma((CHIPS, 2, 2)),
        hop_send=dma((CHIPS, 2, 2)),
        hop_recv=dma((CHIPS, 2)),
        landed=dma((2, 2, 2, 2)),
        beside_recv=dma((2,)),
        cross_send=dma((2, 2)),
        cross_recv=dma((2, 2)),
        cut=dma((n_rows,)),
        cut_in=dma((n_rows,)),
        share=dma((n_rows, 2)),
        shared=dma((n_rows, 2)),
        local=dma((5,)),
        factor_send=dma,
        factor_recv=dma,
        part_send=dma((CHIPS,)),
        part_recv=dma((CHIPS,)),
        chain_send=dma((CHIPS, CHIPS)),
        chain_recv=dma((CHIPS, CHIPS)),
        seed_send=dma((CHIPS, 2)),
        seed_recv=dma((CHIPS, 2)),
        near_send=dma((CHIPS, 2, 2)),
        col_relay=dma((CHIPS, 2, 2)),
        col_recv=dma((CHIPS, 5, 2)),
        total_send=dma,
        total_recv=dma,
        side_send=dma,
        side_recv=dma,
        row_send=dma((CHIPS,)),
        row_recv=dma,
    )


def fused_kernel(names, mine_ref, factor_ref, inverses_ref, gram_ref, panel_ref, solved_ref, *scratch):
    v = types.SimpleNamespace(**dict(zip(names, scratch)))
    row = lax.axis_index("row")
    col = lax.axis_index("col")
    n_rows = lax.axis_size("row")
    n_cols = lax.axis_size("col")
    chip = col // 2
    core = col % 2
    x, y = chip % 4, chip // 4
    z, plane = row % RING, row // RING
    n, width = mine_ref.shape
    piece = width // n_rows
    z_rows = width // RING
    scale = 3.0 / (n * n_rows)
    sibling = (row, 2 * chip + 1 - core)

    barrier = pltpu.get_barrier_semaphore()
    for step in range(1, n_cols):
        pl.semaphore_signal(barrier, inc=1, device_id=(row, (col + step) % n_cols), device_id_type=MESH)
    for step in range(1, n_rows):
        for other in range(2):
            pl.semaphore_signal(
                barrier, inc=1, device_id=((row + step) % n_rows, 2 * chip + other), device_id_type=MESH
            )
    pl.semaphore_wait(barrier, n_cols - 1 + 2 * (n_rows - 1))

    def copy(source, target, out, arrival, device):
        return pltpu.make_async_remote_copy(
            src_ref=source, dst_ref=target, send_sem=out, recv_sem=arrival, device_id=device, device_id_type=MESH
        )

    def at(dx, dy):
        return 4 * ((y + dy) % 2) + (x + dx) % 4

    left, right, partner, far = at(3, 0), at(1, 0), at(0, 1), at(2, 0)
    at_right, at_left = (row, 2 * right + core), (row, 2 * left + core)
    at_partner = (row, 2 * partner + core)
    got = v.got
    top, low_half = pl.ds(0, n // 2), pl.ds(n // 2, n // 2)

    def block_copy(block, span, k, device, source=None):
        place = got.at[block] if span is None else got.at[block, span]
        return copy(place if source is None else source, place, v.send.at[k], v.recv.at[k], device)

    own_sends = [
        block_copy(chip, None, 0, at_right, mine_ref),
        block_copy(chip, None, 1, at_left, mine_ref),
        block_copy(chip, None, 2, at_partner, mine_ref),
    ]
    half_sends = [block_copy(left, top, 3, at_right), block_copy(right, low_half, 4, at_left)]
    thirds = [pl.ds(0, n * 3 // 8), pl.ds(n * 3 // 8, n * 3 // 8), pl.ds(n * 3 // 4, n // 4)]
    partner_sends = [
        [block_copy(partner, span, 5 + k, at_right), block_copy(partner, span, 8 + k, at_left)]
        for k, span in enumerate(thirds)
    ]
    far_sends = [block_copy(far, top, 11, at_partner), block_copy(far, low_half, 12, at_partner)]

    give_mine = copy(mine_ref, v.theirs, v.theirs_send, v.theirs_recv, sibling)
    give_factor = copy(factor_ref.at[:, 1 - core], v.their_factor, v.factor_send, v.factor_recv, sibling)
    own_span = pl.ds(pl.multiple_of(core * width, width), width)
    fetch = [
        pltpu.make_async_copy(factor_ref.at[:, core], v.my_factor, v.local.at[3]),
        pltpu.make_async_copy(inverses_ref.at[chip, 0], v.inverse.at[0], v.local.at[0]),
        pltpu.make_async_copy(inverses_ref.at[chip, 1], v.inverse.at[1], v.local.at[1]),
        pltpu.make_async_copy(
            inverses_ref.at[:, plane, pl.ds(pl.multiple_of(z * z_rows, z_rows), z_rows), own_span], v.starts, v.local.at[2]
        ),
    ]
    give_mine.start()
    own_sends[0].start()
    own_sends[1].start()
    own_sends[2].start()
    give_factor.start()
    for one in fetch:
        one.start()
    keep = pltpu.make_async_copy(mine_ref, got.at[chip], v.local.at[4])
    keep.start()
    keep.wait()
    own_high, own_low = split(got[chip])
    v.high[core] = own_high
    v.low[core] = own_low
    give_mine.wait_recv()
    their_high, their_low = split(v.theirs[...])
    v.high[1 - core] = their_high
    v.low[1 - core] = their_low

    def order(idx):
        dx = jnp.where(
            (idx == 1) | (idx == 5), 3, jnp.where((idx == 2) | (idx == 6), 1, jnp.where((idx == 4) | (idx == 7), 2, 0))
        )
        dy = jnp.where((idx == 3) | (idx > 4), 1, 0)
        return at(dx, dy)

    def ahead(block):
        return (block % RING - z + RING) % RING

    def z_peer(step, to):
        return (RING * plane + (z + step) % RING, 2 * chip + to)

    halves = [pl.ds(0, width // 2), pl.ds(width // 2, width // 2)]

    def hop_to(block, side, c):
        step = (1, RING - 1)[side]
        return copy(
            v.prod.at[block, side, halves[c]],
            v.hop.at[block, halves[c]],
            v.hop_send.at[block, side, c],
            v.hop_recv.at[block, c],
            z_peer(step, core),
        )

    def away(block, side, to, c):
        step = (1, RING - 1)[side]
        return copy(
            v.prod.at[block, to, halves[c]],
            v.land.at[side, block // RING, core, halves[c]],
            v.push.at[block, to, c],
            v.landed.at[side, block // RING, core, c],
            z_peer(step, to),
        )

    def hand_beside(block):
        return copy(
            v.prod.at[block, 1 - core],
            v.beside.at[block // RING],
            v.push.at[block, 1 - core, 0],
            v.beside_recv.at[block // RING],
            sibling,
        )

    def product(idx):
        block = order(idx)
        lefts = split(got[block])
        for to in range(2):
            v.prod[block, to] = dot3_turned(lefts, (v.high[to], v.low[to]))
        pl.when(ahead(block) == 0)(lambda: hand_beside(block).start())

        @pl.when(ahead(block) == 2)
        def _():
            for c in range(2):
                for side in range(2):
                    hop_to(block, side, c).start()

        for side in range(2):

            @pl.when(ahead(block) == (1, RING - 1)[side])
            def _():
                for c in range(2):
                    away(block, side, 1 - side, c).start()

    def add_and_pass(idx):
        block = order(idx)
        for side in range(2):

            @pl.when(ahead(block) == (1, RING - 1)[side])
            def _():
                for c in range(2):
                    rows = halves[c]
                    hop_to(block, side, c).wait_recv()
                    v.prod[block, side, rows] = v.prod[block, side, rows] + v.hop[block, rows]
                    away(block, side, side, c).start()

    def plane_sum(to_plane, part, c):
        rows = halves[c]
        total = v.land[0, to_plane, part, rows] + v.land[1, to_plane, part, rows]
        mine = jnp.where(core == part, 1, 0)
        return total + jnp.where(mine == 1, v.prod[RING * to_plane + z, core, rows], v.beside[to_plane, rows])

    def cross_to(part, c):
        return copy(
            v.cross.at[part, halves[c]],
            v.cross_in.at[part, halves[c]],
            v.cross_send.at[part, c],
            v.cross_recv.at[part, c],
            (RING * (1 - plane) + z, col),
        )

    def arrivals(to_plane, c):
        if c == 0:
            copy(v.cross.at[0], v.beside.at[0], v.push.at[0, 0, 0], v.beside_recv.at[to_plane], sibling).wait_recv()
        for part in range(2):
            for side in range(2):
                copy(
                    v.cross.at[0, halves[0]],
                    v.cross_in.at[0, halves[0]],
                    v.push.at[0, 0, 0],
                    v.landed.at[side, to_plane, part, c],
                    sibling,
                ).wait_recv()

    def cross():
        for c in range(2):
            arrivals(1 - plane, c)
            for part in range(2):
                v.cross[part, halves[c]] = plane_sum(1 - plane, part, c)
                cross_to(part, c).start()

    def slice_to(other):
        return copy(
            v.prod.at[0, :, pl.ds(pl.multiple_of(other * piece, piece), piece)],
            v.slices.at[row],
            v.cut.at[other],
            v.cut_in.at[row],
            (other, core),
        )

    def lead_rows(at_row, at_core):
        return v.lead_in.at[pl.ds(pl.multiple_of(at_core * width + at_row * piece, piece), piece)]

    def share_to(step, to):
        rows = lead_rows(row, core)
        return copy(rows, rows, v.share.at[step, to], v.shared.at[row, core], ((row + step) % n_rows, to))

    def lead_push():
        for step in range(1, n_rows):
            slice_to((row + step) % n_rows).start()
        v.slices[row] = v.prod[0, :, pl.ds(pl.multiple_of(row * piece, piece), piece)]

    def lead_sum():
        for step in range(1, n_rows):
            source = (row + step) % n_rows
            copy(
                v.slices.at[row], v.slices.at[source], v.cut.at[source], v.cut_in.at[source], (source, core)
            ).wait_recv()
            slice_to(source).wait_send()
        total = v.slices[0]
        for other in range(1, n_rows):
            total = total + v.slices[other]
        whole = scale * jnp.concatenate([total[0], total[1]], axis=1)
        first = core * width + row * piece
        shape = (piece, 2 * width)
        there = lax.broadcasted_iota(jnp.int32, shape, 0) + first == lax.broadcasted_iota(jnp.int32, shape, 1)
        lead_rows(row, core)[...] = whole + jnp.where(there, 1.0, 0.0)
        for step in range(1, n_rows):
            for to in range(2):
                share_to(step, to).start()
        share_to(0, 1 - core).start()

    def lead_wait():
        for step in range(n_rows):
            for other in range(2):
                source = (row + step) % n_rows

                @pl.when((step > 0) | (core != other))
                def _():
                    rows = lead_rows(source, other)
                    copy(rows, rows, v.share.at[0, 0], v.shared.at[source, other], (source, 0)).wait_recv()

        v.work[...] = v.lead_in[...]

    def couple(j):
        pairs = [(v.inverse_high[side], v.inverse_low[side]) for side in (core, 1 - core)]
        value = dot3(split(v.my_factor[j]), pairs[0]) + dot3(split(v.their_factor[j]), pairs[1])
        w_high, w_low = split(value)
        v.w_high[j] = w_high
        v.w_low[j] = w_low

    def trade(d):
        return copy(v.part.at[d, 1 - core], v.part_in.at[d], v.part_send.at[d], v.part_recv.at[d], sibling)

    def along(i, j, target):
        return copy(
            v.own.at[i], v.chain.at[i, j], v.chain_send.at[i, target], v.chain_recv.at[i, j], (row, 2 * target + core)
        )

    def z_span(at_z, start=0, size=z_rows):
        return pl.ds(pl.multiple_of(at_z * z_rows + start, size), size)

    def z_device(step, to):
        return (RING * plane + (z + step) % RING, 2 * chip + to)

    def seed_beside(i):
        place = v.cols.at[i, core, z_span(z)]
        return copy(v.own.at[i], place, v.seed_send.at[i, 0], v.seed_recv.at[i, core], sibling)

    def seed_across(i):
        place = v.cols.at[i, core, z_span(z)]
        device = (RING * (1 - plane) + z, 2 * chip + plane)
        return copy(v.own.at[i], place, v.seed_send.at[i, 1], v.seed_recv.at[i, core], device)

    def near(i, side, slot):
        place = v.cols.at[i, side, z_span(z)]
        step = (1, RING - 1)[slot - 1]
        return copy(
            place, place, v.near_send.at[i, side, slot - 1], v.col_recv.at[i, slot, side], z_device(step, core)
        )

    def plant(i):
        seed_across(i).start()
        pl.when(core != plane)(lambda: seed_beside(i).start())

        @pl.when(core == plane)
        def _():
            v.cols[i, core, z_span(z)] = v.own[i]

    def relay_near(i):
        for side in range(2):

            @pl.when((core != plane) | (core != side))
            def _():
                place = v.cols.at[i, side, z_span(z)]
                copy(place, place, v.seed_send.at[i, 0], v.seed_recv.at[i, side], sibling).wait_recv()

            for slot in (1, 2):
                near(i, side, slot).start()

    def onward(i, side, slot):
        step, start = ((1, 0), (RING - 1, z_rows // 2))[slot - 1]
        place = v.cols.at[i, side, z_span((z - step) % RING, start, z_rows // 2)]
        return copy(
            place, place, v.col_relay.at[i, side, slot - 1], v.col_recv.at[i, slot + 2, side], z_device(step, core)
        )

    def arrived(i, side, slot):
        rows = z_span(z) if slot < 3 else z_span(z, 0, z_rows // 2)
        place = v.cols.at[i, side, rows]
        return copy(place, place, v.seed_send.at[i, 0], v.col_recv.at[i, slot, side], sibling)

    def chain_step(d):
        i = chip - d

        def term(left, j):
            return dot3(split(left), (v.w_high[j], v.w_low[j]))

        def add(value):
            for side in range(2):
                v.part[d, side] = v.part[d, side] + value[:, side * width : (side + 1) * width]

        value = term(v.starts[i], i)
        for side in range(2):
            v.part[d, side] = value[:, side * width : (side + 1) * width]

        def more(j, carry):
            copy(v.own.at[i], v.chain.at[i, j], v.chain_send.at[i, 0], v.chain_recv.at[i, j], sibling).wait_recv()
            add(term(v.chain[i, j], j))
            return carry

        lax.fori_loop(i + 1, chip, more, 0)
        trade(d).start()
        trade(d).wait_recv()
        v.own[i] = -(v.part[d, core] + v.part_in[d])

        def tell(target, carry):
            along(i, chip, target).start()
            return carry

        lax.fori_loop(chip + 1, CHIPS, tell, 0)
        plant(i)

    def relay_far(i):
        for side in range(2):
            for slot in (1, 2):
                arrived(i, side, slot).wait_recv()
                onward(i, side, slot).start()

    for one in fetch:
        one.wait()
    for side in range(2):
        high, low = split(v.inverse[side])
        v.inverse_high[side] = high
        v.inverse_low[side] = low

    def accumulate(idx):
        i = order(idx)

        @pl.when(i < chip)
        def _():
            for side in range(2):
                for slot in (3, 4):
                    arrived(i, side, slot).wait_recv()
            lefts = split(got[i])
            for side in range(2):
                v.total[side] = v.total[side] + dot3(lefts, split(v.cols[i, side]))

    product(0)
    pl.when(chip == 0)(lead_push)
    give_factor.wait_recv()

    def couple_one(j, carry):
        couple(j)
        return carry

    lax.fori_loop(0, chip, couple_one, 0)
    lefts = split(got[chip])
    for side in range(2):
        span = slice(side * width, (side + 1) * width)
        v.total[side] = dot3(lefts, (v.inverse_high[core, :, span], v.inverse_low[core, :, span]))

    def one_solved(idx, carry):
        accumulate(idx)
        return carry

    def by_stage(stage, table):
        first, last = 0, 0
        for key, (low, high) in table.items():
            first = jnp.where(stage == key, low, first)
            last = jnp.where(stage == key, high, last)
        return first, last

    def body(stage, carry):
        @pl.when(stage == 1)
        def _():
            for one in own_sends[:2]:
                one.wait_recv()
            for one in half_sends:
                one.start()

        @pl.when(stage == 2)
        def _():
            for one in half_sends:
                one.wait_recv()
            for one in far_sends:
                one.start()

        pl.when(chip > stage)(lambda: chain_step(stage + 1))

        @pl.when(stage == 1)
        def _():
            own_sends[2].wait_recv()

        for k in range(3):

            @pl.when(stage == k + 1)
            def _():
                for one in partner_sends[k]:
                    one.start()

        @pl.when(stage == 4)
        def _():
            for one in sum(partner_sends, far_sends):
                one.wait_recv()

        def one_product(idx, carry):
            product(idx)
            return carry

        def one_pass(idx, carry):
            add_and_pass(idx)
            return carry

        def one_part(step, carry):
            pl.when(step == 0)(lead_wait)
            factor_part(v.work, v.grid, v.inverted, v.below, step // 3, step % 3)
            return carry

        lax.fori_loop(*by_stage(stage, {1: (1, 4), 2: (4, 5), 4: (5, 8)}), one_product, 0)
        pl.when((stage > 0) & (chip >= stage))(lambda: relay_near(chip - stage))
        pl.when((stage > 1) & (chip >= stage - 1))(lambda: relay_far(chip - stage + 1))
        lax.fori_loop(*by_stage(stage, {2: (0, 4), 3: (4, 5), 5: (5, 8)}), one_pass, 0)

        @pl.when(chip == 0)
        def _():
            pl.when(stage == 1)(lead_sum)
            lax.fori_loop(*by_stage(stage, {2: (0, 2), 3: (2, 5), 4: (5, 9), 5: (9, 12)}), one_part, 0)

        lax.fori_loop(*by_stage(stage, {5: (1, 3), 6: (3, 5)}), one_solved, 0)

        return carry

    lax.fori_loop(0, CHIPS - 1, body, 0)
    pl.when(chip == CHIPS - 1)(lambda: relay_near(0))
    pl.when(chip >= CHIPS - 2)(lambda: relay_far(chip - CHIPS + 2))
    pl.when(chip == CHIPS - 1)(lambda: relay_far(0))
    cross()

    lax.fori_loop(5, CHIPS, one_solved, 0)
    give_total = copy(v.total.at[1 - core], v.total_in, v.total_send, v.total_recv, sibling)
    give_total.start()

    @pl.when(chip == 0)
    def _():
        shape = (2 * width, 2 * width)
        eye = lax.broadcasted_iota(jnp.int32, shape, 0) == lax.broadcasted_iota(jnp.int32, shape, 1)
        v.work[...] = jnp.where(eye, 1.0, 0.0)
        solve_rows(v.work, v.inverted, v.below)

    for c in range(2):
        arrivals(plane, c)
        for part in range(2):
            cross_to(part, c).wait_recv()
            total = plane_sum(plane, part, c) + v.cross_in[part, halves[c]]
            shift = (row * 2 + part - (2 * chip + core)) * width + c * (width // 2)
            there = lax.broadcasted_iota(jnp.int32, total.shape, 0) + shift == lax.broadcasted_iota(
                jnp.int32, total.shape, 1
            )
            rows = pl.ds(part * width + c * (width // 2), width // 2)
            gram_ref[rows] = jnp.where(there, 1.0, 0.0) + scale * total

    share = panel_ref.shape[0]
    other_span = pl.ds(pl.multiple_of((1 - core) * width, width), width)
    swap = copy(gram_ref.at[other_span], v.side, v.side_send, v.side_recv, sibling)

    def hand_out(m):
        return copy(
            v.first.at[pl.ds(m * share, share)], panel_ref, v.row_send.at[m], v.row_recv, (row, CHIPS * core + m)
        )

    @pl.when(chip == 0)
    def _():
        swap.start()
        v.first[:, own_span] = gram_ref[own_span]
        swap.wait_recv()
        v.first[:, other_span] = v.side[...]
        v.first[...] = jnp.dot(
            v.first[...], v.work[...], precision=lax.Precision.HIGHEST, preferred_element_type=jnp.float32
        )
        for m in range(1, CHIPS):
            hand_out(m).start()
        pl.when(core == 1)(lambda: hand_out(0).start())

        @pl.when(core == 0)
        def _():
            panel_ref[...] = v.first[pl.ds(0, share)]

    give_total.wait_recv()
    solved_ref[...] = v.total[core] + v.total_in[...]
    pl.when(col > 0)(lambda: hand_out(0).wait_recv())

    @pl.when(chip == 0)
    def _():
        for step in range(1, n_rows):
            for to in range(2):
                share_to(step, to).wait_send()
        share_to(0, 1 - core).wait_send()
        swap.wait_send()
        for m in range(1, CHIPS):
            hand_out(m).wait_send()
        pl.when(core == 1)(lambda: hand_out(0).wait_send())

    for one in sum(partner_sends, own_sends + half_sends + far_sends):
        one.wait_send()
    give_mine.wait_send()
    give_factor.wait_send()
    give_total.wait_send()

    def drain_push(block, carry):
        pl.when(ahead(block) == 0)(lambda: hand_beside(block).wait_send())
        for c in range(2):
            for side in range(2):
                pl.when(ahead(block) == 2)(lambda: hop_to(block, side, c).wait_send())
                for to in range(2):
                    pl.when(ahead(block) == (1, RING - 1)[side])(lambda: away(block, side, to, c).wait_send())
        return carry

    for part in range(2):
        for c in range(2):
            cross_to(part, c).wait_send()
    lax.fori_loop(0, CHIPS, drain_push, 0)

    def drain_chain(i, carry):
        trade(chip - i).wait_send()

        def told(target, carry):
            along(i, chip, target).wait_send()
            return carry

        lax.fori_loop(chip + 1, CHIPS, told, 0)
        seed_across(i).wait_send()
        pl.when(core != plane)(lambda: seed_beside(i).wait_send())
        for side in range(2):
            for slot in (1, 2):
                near(i, side, slot).wait_send()
                onward(i, side, slot).wait_send()
        return carry

    lax.fori_loop(0, chip, drain_chain, 0)


def finish_kernel(*refs):
    for source, target in zip(refs[:3], refs[3:]):
        target[...] = source[...]


def finish(values):
    vmem = pl.BlockSpec(memory_space=pltpu.VMEM)
    return pl.pallas_call(
        finish_kernel,
        out_shape=tuple(jax.ShapeDtypeStruct(a.shape, a.dtype) for a in values),
        in_specs=[vmem] * 3,
        out_specs=(vmem,) * 3,
    )(*values)


def on_device(iterate, factor, inverses):
    n, width = iterate.shape
    n_rows = lax.axis_size("row")
    n_cols = lax.axis_size("col")
    vmem = pl.BlockSpec(memory_space=pltpu.VMEM)
    scratch = scratch_shapes(n, width, n_rows)
    values = pl.pallas_call(
        functools.partial(fused_kernel, tuple(scratch)),
        out_shape=(
            jax.ShapeDtypeStruct((2 * width, width), jnp.float32),
            jax.ShapeDtypeStruct((2 * width // n_cols, 2 * width), jnp.float32),
            jax.ShapeDtypeStruct((n, width), jnp.float32),
        ),
        in_specs=[pl.BlockSpec(memory_space=pl.ANY)] * 3,
        out_specs=(vmem, vmem, vmem),
        scratch_shapes=list(scratch.values()),
        compiler_params=pltpu.CompilerParams(
            collective_id=0, has_side_effects=True, vmem_limit_bytes=60 << 20
        ),
        cost_estimate=pl.CostEstimate(flops=10**10, bytes_accessed=2 * 10**7, transcendentals=0),
    )(iterate, factor.reshape(CHIPS, 2, width, width), inverses.reshape(CHIPS, 2, width, 2 * width))
    return finish(values)


def solution(mesh):
    placed = (P("row", "col"), P(None, "col"), P())
    return jax.shard_map(
        on_device,
        mesh=mesh,
        in_specs=placed,
        out_specs=(P("row", "col"), P(("row", "col"), None), P("row", "col")),
        check_vma=False,
    )
```
